32 devices in a mesh: dp: 4 (over y, core), fsdp: 8 (over z, x).
Axes of the slice: x: 2, y: 2, z: 4, core: 2. Of those that a mesh axis runs over, the one named last changes fastest.
Arguments:
- stem_features: bfloat16 [32, 576, 1024], P(('dp', 'fsdp')), may hold values from -6 to 6
- lengths: int32 [32, 6], P(('dp', 'fsdp')), may hold values from 1 to 196, 576 in all within a row
- embed_weight: bfloat16 [1024, 768], P('fsdp'), may hold values from -0.1875 to 0.1875
- embed_bias: bfloat16 [768], P('fsdp'), may hold values from -1.5 to 1.5
- before_gain: bfloat16 [768], P('fsdp'), may hold values from 0.5 to 1.5
- before_shift: bfloat16 [768], P('fsdp'), may hold values from -1 to 1
- joint_weight: bfloat16 [768, 2304], P('fsdp'), may hold values from -0.21875 to 0.21875
- query_bias: bfloat16 [768], P('fsdp'), may hold values from -1.5 to 1.5
- value_bias: bfloat16 [768], P('fsdp'), may hold values from -1.5 to 1.5
- output_weight: bfloat16 [768, 768], P('fsdp'), may hold values from -1.75 to 1.75
- output_bias: bfloat16 [768], P('fsdp'), may hold values from -1.5 to 1.5
- middle_gain: bfloat16 [768], P('fsdp'), may hold values from 0.5 to 1.5
- middle_shift: bfloat16 [768], P('fsdp'), may hold values from -1 to 1
- expand_weight: bfloat16 [768, 3072], P('fsdp'), may hold values from -0.21875 to 0.21875
- expand_bias: bfloat16 [3072], P('fsdp'), may hold values from -1.5 to 1.5
- shrink_weight: bfloat16 [3072, 768], P('fsdp'), may hold values from -0.109375 to 0.109375
- shrink_bias: bfloat16 [768], P('fsdp'), may hold values from -1.5 to 1.5
- cotangent: bfloat16 [32, 576, 768], P(('dp', 'fsdp')), may hold values from -6 to 6
Outputs:
- activations: bfloat16 [32, 576, 768], P(('dp', 'fsdp'))
- stem_gradient: bfloat16 [32, 576, 1024], P(('dp', 'fsdp'))
- embed_weight_gradient: float32 [1024, 768], P('fsdp')
- embed_bias_gradient: float32 [768], P('fsdp')
- before_gain_gradient: float32 [768], P('fsdp')
- before_shift_gradient: float32 [768], P('fsdp')
- joint_weight_gradient: float32 [768, 2304], P('fsdp')
- query_bias_gradient: float32 [768], P('fsdp')
- value_bias_gradient: float32 [768], P('fsdp')
- output_weight_gradient: float32 [768, 768], P('fsdp')
- output_bias_gradient: float32 [768], P('fsdp')
- middle_gain_gradient: float32 [768], P('fsdp')
- middle_shift_gradient: float32 [768], P('fsdp')
- expand_weight_gradient: float32 [768, 3072], P('fsdp')
- expand_bias_gradient: float32 [3072], P('fsdp')
- shrink_weight_gradient: float32 [3072, 768], P('fsdp')
- shrink_bias_gradient: float32 [768], P('fsdp')
The draws below stay inside these ranges and needn't reach their ends.
Inputs may be any that keep to these rules, and one draw needn't show every extreme that they name: In each row the 6 region lengths sum to 576, and the largest of them is 196.
All inputs are finite; a program needn't handle non-finite values.
Results may differ from the reference program's by a relative error of at most 0.015.
Values may be sent and summed in bfloat16 or wider, within the bound.
A program may use at most 256 MiB of HBM per device.

```python
import math
import jax
import jax.numpy as jnp
import numpy as np
from jax import lax

D = 768
HEADS = 12
HEAD_DIM = 64
MLP = 3072
STEM = 1024
ROW_LEN = 576
REGIONS = 6
MOST = 196
ROWS = 32


def spiked(drawn, rng, source, target, shards_of, factor):
    def block_of(dim):
        return (jnp.arange(drawn.shape[dim]) // (drawn.shape[dim] // shards_of)).reshape((-1,) + (1,) * (drawn.ndim - 1 - dim))

    first = jax.random.permutation(rng, shards_of)[block_of(target)]
    far = (block_of(target) + shards_of // 2) % shards_of
    return jnp.where((block_of(source) == first) | (block_of(source) == far), factor * drawn, drawn)


def levels(stream_key, dims, split, least, high):
    factor_of = 1.0
    for dim, parts in split:
        draws = jax.random.uniform(jax.random.fold_in(jax.random.fold_in(stream_key, 6), dim), (parts,), jnp.float32, least / len(split), high / len(split))
        factor_of = factor_of * jnp.repeat(jnp.exp(draws), dims[dim] // parts).reshape((-1,) + (1,) * (len(dims) - 1 - dim))
    return factor_of


def length_profile(count, total, most, skew):
    loads = [(1 << 20) // math.isqrt(standing ** skew) + 1 for standing in range(2, count + 1)]
    surplus, given = total - most - (count - 1), [1] * (count - 1)
    while surplus > 0:
        movable = [i for i in range(count - 1) if given[i] < most]
        pool, remaining = sum([loads[i] for i in movable]), surplus
        for i in movable:
            more = min(most - given[i], max(1, remaining * loads[i] // pool), surplus)
            given[i] = given[i] + more
            surplus = surplus - more
    return np.array([most] + given)


def uneven(stream_key, count, total, limit, slope):
    if count == 2:
        one = jax.random.randint(stream_key, (), max(1, total - limit), min(limit, total - 1) + 1)
        return jnp.stack([one, total - one])
    sizes = jnp.asarray(length_profile(count, total, limit, slope), jnp.int32)
    twos = (count - 1) // 2
    giver, sink = sizes[1:1 + 2 * twos:2], sizes[2:2 + 2 * twos:2]
    room = jnp.minimum(giver - 1, limit - sink)
    shifted = jax.random.randint(jax.random.fold_in(stream_key, 1), (twos,), 0, 1 << 20) % (room + 1)
    sizes = sizes.at[1:1 + 2 * twos:2].set(giver - shifted).at[2:2 + 2 * twos:2].set(sink + shifted)
    return sizes[jax.random.permutation(jax.random.fold_in(stream_key, 2), count)]


def bell_draw(stream_key, dims, scale, bound, pieces=(), kind=jnp.bfloat16):
    values = jax.random.normal(stream_key, dims, jnp.float32) * scale
    if len(pieces) > 0:
        values = levels(stream_key, dims, pieces, -0.22, 0.18) * values
    return jnp.clip(values, min=-bound, max=bound).astype(kind)


def bell_draw_with(rng, dims, scale, most, split, heavy, kind=jnp.bfloat16):
    entries = scale * jax.random.normal(rng, dims, jnp.float32)
    if split:
        entries = entries * levels(rng, dims, split, -0.22, 0.18)
    return jnp.clip(spiked(entries, jax.random.fold_in(rng, 3), *heavy), -most, most).astype(kind)


def setup_inputs(seed: int = 0) -> dict:
    splits = jax.random.split(jax.random.key(seed), 19)
    stem_features = bell_draw(splits[0], (ROWS, ROW_LEN, STEM), 1.0, 6.0, ((0, 32),))
    lengths = jax.vmap(lambda own: uneven(own, REGIONS, ROW_LEN, MOST, 1))(jax.random.split(splits[1], ROWS)).reshape((ROWS, REGIONS)).astype(jnp.int32)
    embed_weight = bell_draw(splits[2], (STEM, D), STEM ** -0.5, 0.1875, ((0, 8),))
    embed_bias = bell_draw(splits[3], (D,), 0.3, 1.5, ((0, 8),))
    before_gain = jnp.clip(1.0 + 0.1 * jax.random.normal(splits[4], (D,), jnp.float32), 0.5, 1.5).astype(jnp.bfloat16)
    before_shift = bell_draw(splits[5], (D,), 0.2, 1.0, ((0, 8),))
    joint_weight = bell_draw(splits[6], (D, 3 * D), D ** -0.5, 0.21875, ((0, 8),))
    query_bias = bell_draw(splits[7], (D,), 0.3, 1.5, ((0, 8),))
    value_bias = bell_draw(splits[8], (D,), 0.3, 1.5, ((0, 8),))
    output_weight = bell_draw(splits[9], (D, D), (max(D // 64, 4)) ** -0.5, 1.75, ((0, 8),))
    output_bias = bell_draw(splits[10], (D,), 0.3, 1.5, ((0, 8),))
    middle_gain = jnp.clip(1.0 + 0.1 * jax.random.normal(splits[11], (D,), jnp.float32), 0.5, 1.5).astype(jnp.bfloat16)
    middle_shift = bell_draw(splits[12], (D,), 0.2, 1.0, ((0, 8),))
    expand_weight = bell_draw(splits[13], (D, MLP), D ** -0.5, 0.21875, ((0, 8),))
    expand_bias = bell_draw(splits[14], (MLP,), 0.3, 1.5, ((0, 8),))
    shrink_weight = bell_draw(splits[15], (MLP, D), MLP ** -0.5, 0.109375, ((0, 8),))
    shrink_bias = bell_draw(splits[16], (D,), 0.3, 1.5, ((0, 8),))
    cotangent = bell_draw_with(splits[17], (ROWS, ROW_LEN, D), 1.0, 6.0, ((0, 32),), (0, 2, 32, 2.75))
    return dict(stem_features=stem_features, lengths=lengths, embed_weight=embed_weight, embed_bias=embed_bias, before_gain=before_gain, before_shift=before_shift, joint_weight=joint_weight, query_bias=query_bias, value_bias=value_bias, output_weight=output_weight, output_bias=output_bias, middle_gain=middle_gain, middle_shift=middle_shift, expand_weight=expand_weight, expand_bias=expand_bias, shrink_weight=shrink_weight, shrink_bias=shrink_bias, cotangent=cotangent)


@jax.custom_vjp
def low(v):
    return lax.optimization_barrier(v.astype(jnp.bfloat16)).astype(jnp.float32)

@jax.custom_vjp
def low_back(v):
    return v

def low_keep(v):
    return (low(v), None)

def low_pass(kept, grad):
    return (grad,)

def back_keep(v):
    return (v, None)

def back_low(kept, grad):
    return (low(grad),)
low.defvjp(low_keep, low_pass)
low_back.defvjp(back_keep, back_low)
exact_mode = lax.Precision.HIGHEST

def matmul(left, right):
    return jnp.dot(left, right, precision=exact_mode)

def layer_norm(values, gain, shift):
    center = values - lax.optimization_barrier(jnp.mean(values, axis=-1, keepdims=True))
    spread = lax.optimization_barrier(jnp.mean(center * center, axis=-1, keepdims=True))
    return center * lax.rsqrt(spread + 1e-06) * gain + shift

def region_labels(length_row):
    bounds = jnp.cumsum(length_row)
    places = jnp.arange(ROW_LEN, dtype=jnp.int32)
    return lax.optimization_barrier(jnp.sum((places[:, None] >= bounds[None, :]).astype(jnp.int32), axis=1))

def forward(stem_row, same_region, params):
    embed_weight, embed_bias, before_gain, before_shift, joint_weight, query_bias, value_bias, output_weight, output_bias, middle_gain, middle_shift, expand_weight, expand_bias, shrink_weight, shrink_bias = params
    embedded = low_back(matmul(stem_row, embed_weight) + embed_bias)
    normed = low(layer_norm(embedded, before_gain, before_shift))
    joint_bias = jnp.concatenate([query_bias, jnp.zeros_like(query_bias), value_bias])
    projected = low(low_back(matmul(normed, joint_weight) + joint_bias))
    query = projected[:, :D].reshape(ROW_LEN, HEADS, HEAD_DIM)
    keys = projected[:, D:2 * D].reshape(ROW_LEN, HEADS, HEAD_DIM)
    values = projected[:, 2 * D:].reshape(ROW_LEN, HEADS, HEAD_DIM)
    products = jnp.einsum('qhe,khe->hqk', query, keys, precision=exact_mode) * (1.0 / math.sqrt(HEAD_DIM))
    scores = low_back(jnp.where(same_region[None], products, -1e+30))
    attend = jax.nn.softmax(scores, axis=-1)
    mixed = jnp.einsum('hqk,khe->qhe', low(attend), values, precision=exact_mode).reshape(ROW_LEN, D)
    mixed = low(low_back(mixed))
    residual = embedded + low_back(matmul(mixed, output_weight) + output_bias)
    normed_mid = low(layer_norm(residual, middle_gain, middle_shift))
    upper = low_back(matmul(normed_mid, expand_weight) + expand_bias)
    hidden = low(jax.nn.gelu(upper, approximate=False))
    return residual + low_back(matmul(hidden, shrink_weight) + shrink_bias)

def reference(stem_features, lengths, embed_weight, embed_bias, before_gain, before_shift, joint_weight, query_bias, value_bias, output_weight, output_bias, middle_gain, middle_shift, expand_weight, expand_bias, shrink_weight, shrink_bias, cotangent):
    params = tuple((item.astype(jnp.float32) for item in (embed_weight, embed_bias, before_gain, before_shift, joint_weight, query_bias, value_bias, output_weight, output_bias, middle_gain, middle_shift, expand_weight, expand_bias, shrink_weight, shrink_bias)))

    def one_row(totals, item):
        stem_row, length_row, cot_row = item
        labels = region_labels(length_row)
        same_region = labels[:, None] == labels[None, :]
        output, pull = jax.vjp(lambda source, weights: forward(source, same_region, weights), stem_row.astype(jnp.float32), params)
        stem_grad, param_grads = pull(cot_row.astype(jnp.float32))
        totals = jax.tree.map(jnp.add, totals, param_grads)
        return (totals, (output.astype(jnp.bfloat16), stem_grad.astype(jnp.bfloat16)))
    zeros = tuple((jnp.zeros_like(item) for item in params))
    totals, (activations, stem_gradient) = lax.scan(one_row, zeros, (stem_features, lengths, cotangent))
    return (activations, stem_gradient, totals[0], totals[1], totals[2], totals[3], totals[4], totals[5], totals[6], totals[7], totals[8], totals[9], totals[10], totals[11], totals[12], totals[13], totals[14])
```

```python
import math
import types

import jax
import jax.numpy as jnp
from jax import lax
from jax.experimental import pallas as pl
from jax.experimental.pallas import tpu as pltpu
from jax.sharding import PartitionSpec as P

HEADS = 12
HEAD_DIM = 64
AXIS = "fsdp"
MESH = pl.DeviceIdType.MESH
WIDE = jnp.float32
NARROW = jnp.bfloat16

EMBED_BIAS, FIRST_GAIN, FIRST_SHIFT, QUERY_BIAS, VALUE_BIAS, OUT_BIAS = 0, 1, 2, 3, 4, 5
SECOND_GAIN, SECOND_SHIFT, SHRINK_BIAS, EXPAND_BIAS = 6, 7, 8, 9
VECTOR_ROWS = 16

EMBED, JOINT, OUT, EXPAND, SHRINK = 0, 1, 2, 3, 4

ORDER = (
    32, 33, 34, 35, 64, 65, 66, 0, 96, 544, 128, 97, 129, 98, 130, 545, 0, 99, 131, 160,
    36, 67, 68, 69, 70, 161, 37, 71, 162, 38, 72, 163, 39, 73, 100, 132, 192, 101, 133, 164,
    40, 74, 102, 134, 224, 165, 41, 75, 103, 135, 193, 256, 0, 166, 42, 76, 194, 167, 43, 77,
    225, 104, 136, 288, 195, 257, 0, 226, 0, 168, 44, 78, 105, 137, 258, 0, 106, 227, 138, 289,
    196, 169, 45, 79, 107, 139, 170, 46, 259, 0, 290, 108, 171, 47, 140, 197, 228, 172, 291, 109,
    260, 141, 0, 198, 0, 110, 173, 199, 229, 142, 111, 143, 0, 292, 0, 174, 261, 175, 230, 200,
    0, 0, 231, 262, 0, 201, 293, 0, 263, 232, 0, 202, 294, 203, 0, 233, 264, 204, 0, 234,
    295, 0, 205, 265, 235, 0, 266, 206, 207, 236, 296, 0, 267, 237, 0, 268, 297, 0, 238, 269,
    239, 298, 0, 320, 321, 322, 299, 0, 300, 270, 271, 0, 301, 352, 0, 353, 302, 0, 354, 303,
    0, 0, 384, 0, 385, 0, 323, 0, 324, 386, 0, 325, 355, 416, 0, 326, 356, 0, 357, 358,
    0, 0, 327, 387, 417, 0, 448, 0, 359, 388, 0, 418, 0, 389, 449, 0, 419, 0, 0, 328,
    390, 0, 329, 480, 0, 330, 0, 360, 450, 481, 361, 423, 362, 512, 0, 451, 420, 392, 513, 0,
    482, 0, 0, 393, 421, 455, 0, 331, 394, 514, 0, 332, 483, 0, 333, 422, 363, 487, 0, 452,
    364, 424, 365, 515, 519, 425, 0, 334, 395, 0, 335, 453, 484, 426, 0, 336, 366, 396, 0, 0,
    367, 427, 368, 454, 397, 577, 485, 516, 428, 456, 398, 578, 399, 457, 517, 429, 400, 579, 458, 486,
    488, 430, 489, 580, 459, 490, 518, 431, 520, 581, 460, 521, 491, 522, 432, 461, 492, 523, 462, 493,
    524, 463, 494, 525, 464, 495, 526, 496, 527, 528,
)


def nn(left, right):
    return lax.dot_general(left, right, (((1,), (0,)), ((), ())), preferred_element_type=WIDE)


def nt(left, right):
    return lax.dot_general(left, right, (((1,), (1,)), ((), ())), preferred_element_type=WIDE)


def tn(left, right):
    return lax.dot_general(left, right, (((0,), (0,)), ((), ())), preferred_element_type=WIDE)


def aligned(value, step):
    return pl.multiple_of(value, step)


def gelu_pair(upper):
    cdf = 0.5 * (1.0 + lax.erf(upper * (1.0 / math.sqrt(2.0))))
    density = jnp.exp(-0.5 * upper * upper) * (1.0 / math.sqrt(2.0 * math.pi))
    return upper * cdf, cdf + upper * density


def gather_split(rows):
    half = rows // 2
    share = 16 * max(1, (half * 5) // 192)
    return share, half - 2 * share


def reduce_split(weight, rows):
    half = rows // 2
    share = 0 if weight == OUT else 16 * max(1, half // 64)
    return share, half - 2 * share


def column_chunks(width, step):
    return [(start, step) for start in range(0, width, step)]


def fused_kernel(tokens, width, stem_width, mlp, sizes, gather_plan, reduce_plan, names, *refs):
    vec_in, lengths, stem_hbm, cot_hbm = refs[:4]
    shard, (act_hbm, stem_grad_hbm) = refs[4:9], refs[9:11]
    result, vec_out = refs[11:16], refs[16]
    ref = types.SimpleNamespace(**dict(zip(names, refs[17:])))
    full = ref.full
    local_grad = [ref.core_shrink] + list(full[1:4]) + [ref.shrink_grad]
    resid, work, bias = ref.resid, ref.work, ref.bias
    unit1, unit2, scale1, scale2 = ref.unit1, ref.unit2, ref.scale1, ref.scale2
    normed, normed_mid, proj = ref.normed, ref.normed_mid, ref.proj
    mixed_t, mixed, lse, delta = ref.mixed_t, ref.mixed, ref.lse, ref.delta
    pull, hidden, cot, stem, low = ref.pull, ref.hidden, ref.cot, ref.stem, ref.low
    vecs, vec_all, vec_sum = ref.vecs, ref.vec_all, ref.vec_sum
    fold = ref.fold

    dp, fs = lax.axis_index("dp"), lax.axis_index(AXIS)
    y, c = lax.div(dp, 2), lax.rem(dp, 2)
    z, x = lax.div(fs, 2), lax.rem(fs, 2)
    z_others = (z + 1 - 2 * lax.rem(z, 2), lax.rem(z + 2, 4), 3 - z)
    at_core = (y * 2 + 1 - c, fs)
    at_y = ((1 - y) * 2 + c, fs)
    at_x = (dp, z * 2 + 1 - x)
    at_z = tuple((dp, other * 2 + x) for other in z_others)

    def send(src, dst, send_sem, recv_sem, where):
        return pltpu.make_async_remote_copy(
            src_ref=src,
            dst_ref=dst,
            send_sem=send_sem,
            recv_sem=recv_sem,
            device_id=where,
            device_id_type=MESH,
        )


    up = lax.div(z, 2)
    inner = (z == 1) | (z == 2)
    arrivals = (z_others[0], 2 - up, 3 - 3 * up)
    fill, g_send, g_recv = ref.fill, ref.g_send, ref.g_recv

    def gather_refs(k):
        weight, start, count = gather_plan[k]
        rows = sizes[weight][0]
        half = rows // 2
        share, both = gather_split(rows)
        mine = pl.ds(aligned(c * half + y * share, 16), share + both)
        passed = pl.ds(aligned(c * half + y * (share + both), 16), share)
        halves = pl.ds(aligned(c * half, 16), half)
        return full[weight], shard[weight], mine, passed, halves, pl.ds(start, count)

    def fill_copy(k):
        whole, own, _, _, halves, cols = gather_refs(k)
        return pltpu.make_async_copy(own.at[halves, cols], whole.at[z, x, halves, cols], fill.at[k])

    def own_copy(k, sent, got, where):
        whole, own, mine, _, _, cols = gather_refs(k)
        return send(own.at[mine, cols], whole.at[z, x, mine, cols], g_send.at[sent, k], g_recv.at[got, k], where)

    def same_copy(part, k, sent, got, where):
        return send(part, part, g_send.at[sent, k], g_recv.at[got, k], where)

    def z_copy(k, order, sent, got, where):
        whole, _, mine, _, _, cols = gather_refs(k)
        return same_copy(whole.at[arrivals[order], x, mine, cols], k, sent, got, where)

    def across(k):
        return (z_copy(k, 0, 2, 2, at_z[2]), z_copy(k, 1, 3, 1, at_z[0]), z_copy(k, 2, 4, 2, at_z[0]))

    def x_copy(k, order):
        whole, _, mine, _, _, cols = gather_refs(k)
        return same_copy(whole.at[arrivals[order], x, mine, cols], k, 5, 5, at_x)

    def x_bytes(k):
        whole, _, mine, _, _, cols = gather_refs(k)
        return same_copy(whole.at[:, x, mine, cols], k, 5, 5, at_x)

    def y_copy(k, order):
        whole, _, _, passed, _, cols = gather_refs(k)
        return same_copy(whole.at[arrivals[order], x, passed, cols], k, 6, 6, at_y)

    def y_bytes(k):
        whole, _, _, passed, _, cols = gather_refs(k)
        return same_copy(whole.at[pl.ds(0, 3), x, passed, cols], k, 6, 6, at_y)

    def y_copy_late(k):
        whole, _, _, passed, _, cols = gather_refs(k)
        return same_copy(whole.at[:, 1 - x, passed, cols], k, 7, 7, at_y)

    def core_copy(k):
        whole, _, _, _, halves, cols = gather_refs(k)
        return same_copy(whole.at[:, :, halves, cols], k, 8, 8, at_core)

    def start_z(k):
        own_copy(k, 0, 0, at_z[0]).start()

        @pl.when(inner)
        def _():
            own_copy(k, 1, 1, at_z[2]).start()

        fill_copy(k).start()

    def start_x(k):
        own_copy(k, 5, 5, at_x).start()

    def gather_z(order):
        def step(k):
            z_copy(k, order, order, order, at_z[0]).wait_recv()

            @pl.when(inner)
            def _():
                across(k)[order].start()

            x_copy(k, order).start()
            y_copy(k, order).start()

        return step

    def gather_x(k):
        x_bytes(k).wait_recv()
        y_copy_late(k).start()

    def gather_y(k):
        fill_copy(k).wait()
        y_bytes(k).wait_recv()
        y_copy_late(k).wait_recv()
        core_copy(k).start()

    def gather_core(k):
        core_copy(k).wait_recv()

    def gather_sent(k):
        own_copy(k, 0, 0, at_z[0]).wait_send()

        @pl.when(inner)
        def _():
            own_copy(k, 1, 1, at_z[2]).wait_send()
            for copy in across(k):
                copy.wait_send()

        x_bytes(k).wait_send()
        y_bytes(k).wait_send()
        y_copy_late(k).wait_send()
        core_copy(k).wait_send()

    r_send, r_recv, r_done = ref.r_send, ref.r_recv, ref.r_done
    from_y, from_x, from_z = ref.from_y, ref.from_x, ref.from_z
    part_out, part_in, final = ref.part_out, ref.part_in, ref.final
    free = ref.free

    def core_slot(k):
        weight, start, count = reduce_plan[k]
        if weight == SHRINK:
            return ref.core_shrink.at[:, :, :, pl.ds(start, count)]
        if weight == EMBED:
            return ref.core_embed.at[:, :, :, pl.ds(start, count)]
        half = sizes[weight][0] // 2
        before = {EXPAND: 0, OUT: mlp // width, JOINT: mlp // width + 1}[weight]
        return full[SHRINK].at[:, :, pl.ds((before + start // width) * half, half), pl.ds(start % width, count)]

    def reduce_refs(k):
        weight, start, count = reduce_plan[k]
        share, both = reduce_split(weight, sizes[weight][0])
        return weight, sizes[weight][0] // 2, share, both, pl.ds(start, count)

    def r1_copy(k):
        weight, half, _, _, cols = reduce_refs(k)
        src = local_grad[weight].at[:, :, pl.ds(aligned((1 - c) * half, 16), half), cols]
        return send(src, core_slot(k), r_send.at[0, k], r_recv.at[0, k], at_core)

    def r2_copy(k):
        weight, half, share, both, cols = reduce_refs(k)
        rows = pl.ds(aligned(c * half + (1 - y) * (share + both), 16), share)
        return send(
            local_grad[weight].at[:, :, rows, cols],
            from_y[weight].at[:, :, :, cols],
            r_send.at[1, k],
            r_recv.at[1, k],
            at_y,
        )

    def mine_rows(half, share, both):
        return pl.ds(aligned(c * half + y * share, 16), share + both)

    def r3_copy(k):
        weight, half, share, both, cols = reduce_refs(k)
        return send(
            local_grad[weight].at[:, 1 - x, mine_rows(half, share, both), cols],
            from_x[weight].at[:, :, cols],
            r_send.at[2, k],
            r_recv.at[2, k],
            at_x,
        )

    def r4_copy(k, j):
        weight, half, share, both, cols = reduce_refs(k)
        return send(
            local_grad[weight].at[z_others[j], x, mine_rows(half, share, both), cols],
            from_z[weight].at[j, :, cols],
            r_send.at[3, k],
            r_recv.at[3, k],
            at_z[j],
        )

    def r4_bytes(k):
        weight, _, _, _, cols = reduce_refs(k)
        part = from_z[weight].at[:, :, cols]
        return send(part, part, r_send.at[3, k], r_recv.at[3, k], at_z[0])

    def r5_copy(k):
        weight, _, _, _, cols = reduce_refs(k)
        return send(
            part_out[weight].at[:, cols], part_in[weight].at[:, cols], r_send.at[4, k], r_recv.at[4, k], at_y
        )

    def r6_copies(k):
        weight, half, _, _, cols = reduce_refs(k)
        rows = pl.ds(aligned(c * half, 16), half)
        src, dst = final[weight].at[:, cols], result[weight].at[rows, cols]
        return (
            send(src, dst, r_send.at[5, k], r_recv.at[5, k], at_core),
            pltpu.make_async_copy(src, dst, r_done.at[k]),
        )

    def r6_incoming(k):
        weight, half, _, _, cols = reduce_refs(k)
        rows = pl.ds(aligned((1 - c) * half, 16), half)
        part = result[weight].at[rows, cols]
        return send(part, part, r_send.at[5, k], r_recv.at[5, k], at_core)

    def reduce_1(k):
        if reduce_plan[k][:2] == (EXPAND, 0):
            pl.semaphore_wait(free, 1)
        r1_copy(k).start()

    def reduce_2(k):
        weight, half, share, _, cols = reduce_refs(k)
        r1_copy(k).wait_recv()
        slot, total = core_slot(k), local_grad[weight]
        rows = pl.ds(aligned(c * half, 16), half)
        for i in range(4):
            for j in range(2):
                total[i, j, rows, cols] = total[i, j, rows, cols] + slot[i, j]
        if share:
            r2_copy(k).start()
        else:
            r3_copy(k).start()

    def reduce_3(k):
        weight, half, share, both, cols = reduce_refs(k)
        r2_copy(k).wait_recv()
        total = local_grad[weight]
        rows = pl.ds(aligned(c * half + y * (share + both), 16), share)
        for i in range(4):
            for j in range(2):
                total[i, j, rows, cols] = total[i, j, rows, cols] + from_y[weight][i, j, :, cols]
        r3_copy(k).start()

    def reduce_4(k):
        weight, half, share, both, cols = reduce_refs(k)
        r3_copy(k).wait_recv()
        total = local_grad[weight]
        rows = mine_rows(half, share, both)
        for i in range(4):
            total[i, x, rows, cols] = total[i, x, rows, cols] + from_x[weight][i, :, cols]
        for j in range(3):
            r4_copy(k, j).start()

    def reduce_5(k):
        weight, half, share, both, cols = reduce_refs(k)
        r4_bytes(k).wait_recv()
        value = local_grad[weight][z, x, mine_rows(half, share, both), cols].astype(WIDE)
        for j in range(3):
            value = value + from_z[weight][j, :, cols].astype(WIDE)
        part_out[weight][:, cols] = value.astype(NARROW)
        r5_copy(k).start()

    def reduce_6(k):
        weight, half, share, both, cols = reduce_refs(k)
        r5_copy(k).wait_recv()
        own, came, whole = part_out[weight], part_in[weight], final[weight]

        def rows(start, count):
            return pl.ds(aligned(start, 16), count)

        if share:
            whole[rows(y * (share + both), share), cols] = own[rows(y * both, share), cols].astype(WIDE)
            whole[rows((1 - y) * (share + both), share), cols] = came[rows((1 - y) * both, share), cols].astype(WIDE)
        whole[share : share + both, cols] = own[rows((1 - y) * share, both), cols].astype(WIDE) + came[
            rows(y * share, both), cols
        ].astype(WIDE)
        for copy in r6_copies(k):
            copy.start()

    def reduce_7(k):
        r6_incoming(k).wait_recv()
        r1_copy(k).wait_send()
        if reduce_refs(k)[2]:
            r2_copy(k).wait_send()
        r3_copy(k).wait_send()
        r4_bytes(k).wait_send()
        r5_copy(k).wait_send()
        remote, local = r6_copies(k)
        remote.wait_send()
        local.wait()

    def row(place):
        return vecs[place : place + 1, :]

    def layer_norm(unit, scale, out, gain, shift):
        def step(n, carry):
            rows = pl.ds(aligned(n * 96, 96), 96)
            values = resid[rows, :]
            center = values - jnp.mean(values, axis=1, keepdims=True)
            factor = lax.rsqrt(jnp.mean(center * center, axis=1, keepdims=True) + 1e-6)
            units = center * factor
            scale[rows, :] = factor
            unit[rows, :] = units.astype(NARROW)
            out[rows, :] = (units * row(gain) + row(shift)).astype(NARROW)
            return carry

        lax.fori_loop(0, tokens // 96, step, 0)

    def eight(values):
        return jnp.sum(values.reshape(values.shape[0] // 8, 8, values.shape[1]), axis=0)

    def norm_backward(unit, scale, gain, upstream, keep_wide, places):
        fold[...] = jnp.zeros_like(fold)

        def step(n, carry):
            rows = pl.ds(aligned(n * 96, 96), 96)
            grads = work[rows, :]
            units = unit[rows, :].astype(WIDE)
            inner = grads * row(gain)
            fold[0:8, :] += eight(grads * units)
            fold[8:16, :] += eight(grads)
            value = upstream[rows, :].astype(WIDE) + scale[rows, :] * (
                inner
                - jnp.mean(inner, axis=1, keepdims=True)
                - units * jnp.mean(inner * units, axis=1, keepdims=True)
            )
            if keep_wide:
                resid[rows, :] = value
            narrow = value.astype(NARROW)
            low[rows, :] = narrow
            fold[16:24, :] += eight(narrow.astype(WIDE))
            return carry

        lax.fori_loop(0, tokens // 96, step, 0)
        for n, place in enumerate(places):
            vec_sum[0, place : place + 1, :] = jnp.sum(fold[8 * n : 8 * n + 8, :], axis=0, keepdims=True)

    def column_sum(source, start, place, at=0, count=width):
        def step(n, total):
            return total + eight(source[pl.ds(aligned(n * 96, 96), 96), start : start + count].astype(WIDE))

        total = lax.fori_loop(0, tokens // 96, step, jnp.zeros((8, count), WIDE))
        vec_sum[0, place : place + 1, at : at + count] = jnp.sum(total, axis=0, keepdims=True)

    lane = lax.broadcasted_iota(jnp.int32, (1, 2 * HEAD_DIM), 1)

    def head_lanes(head, value):
        return jnp.where((lane < HEAD_DIM) == (head == 0), value, 0.0).astype(NARROW)

    factor = 1.0 / math.sqrt(HEAD_DIM)

    def attend_forward(p):
        def run():
            at = p * 128
            query = proj[:, pl.ds(at, 128)]
            keys = proj[:, pl.ds(width + at, 128)]
            values_t = proj[:, pl.ds(2 * width + at, 128)].T
            for head in range(2):
                scores = nt(keys * head_lanes(head, factor), query) + bias[...].astype(WIDE)
                largest = jnp.max(scores, axis=0, keepdims=True)
                expos = jnp.exp(scores - largest)
                total = jnp.sum(expos, axis=0, keepdims=True)
                mix = nn(values_t[64 * head : 64 * head + 64], expos.astype(NARROW)) * (1.0 / total)
                mixed_t[pl.ds(aligned(at + 64 * head, 64), 64), :] = mix.astype(NARROW)
                lse[pl.ds(2 * p + head, 1), :] = largest + jnp.log(total)

        return run

    def attend_backward(p):
        def run():
            at = p * 128
            query = proj[:, pl.ds(at, 128)]
            keys = proj[:, pl.ds(width + at, 128)]
            values = proj[:, pl.ds(2 * width + at, 128)]
            grads = mixed[:, pl.ds(at, 128)]
            keys_t = keys.T
            value_grads, key_grads = [], []
            for head in range(2):
                scores = nt(keys * head_lanes(head, factor), query) + bias[...].astype(WIDE)
                attend = jnp.exp(scores - lse[pl.ds(2 * p + head, 1), :])
                attend_grad = nt(values * head_lanes(head, 1.0), grads)
                scores_grad = (attend * (attend_grad - delta[pl.ds(2 * p + head, 1), :])).astype(NARROW)
                value_grads.append(nn(attend.astype(NARROW), grads))
                key_grads.append(nn(scores_grad, query))
                query_grad = nn(keys_t[64 * head : 64 * head + 64], scores_grad) * factor
                mixed_t[pl.ds(aligned(at + 64 * head, 64), 64), :] = query_grad.astype(NARROW)
            first_head = lane < HEAD_DIM
            pull[:, pl.ds(2 * width + at, 128)] = jnp.where(first_head, *value_grads).astype(NARROW)
            pull[:, pl.ds(width + at, 128)] = (jnp.where(first_head, *key_grads) * factor).astype(NARROW)

        return run

    barrier = pltpu.get_barrier_semaphore()
    partners = (at_core, at_y, at_x) + at_z
    for partner in partners:
        pl.semaphore_signal(barrier, inc=1, device_id=partner, device_id_type=MESH)
    load_stem = pltpu.make_async_copy(stem_hbm, stem, ref.load.at[0])
    load_cot = pltpu.make_async_copy(cot_hbm, cot, ref.load.at[1])
    load_stem.start()
    load_cot.start()
    pl.semaphore_wait(barrier, len(partners))

    v_send, v_recv = ref.v_send, ref.v_recv
    vec_z = [send(vec_in, vec_all.at[z, x], v_send.at[0], v_recv.at[0], at_z[j]) for j in range(3)]
    vec_z_part = vec_all.at[pl.ds(0, 3), x]
    vec_z_bytes = send(vec_z_part, vec_z_part, v_send.at[0], v_recv.at[0], at_z[0])
    vec_x_part = vec_all.at[:, x]
    vec_x = send(vec_x_part, vec_x_part, v_send.at[1], v_recv.at[1], at_x)
    vec_all[z, x] = vec_in[...]
    for copy in vec_z:
        copy.start()

    def vec_gather(n):
        if n == 0:
            vec_z_bytes.wait_recv()
            vec_x.start()
        else:
            vec_x.wait_recv()

    vec_from = ref.vec_from
    vec_partners = (at_core, at_y, at_x, at_z[0], at_z[1])

    def vec_copy(n):
        return send(vec_sum.at[n], vec_from.at[n], v_send.at[2 + n], v_recv.at[2 + n], vec_partners[n])

    def vec_step(n):
        vec_copy(n - 1).wait_recv()
        vec_sum[n] = vec_sum[n - 1] + vec_from[n - 1]
        if n < len(vec_partners):
            vec_copy(n).start()

    blocks = []
    block = blocks.append

    @block
    def make_bias():
        places = lax.broadcasted_iota(jnp.int32, (1, tokens), 1)
        places_down = lax.broadcasted_iota(jnp.int32, (tokens, 1), 0)
        labels = jnp.zeros((1, tokens), jnp.int32)
        labels_down = jnp.zeros((tokens, 1), jnp.int32)
        bound = 0
        for n in range(lengths.shape[1]):
            bound = bound + lengths[0, n]
            labels = labels + (places >= bound).astype(jnp.int32)
            labels_down = labels_down + (places_down >= bound).astype(jnp.int32)
        bias[...] = jnp.where(labels_down == labels, 0.0, -1e30).astype(NARROW)
        vec_sum[0] = jnp.zeros((VECTOR_ROWS, width), WIDE)

    @block
    def add_vectors():
        totals = vec_all[0, 0].astype(WIDE)
        for i in range(4):
            for j in range(2):
                if i + j > 0:
                    totals = totals + vec_all[i, j].astype(WIDE)
        vecs[...] = totals
        vec_z_bytes.wait_send()
        vec_x.wait_send()
        load_stem.wait()
        load_cot.wait()

    def chunks(plan, weight):
        return [item[1:] for item in plan if item[0] == weight]

    def embed(start, count):
        def run():
            piece = full[EMBED][:, :, :, start : start + count].reshape(stem_width, count)
            offset = vecs[EMBED_BIAS : EMBED_BIAS + 1, start : start + count]
            resid[:, start : start + count] = nn(stem[...], piece) + offset

        return run

    def project(start, count):
        def run():
            value = nn(normed[...], full[JOINT][:, :, :, start : start + count].reshape(width, count))
            at = start % width
            if start // width == 0:
                value = value + vecs[QUERY_BIAS : QUERY_BIAS + 1, at : at + count]
            if start // width == 2:
                value = value + vecs[VALUE_BIAS : VALUE_BIAS + 1, at : at + count]
            proj[:, start : start + count] = value.astype(NARROW)

        return run

    for item in chunks(gather_plan, EMBED):
        block(embed(*item))

    @block
    def first_norm():
        layer_norm(unit1, scale1, normed, FIRST_GAIN, FIRST_SHIFT)

    for item in chunks(gather_plan, JOINT):
        block(project(*item))
    for p in range(HEADS // 2):
        block(attend_forward(p))

    @block
    def join_heads():
        mixed[...] = mixed_t[...].T
        resid[...] = resid[...] + nn(mixed[...], full[OUT][...].reshape(width, width)) + row(OUT_BIAS)

    @block
    def second_norm():
        layer_norm(unit2, scale2, normed_mid, SECOND_GAIN, SECOND_SHIFT)

    def expand_forward(i):
        def run():
            start = i * width
            work[...] = nn(normed_mid[...], full[EXPAND][:, :, :, start : start + width].reshape(width, width))

            def gelu_step(n, carry):
                rows = pl.ds(aligned(n * 64, 64), 64)
                for at in range(0, width, 128):
                    offset = vecs[EXPAND_BIAS + i : EXPAND_BIAS + i + 1, at : at + 128]
                    value, slope = gelu_pair(work[rows, at : at + 128] + offset)
                    hidden[rows, start + at : start + at + 128] = value.astype(NARROW)
                    pull[rows, start + at : start + at + 128] = slope.astype(NARROW)
                return carry

            lax.fori_loop(0, tokens // 64, gelu_step, 0)

        return run

    rows_shrink = sizes[SHRINK][0]

    def shrink_gradient(i):
        def run():
            for j in range(2):
                at = rows_shrink * (2 * i + j)
                local_grad[SHRINK][i, j] = tn(hidden[:, at : at + rows_shrink], cot[...]).astype(NARROW)

        return run

    for i in range(4):
        block(expand_forward(i))
        block(shrink_gradient(i))

    @block
    def cotangent_sum():
        column_sum(cot, 0, SHRINK_BIAS)

    def hidden_backward(i):
        def run():
            at = i * width
            grads = nt(cot[...], full[SHRINK][i].reshape(width, width))
            pull[:, at : at + width] = (grads * pull[:, at : at + width].astype(WIDE)).astype(NARROW)
            column_sum(pull, at, EXPAND_BIAS + i)

        return run

    for i in range(4):
        block(hidden_backward(i))
    store_act = pltpu.make_async_copy(low, act_hbm, ref.load.at[0])
    store_stem = pltpu.make_async_copy(hidden.at[:, pl.ds(0, stem_width)], stem_grad_hbm, ref.load.at[1])

    @block
    def activations():
        value = nn(hidden[...], full[SHRINK][...].reshape(mlp, width))
        low[...] = (resid[...] + value + row(SHRINK_BIAS)).astype(NARROW)
        store_act.start()
        pl.semaphore_signal(free, inc=1, device_id=at_core, device_id_type=MESH)

    @block
    def expand_backward():
        work[...] = nt(pull[...], full[EXPAND][...].reshape(width, mlp))

    def expand_gradient(i):
        def run():
            at = i * width
            value = tn(normed_mid[...], pull[:, at : at + width]).astype(NARROW)
            full[EXPAND][:, :, :, at : at + width] = value.reshape(4, 2, width // 8, width)

        return run

    for i in range(4):
        block(expand_gradient(i))

    @block
    def second_norm_backward():
        store_act.wait()
        norm_backward(unit2, scale2, SECOND_GAIN, cot, True, (SECOND_GAIN, SECOND_SHIFT, OUT_BIAS))

    @block
    def out_backward():
        mixed[...] = nt(low[...], full[OUT][...].reshape(width, width)).astype(NARROW)

    @block
    def out_gradient():
        full[OUT][...] = nn(mixed_t[...], low[...]).astype(NARROW).reshape(4, 2, width // 8, width)

    @block
    def row_sums():
        grads_t = mixed[...].T
        for head in range(HEADS):
            span = slice(64 * head, 64 * head + 64)
            product = grads_t[span].astype(WIDE) * mixed_t[span, :].astype(WIDE)
            delta[head : head + 1, :] = jnp.sum(product, axis=0, keepdims=True)

    def gather_query(half):
        def run():
            at = half * width // 2
            pull[:, at : at + width // 2] = mixed_t[at : at + width // 2, :].T
            column_sum(pull, at, QUERY_BIAS, at, width // 2)
            column_sum(pull, 2 * width + at, VALUE_BIAS, at, width // 2)

        return run

    def joint_backward(half):
        def run():
            total = 0.0 if half == 0 else work[...]
            for part in range(3):
                at = part * width + half * width // 2
                weight = full[JOINT][:, :, :, at : at + width // 2].reshape(width, width // 2)
                total = total + nt(pull[:, at : at + width // 2], weight)
            work[...] = total

        return run

    def joint_gradient(start, count):
        def run():
            value = tn(normed[...], pull[:, start : start + count]).astype(NARROW)
            full[JOINT][:, :, :, start : start + count] = value.reshape(4, 2, width // 8, count)

        return run

    for half in range(2):
        for p in range(HEADS // 4):
            block(attend_backward(half * HEADS // 4 + p))
        block(gather_query(half))
        block(joint_backward(half))
        for item in chunks(reduce_plan, JOINT)[3 * half : 3 * half + 3]:
            block(joint_gradient(*item))

    @block
    def first_norm_backward():
        norm_backward(unit1, scale1, FIRST_GAIN, resid, False, (FIRST_GAIN, FIRST_SHIFT, EMBED_BIAS))

    rows_embed = sizes[EMBED][0]

    def embed_gradient(start, count):
        def run():
            value = tn(stem[...], low[:, start : start + count]).astype(NARROW)
            local_grad[EMBED][:, :, 0:rows_embed, start : start + count] = value.reshape(4, 2, rows_embed, count)

        return run

    for item in chunks(reduce_plan, EMBED):
        block(embed_gradient(*item))

    @block
    def start_vectors():
        vec_copy(0).start()

    @block
    def stem_backward():
        value = nt(low[...], full[EMBED][...].reshape(stem_width, width))
        hidden[:, 0:stem_width] = value.astype(NARROW)
        store_stem.start()

    work_left = iter(blocks)
    steps = (
        lambda k: next(work_left)(),
        start_z,
        start_x,
        gather_z(0),
        gather_z(1),
        gather_z(2),
        gather_x,
        gather_y,
        gather_core,
        gather_sent,
        reduce_1,
        reduce_2,
        reduce_3,
        reduce_4,
        reduce_5,
        reduce_6,
        reduce_7,
        vec_gather,
        vec_step,
    )
    for code in ORDER:
        steps[code // 32](code % 32)
    vec_out[...] = vec_sum[len(vec_partners)]
    for n in range(len(vec_partners)):
        vec_copy(n).wait_send()
    store_stem.wait()


def fused(mesh):
    def local(
        stem_features,
        lengths,
        embed_weight,
        embed_bias,
        before_gain,
        before_shift,
        joint_weight,
        query_bias,
        value_bias,
        output_weight,
        output_bias,
        middle_gain,
        middle_shift,
        expand_weight,
        expand_bias,
        shrink_weight,
        shrink_bias,
        cotangent,
    ):
        _, tokens, stem_width = stem_features.shape
        width = embed_weight.shape[1]
        mlp = expand_weight.shape[1]
        shards = (embed_weight, joint_weight, output_weight, expand_weight, shrink_weight)
        sizes = [item.shape for item in shards]
        fsdp = lax.axis_index(AXIS)

        nine = jnp.stack(
            [
                embed_bias,
                before_gain,
                before_shift,
                query_bias,
                value_bias,
                output_bias,
                middle_gain,
                middle_shift,
                shrink_bias,
            ]
        )
        piece = nine.shape[1]
        owner = jnp.arange(width) // piece
        rows_nine = jnp.where(owner[None] == fsdp, jnp.tile(nine, (1, width // piece)), 0)
        owner = jnp.arange(mlp) // expand_bias.shape[0]
        rows_expand = jnp.where(owner == fsdp, jnp.tile(expand_bias, mlp // expand_bias.shape[0]), 0)
        rows_expand = rows_expand.reshape(mlp // width, width)
        used = 9 + mlp // width
        vec_in = jnp.concatenate([rows_nine, rows_expand, jnp.zeros((VECTOR_ROWS - used, width), NARROW)])
        vec_in = vec_in.astype(NARROW)

        gather_plan = (
            [(EMBED,) + item for item in column_chunks(width, 384)]
            + [(JOINT,) + item for item in column_chunks(3 * width, width)]
            + [(OUT, 0, width)]
            + [(EXPAND,) + item for item in column_chunks(mlp, width)]
            + [(SHRINK,) + item for item in column_chunks(width, 128)]
        )
        reduce_plan = (
            [(SHRINK,) + item for item in column_chunks(width, 256)]
            + [(EXPAND,) + item for item in column_chunks(mlp, width)]
            + [(OUT, 0, width)]
            + [(JOINT, part * width + at, 384) for at in (0, 384) for part in range(3)]
            + [(EMBED,) + item for item in column_chunks(width, 256)]
        )
        steps, folds = len(gather_plan), len(reduce_plan)
        vmem, dma = pltpu.VMEM, pltpu.SemaphoreType.DMA

        def shares(make):
            splits = [reduce_split(n, rows) for n, (rows, _) in enumerate(sizes)]
            return [make(rows, cols, max(share, 16), share + both) for (rows, cols), (share, both) in zip(sizes, splits)]

        def square(cols):
            return vmem((tokens, cols), NARROW)

        scratch = dict(
            full=[vmem((4, 2) + item, NARROW) for item in sizes],
            shrink_grad=vmem((4, 2) + sizes[SHRINK], NARROW),
            core_shrink=vmem((4, 2, sizes[SHRINK][0] // 2, width), NARROW),
            core_embed=vmem((4, 2, sizes[EMBED][0] // 2, width), NARROW),
            from_y=shares(lambda rows, cols, share, mine: vmem((4, 2, share, cols), NARROW)),
            from_x=shares(lambda rows, cols, share, mine: vmem((4, mine, cols), NARROW)),
            from_z=shares(lambda rows, cols, share, mine: vmem((3, mine, cols), NARROW)),
            part_out=shares(lambda rows, cols, share, mine: vmem((mine, cols), NARROW)),
            part_in=shares(lambda rows, cols, share, mine: vmem((mine, cols), NARROW)),
            final=shares(lambda rows, cols, share, mine: vmem((rows // 2, cols), WIDE)),
            resid=vmem((tokens, width), WIDE),
            work=vmem((tokens, width), WIDE),
            bias=square(tokens),
            unit1=square(width),
            unit2=square(width),
            normed=square(width),
            normed_mid=square(width),
            mixed=square(width),
            cot=square(width),
            low=square(width),
            scale1=vmem((tokens, 1), WIDE),
            scale2=vmem((tokens, 1), WIDE),
            proj=square(3 * width),
            mixed_t=vmem((width, tokens), NARROW),
            lse=vmem((16, tokens), WIDE),
            delta=vmem((16, tokens), WIDE),
            pull=square(mlp),
            hidden=square(mlp),
            stem=square(stem_width),
            vecs=vmem((VECTOR_ROWS, width), WIDE),
            vec_all=vmem((4, 2, VECTOR_ROWS, width), NARROW),
            vec_sum=vmem((6, VECTOR_ROWS, width), WIDE),
            vec_from=vmem((5, VECTOR_ROWS, width), WIDE),
            fold=vmem((24, width), WIDE),
            fill=dma((steps,)),
            g_send=dma((9, steps)),
            g_recv=dma((9, steps)),
            r_send=dma((6, folds)),
            r_recv=dma((6, folds)),
            r_done=dma((folds,)),
            load=dma((2,)),
            v_send=dma((7,)),
            v_recv=dma((7,)),
            free=pltpu.SemaphoreType.REGULAR,
        )
        names = list(scratch)

        def body(*refs):
            fused_kernel(tokens, width, stem_width, mlp, sizes, gather_plan, reduce_plan, names, *refs)

        far = pl.BlockSpec(memory_space=pl.ANY)
        near = pl.BlockSpec(memory_space=pltpu.VMEM)
        outs = pl.pallas_call(
            body,
            out_shape=(
                jax.ShapeDtypeStruct((tokens, width), NARROW),
                jax.ShapeDtypeStruct((tokens, stem_width), NARROW),
            )
            + tuple(jax.ShapeDtypeStruct(item, WIDE) for item in sizes)
            + (jax.ShapeDtypeStruct((VECTOR_ROWS, width), WIDE),),
            in_specs=[near, pl.BlockSpec(memory_space=pltpu.SMEM)] + [far] * 7,
            out_specs=(far,) * 7 + (near,),
            scratch_shapes=list(scratch.values()),
            compiler_params=pltpu.CompilerParams(
                collective_id=0, has_side_effects=True, vmem_limit_bytes=64 * 2**20
            ),
        )(vec_in, lengths, stem_features[0], cotangent[0], *shards)
        act, stem_grad, grads, vec_out = outs[0], outs[1], outs[2:7], outs[7]
        mine = lax.dynamic_slice(vec_out, (0, fsdp * piece), (9, piece))
        mine_expand = vec_out[9:used].reshape(mlp)
        mine_expand = lax.dynamic_slice(mine_expand, (fsdp * expand_bias.shape[0],), expand_bias.shape)
        return (
            act[None],
            stem_grad[None],
            grads[EMBED],
            mine[EMBED_BIAS],
            mine[FIRST_GAIN],
            mine[FIRST_SHIFT],
            grads[JOINT],
            mine[QUERY_BIAS],
            mine[VALUE_BIAS],
            grads[OUT],
            mine[OUT_BIAS],
            mine[SECOND_GAIN],
            mine[SECOND_SHIFT],
            grads[EXPAND],
            mine_expand,
            grads[SHRINK],
            mine[SHRINK_BIAS],
        )

    return local


def normalize(values):
    center = values - jnp.mean(values, axis=-1, keepdims=True)
    scaled = lax.rsqrt(jnp.mean(center * center, axis=-1, keepdims=True) + 1e-06)
    return (center * scaled, scaled)


def norm_backward(upstream, unit, scaled, gain):
    gain_part = jnp.sum(upstream * unit, axis=0)
    shift_part = jnp.sum(upstream, axis=0)
    inner = upstream * gain
    result = scaled * (
        inner
        - jnp.mean(inner, axis=-1, keepdims=True)
        - unit * jnp.mean(inner * unit, axis=-1, keepdims=True)
    )
    return (result, gain_part, shift_part)


def region_mask(lengths, row_len):
    bounds = jnp.cumsum(lengths, axis=1)
    places = jnp.arange(row_len, dtype=jnp.int32)
    labels = jnp.sum((places[None, :, None] >= bounds[:, None, :]).astype(jnp.int32), axis=2)
    return labels[:, :, None] == labels[:, None, :]


def column_sum(matrix):
    return jnp.sum(matrix.astype(jnp.float32), axis=0)


def general(
    stem_features,
    lengths,
    embed_weight,
    embed_bias,
    before_gain,
    before_shift,
    joint_weight,
    query_bias,
    value_bias,
    output_weight,
    output_bias,
    middle_gain,
    middle_shift,
    expand_weight,
    expand_bias,
    shrink_weight,
    shrink_bias,
    cotangent,
):
    wide = jnp.float32
    narrow = jnp.bfloat16
    shards = (
        embed_weight,
        embed_bias,
        before_gain,
        before_shift,
        joint_weight,
        query_bias,
        value_bias,
        output_weight,
        output_bias,
        middle_gain,
        middle_shift,
        expand_weight,
        expand_bias,
        shrink_weight,
        shrink_bias,
    )
    gathered = tuple(lax.all_gather(item, AXIS, axis=0, tiled=True) for item in shards)
    (
        embedding,
        embed_offset,
        first_gain,
        first_shift,
        joint,
        query_offset,
        value_offset,
        outward,
        out_offset,
        second_gain,
        second_shift,
        expand,
        expand_offset,
        shrink,
        shrink_offset,
    ) = gathered
    rows, row_len, stem_width = stem_features.shape
    width = embed_weight.shape[1]
    tokens = rows * row_len
    factor = 1.0 / math.sqrt(HEAD_DIM)
    heads_shape = (rows, row_len, HEADS, HEAD_DIM)
    same_region = region_mask(lengths, row_len)[:, None]
    inputs = stem_features.reshape(tokens, stem_width)
    embedded = jnp.dot(inputs, embedding, preferred_element_type=wide) + embed_offset.astype(wide)
    unit_first, scale_first = normalize(embedded)
    normed = (unit_first * first_gain.astype(wide) + first_shift.astype(wide)).astype(narrow)
    joint_offset = jnp.concatenate(
        [query_offset, jnp.zeros_like(query_offset), value_offset]
    ).astype(wide)
    projected = (jnp.dot(normed, joint, preferred_element_type=wide) + joint_offset).astype(narrow)
    query = projected[:, :width].reshape(heads_shape)
    keys = projected[:, width : 2 * width].reshape(heads_shape)
    values = projected[:, 2 * width :].reshape(heads_shape)

    def masked_scores():
        products = jnp.einsum("rqhe,rkhe->rhqk", query, keys, preferred_element_type=wide) * factor
        return jnp.where(same_region, products, -1e30)

    scores = masked_scores()
    largest = jnp.max(scores, axis=-1, keepdims=True)
    expos = jnp.exp(scores - largest)
    totals = jnp.sum(expos, axis=-1, keepdims=True)
    log_total = largest + jnp.log(totals)
    attend = (expos / totals).astype(narrow)
    mixed = jnp.einsum("rhqk,rkhe->rqhe", attend, values, preferred_element_type=wide)
    mixed = mixed.reshape(tokens, width).astype(narrow)
    residual = (
        embedded + jnp.dot(mixed, outward, preferred_element_type=wide) + out_offset.astype(wide)
    )
    unit_second, scale_second = normalize(residual)
    normed_mid = (unit_second * second_gain.astype(wide) + second_shift.astype(wide)).astype(narrow)
    upper = jnp.dot(normed_mid, expand, preferred_element_type=wide) + expand_offset.astype(wide)
    hidden_wide, gelu_pull = jax.vjp(lambda inner: jax.nn.gelu(inner, approximate=False), upper)
    hidden = hidden_wide.astype(narrow)
    output = (
        residual + jnp.dot(hidden, shrink, preferred_element_type=wide) + shrink_offset.astype(wide)
    )
    activations = output.astype(narrow).reshape(rows, row_len, width)
    backward_set = gathered
    embedding = backward_set[0]
    first_gain = backward_set[2]
    joint = backward_set[4]
    outward = backward_set[7]
    second_gain = backward_set[9]
    expand = backward_set[11]
    shrink = backward_set[13]
    upstream = cotangent.reshape(tokens, width).astype(wide)
    upstream_low = upstream.astype(narrow)
    shrink_grad = jnp.einsum("tm,td->md", hidden, upstream_low, preferred_element_type=wide)
    shrink_offset_grad = column_sum(upstream_low)
    hidden_grad = jnp.einsum("td,md->tm", upstream_low, shrink, preferred_element_type=wide)
    upper_grad = gelu_pull(hidden_grad)[0].astype(narrow)
    expand_grad = jnp.einsum("td,tm->dm", normed_mid, upper_grad, preferred_element_type=wide)
    expand_offset_grad = column_sum(upper_grad)
    normed_mid_grad = jnp.einsum("tm,dm->td", upper_grad, expand, preferred_element_type=wide)
    second_part, second_gain_grad, second_shift_grad = norm_backward(
        normed_mid_grad, unit_second, scale_second, second_gain.astype(wide)
    )
    residual_grad = upstream + second_part
    residual_low = residual_grad.astype(narrow)
    outward_grad = jnp.einsum("te,td->ed", mixed, residual_low, preferred_element_type=wide)
    out_offset_grad = column_sum(residual_low)
    mixed_grad = jnp.einsum("td,ed->te", residual_low, outward, preferred_element_type=wide)
    mixed_grad = mixed_grad.astype(narrow).reshape(heads_shape)
    attend_wide = jnp.exp(masked_scores() - log_total)
    attend = attend_wide.astype(narrow)
    values_grad = jnp.einsum("rhqk,rqhe->rkhe", attend, mixed_grad, preferred_element_type=wide)
    attend_grad = jnp.einsum("rqhe,rkhe->rhqk", mixed_grad, values, preferred_element_type=wide)
    centered = jnp.sum(attend_grad * attend_wide, axis=-1, keepdims=True)
    scores_grad = (attend_wide * (attend_grad - centered)).astype(narrow)
    query_grad = (
        jnp.einsum("rhqk,rkhe->rqhe", scores_grad, keys, preferred_element_type=wide) * factor
    )
    keys_grad = (
        jnp.einsum("rhqk,rqhe->rkhe", scores_grad, query, preferred_element_type=wide) * factor
    )
    projected_grad = jnp.concatenate(
        [
            query_grad.reshape(tokens, width),
            keys_grad.reshape(tokens, width),
            values_grad.reshape(tokens, width),
        ],
        axis=1,
    ).astype(narrow)
    joint_grad = jnp.einsum("td,tj->dj", normed, projected_grad, preferred_element_type=wide)
    query_offset_grad = column_sum(projected_grad[:, :width])
    value_offset_grad = column_sum(projected_grad[:, 2 * width :])
    normed_grad = jnp.einsum("tj,dj->td", projected_grad, joint, preferred_element_type=wide)
    first_part, first_gain_grad, first_shift_grad = norm_backward(
        normed_grad, unit_first, scale_first, first_gain.astype(wide)
    )
    embedded_low = (residual_grad + first_part).astype(narrow)
    embedding_grad = jnp.einsum("ts,td->sd", inputs, embedded_low, preferred_element_type=wide)
    embed_offset_grad = column_sum(embedded_low)
    stem_gradient = jnp.einsum("td,sd->ts", embedded_low, embedding, preferred_element_type=wide)
    stem_gradient = stem_gradient.astype(narrow).reshape(rows, row_len, stem_width)
    terms = (
        embedding_grad,
        embed_offset_grad,
        first_gain_grad,
        first_shift_grad,
        joint_grad,
        query_offset_grad,
        value_offset_grad,
        outward_grad,
        out_offset_grad,
        second_gain_grad,
        second_shift_grad,
        expand_grad,
        expand_offset_grad,
        shrink_grad,
        shrink_offset_grad,
    )
    owned = tuple(lax.psum_scatter(item, AXIS, scatter_dimension=0, tiled=True) for item in terms)
    summed = lax.psum(owned, "dp")
    return (activations, stem_gradient) + tuple(summed)


def solution(mesh):
    rows, whole, vector = P(("dp", AXIS), None, None), P(AXIS, None), P(AXIS)
    params = (whole, vector, vector, vector, whole, vector, vector, whole, vector)
    params = params + (vector, vector, whole, vector, whole, vector)
    plain = mesh.shape["dp"] != 4 or mesh.shape[AXIS] != 8
    return jax.shard_map(
        general if plain else fused(mesh),
        mesh=mesh,
        in_specs=(rows, P(("dp", AXIS), None)) + params + (rows,),
        out_specs=(rows, rows) + params,
        check_vma=False,
    )
```

```python
import math
import types

import jax
import jax.numpy as jnp
from jax import lax
from jax.experimental import pallas as pl
from jax.experimental.pallas import tpu as pltpu
from jax.sharding import PartitionSpec as P

HEADS = 12
HEAD_DIM = 64
AXIS = "fsdp"
MESH = pl.DeviceIdType.MESH
WIDE = jnp.float32
NARROW = jnp.bfloat16

EMBED_BIAS, FIRST_GAIN, FIRST_SHIFT, QUERY_BIAS, VALUE_BIAS, OUT_BIAS = 0, 1, 2, 3, 4, 5
SECOND_GAIN, SECOND_SHIFT, SHRINK_BIAS, EXPAND_BIAS = 6, 7, 8, 9
VECTOR_ROWS = 16

EMBED, JOINT, OUT, EXPAND, SHRINK = 0, 1, 2, 3, 4

GATHER_STEPS = (256, 768, 768, 768, 128)
REDUCE_STEPS = (128, 384, 768, 768, 256)
GATHER_SHARES = (2, 2, 1, 1, 1, 1, 1, 0, 1, 1, 1, 6, 6, 6, 3, 5, 0)
REDUCE_SHARES = (0, 5, 4, 1, 0, 1, 1, 1, 1, 1, 0, 1, 1, 1, 1, 2, 1, 2, 2, 2)
ORDER = (
    32, 33, 34, 35, 64, 65, 66, 67, 0, 544, 96, 128, 97, 129, 98, 130, 545, 99, 131, 0,
    160, 36, 161, 37, 162, 38, 163, 39, 100, 132, 192, 193, 194, 101, 133, 195, 102, 134, 164, 40,
    68, 224, 165, 41, 69, 103, 135, 225, 166, 42, 70, 226, 256, 0, 257, 0, 258, 0, 196, 0,
    227, 167, 43, 71, 104, 136, 288, 197, 289, 105, 137, 290, 259, 0, 228, 168, 44, 72, 169, 45,
    73, 106, 138, 198, 291, 229, 260, 0, 107, 139, 199, 170, 46, 74, 261, 0, 171, 47, 75, 292,
    0, 108, 230, 140, 0, 109, 231, 141, 293, 0, 172, 48, 76, 262, 0, 200, 110, 173, 77, 142,
    263, 0, 201, 111, 143, 0, 174, 78, 294, 0, 112, 232, 175, 79, 144, 295, 0, 0, 202, 233,
    203, 264, 176, 80, 0, 0, 204, 265, 0, 234, 205, 296, 0, 235, 297, 206, 0, 266, 236, 0,
    207, 267, 237, 238, 0, 320, 321, 322, 268, 208, 298, 0, 269, 270, 299, 239, 240, 352, 300, 353,
    301, 354, 302, 271, 272, 0, 0, 0, 303, 304, 0, 0, 385, 416, 0, 0, 323, 386, 0, 324,
    0, 325, 417, 0, 326, 355, 356, 0, 357, 448, 0, 358, 418, 0, 327, 0, 0, 387, 449, 0,
    359, 420, 0, 389, 0, 450, 0, 480, 0, 328, 419, 0, 329, 0, 330, 0, 390, 360, 361, 481,
    421, 452, 362, 512, 0, 0, 391, 451, 513, 0, 482, 422, 0, 0, 331, 392, 0, 332, 453, 0,
    333, 426, 393, 514, 0, 363, 484, 364, 365, 483, 454, 0, 334, 423, 485, 0, 335, 0, 336, 0,
    337, 0, 338, 0, 339, 424, 516, 0, 366, 458, 395, 367, 368, 369, 425, 370, 577, 371, 396, 515,
    517, 0, 455, 397, 578, 427, 486, 398, 456, 490, 579, 428, 457, 399, 518, 400, 580, 429, 522, 459,
    401, 430, 581, 431, 402, 432, 460, 403, 433, 487, 461, 488, 434, 489, 462, 491, 435, 463, 492, 464,
    493, 519, 465, 494, 520, 521, 466, 495, 523, 467, 524, 496, 497, 525, 498, 526, 499, 527, 528, 529,
    530, 531,
)


def nn(left, right):
    return lax.dot_general(left, right, (((1,), (0,)), ((), ())), preferred_element_type=WIDE)


def nt(left, right):
    return lax.dot_general(left, right, (((1,), (1,)), ((), ())), preferred_element_type=WIDE)


def tn(left, right):
    return lax.dot_general(left, right, (((0,), (0,)), ((), ())), preferred_element_type=WIDE)


def aligned(value, step):
    return pl.multiple_of(value, step)


def gelu_pair(upper):
    cdf = 0.5 * (1.0 + lax.erf(upper * (1.0 / math.sqrt(2.0))))
    density = jnp.exp(-0.5 * upper * upper) * (1.0 / math.sqrt(2.0 * math.pi))
    return upper * cdf, cdf + upper * density


def column_chunks(width, step):
    return [(start, step) for start in range(0, width, step)]


def fused_kernel(tokens, width, stem_width, mlp, sizes, gather_plan, reduce_plan, names, *refs):
    vec_in, lengths, stem_hbm, cot_hbm = refs[:4]
    shard, (act_hbm, stem_grad_hbm) = refs[4:9], refs[9:11]
    result, vec_out = refs[11:16], refs[16]
    ref = types.SimpleNamespace(**dict(zip(names, refs[17:])))
    full = ref.full
    local_grad = [ref.core_shrink] + list(full[1:4]) + [ref.shrink_grad]
    resid, work, bias = ref.resid, ref.work, ref.bias
    unit1, unit2, scale1, scale2 = ref.unit1, ref.unit2, ref.scale1, ref.scale2
    normed, normed_mid, proj = ref.normed, ref.normed_mid, ref.proj
    mixed_t, mixed, lse, delta = ref.mixed_t, ref.mixed, ref.lse, ref.delta
    pull, hidden, cot, stem, low = ref.pull, ref.hidden, ref.cot, ref.stem, ref.low
    vecs, vec_all, vec_sum = ref.vecs, ref.vec_all, ref.vec_sum
    fold = ref.fold

    dp, fs = lax.axis_index("dp"), lax.axis_index(AXIS)
    y, c = lax.div(dp, 2), lax.rem(dp, 2)
    z, x = lax.div(fs, 2), lax.rem(fs, 2)
    z_others = (z + 1 - 2 * lax.rem(z, 2), lax.rem(z + 2, 4), 3 - z)
    at_core = (y * 2 + 1 - c, fs)
    at_y = ((1 - y) * 2 + c, fs)
    at_x = (dp, z * 2 + 1 - x)
    at_z = tuple((dp, other * 2 + x) for other in z_others)

    def send(src, dst, send_sem, recv_sem, where):
        return pltpu.make_async_remote_copy(
            src_ref=src,
            dst_ref=dst,
            send_sem=send_sem,
            recv_sem=recv_sem,
            device_id=where,
            device_id_type=MESH,
        )


    up = lax.div(z, 2)
    inner = (z == 1) | (z == 2)
    arrivals = (z_others[0], 2 - up, 3 - 3 * up)
    fill, g_send, g_recv = ref.fill, ref.g_send, ref.g_recv

    def gather_refs(k):
        weight, start, count, share = gather_plan[k]
        half = sizes[weight][0] // 2
        both = half - 2 * share
        mine = pl.ds(aligned(c * half + y * share, 16), share + both)
        passed = pl.ds(aligned(c * half + y * (share + both), 16), share)
        halves = pl.ds(aligned(c * half, 16), half)
        return full[weight], shard[weight], mine, passed, halves, pl.ds(start, count)

    def fill_copy(k):
        whole, own, _, _, halves, cols = gather_refs(k)
        return pltpu.make_async_copy(own.at[halves, cols], whole.at[z, x, halves, cols], fill.at[k])

    def own_copy(k, sent, got, where):
        whole, own, mine, _, _, cols = gather_refs(k)
        return send(own.at[mine, cols], whole.at[z, x, mine, cols], g_send.at[sent, k], g_recv.at[got, k], where)

    def same_copy(part, k, sent, got, where):
        return send(part, part, g_send.at[sent, k], g_recv.at[got, k], where)

    def z_copy(k, order, sent, got, where):
        whole, _, mine, _, _, cols = gather_refs(k)
        return same_copy(whole.at[arrivals[order], x, mine, cols], k, sent, got, where)

    def across(k, step):
        order, got, where = ((0, 2, at_z[2]), (1, 1, at_z[0]), (2, 2, at_z[0]))[step]
        return z_copy(k, order, 1, got, where)

    def x_copy(k, order):
        whole, _, mine, _, _, cols = gather_refs(k)
        return same_copy(whole.at[arrivals[order], x, mine, cols], k, 2, 3, at_x)

    def inner_bytes(k):
        whole, _, mine, _, _, cols = gather_refs(k)
        return same_copy(whole.at[:, x, mine, cols], k, 1, 1, at_z[2])

    def x_bytes(k):
        whole, _, mine, _, _, cols = gather_refs(k)
        return same_copy(whole.at[:, x, mine, cols], k, 2, 3, at_x)

    def y_copy(k, order):
        whole, _, _, passed, _, cols = gather_refs(k)
        return same_copy(whole.at[arrivals[order], x, passed, cols], k, 3, 4, at_y)

    def y_bytes(k):
        whole, _, _, passed, _, cols = gather_refs(k)
        return same_copy(whole.at[pl.ds(0, 3), x, passed, cols], k, 3, 4, at_y)

    def y_copy_late(k):
        whole, _, _, passed, _, cols = gather_refs(k)
        return same_copy(whole.at[:, 1 - x, passed, cols], k, 4, 5, at_y)

    def core_copy(k):
        whole, _, _, _, halves, cols = gather_refs(k)
        return same_copy(whole.at[:, :, halves, cols], k, 5, 6, at_core)

    def start_z(k):
        own_copy(k, 0, 0, at_z[0]).start()

        @pl.when(inner)
        def _():
            own_copy(k, 1, 1, at_z[2]).start()

        fill_copy(k).start()

    def start_x(k):
        own_copy(k, 2, 3, at_x).start()

    def gather_z(order):
        def step(k):
            z_copy(k, order, order, order, at_z[0]).wait_recv()

            @pl.when(inner)
            def _():
                across(k, order).start()

            x_copy(k, order).start()
            if gather_plan[k][3]:
                y_copy(k, order).start()

        return step

    def gather_x(k):
        x_bytes(k).wait_recv()
        if gather_plan[k][3]:
            y_copy_late(k).start()

    def gather_y(k):
        fill_copy(k).wait()
        if gather_plan[k][3]:
            y_bytes(k).wait_recv()
            y_copy_late(k).wait_recv()
        core_copy(k).start()

    def gather_core(k):
        core_copy(k).wait_recv()

    def gather_sent(k):
        own_copy(k, 0, 0, at_z[0]).wait_send()

        @pl.when(inner)
        def _():
            inner_bytes(k).wait_send()

        x_bytes(k).wait_send()
        if gather_plan[k][3]:
            y_bytes(k).wait_send()
            y_copy_late(k).wait_send()
        core_copy(k).wait_send()

    r_send, r_recv, r_done = g_send, ref.r_recv, ref.r_done
    from_y, from_x, from_z = ref.from_y, ref.from_x, ref.from_z
    part_out, part_in, final = ref.part_out, ref.part_in, ref.final
    free = ref.free

    def core_slot(k):
        weight, start, count, _ = reduce_plan[k]
        if weight == SHRINK:
            return ref.core_shrink.at[:, :, :, pl.ds(start, count)]
        if weight == EMBED:
            return ref.core_embed.at[:, :, :, pl.ds(start, count)]
        half = sizes[weight][0] // 2
        before = {EXPAND: 0, OUT: mlp // width, JOINT: mlp // width + 1}[weight]
        return full[SHRINK].at[:, :, pl.ds((before + start // width) * half, half), pl.ds(start % width, count)]

    def reduce_refs(k):
        weight, start, count, share = reduce_plan[k]
        half = sizes[weight][0] // 2
        return weight, half, share, half - 2 * share, pl.ds(start, count)

    def r1_copy(k):
        weight, half, _, _, cols = reduce_refs(k)
        src = local_grad[weight].at[:, :, pl.ds(aligned((1 - c) * half, 16), half), cols]
        return send(src, core_slot(k), r_send.at[0, k], r_recv.at[0, k], at_core)

    def r2_copy(k):
        weight, half, share, both, cols = reduce_refs(k)
        rows = pl.ds(aligned(c * half + (1 - y) * (share + both), 16), share)
        return send(
            local_grad[weight].at[:, :, rows, cols],
            from_y[k],
            r_send.at[1, k],
            r_recv.at[1, k],
            at_y,
        )

    def mine_rows(half, share, both):
        return pl.ds(aligned(c * half + y * share, 16), share + both)

    def r3_copy(k):
        weight, half, share, both, cols = reduce_refs(k)
        return send(
            local_grad[weight].at[:, 1 - x, mine_rows(half, share, both), cols],
            from_x[k],
            r_send.at[2, k],
            r_recv.at[2, k],
            at_x,
        )

    def r4_copy(k, j):
        weight, half, share, both, cols = reduce_refs(k)
        return send(
            local_grad[weight].at[z_others[j], x, mine_rows(half, share, both), cols],
            from_z[k].at[j],
            r_send.at[3, k],
            r_recv.at[3, k],
            at_z[j],
        )

    def r4_bytes(k):
        return send(from_z[k], from_z[k], r_send.at[3, k], r_recv.at[3, k], at_z[0])

    def r5_copy(k):
        return send(part_out[k], part_in[k], r_send.at[4, k], r_recv.at[4, k], at_y)

    def r6_copies(k):
        weight, half, _, _, cols = reduce_refs(k)
        rows = pl.ds(aligned(c * half, 16), half)
        src, dst = final[k], result[weight].at[rows, cols]
        return (
            send(src, dst, r_send.at[5, k], r_recv.at[5, k], at_core),
            pltpu.make_async_copy(src, dst, r_done.at[k]),
        )

    def r6_incoming(k):
        weight, half, _, _, cols = reduce_refs(k)
        rows = pl.ds(aligned((1 - c) * half, 16), half)
        part = result[weight].at[rows, cols]
        return send(part, part, r_send.at[5, k], r_recv.at[5, k], at_core)

    def reduce_1(k):
        if reduce_plan[k][:2] == (EXPAND, 0):
            pl.semaphore_wait(free, 1)
        r1_copy(k).start()

    def reduce_2(k):
        weight, half, share, _, cols = reduce_refs(k)
        r1_copy(k).wait_recv()
        slot, total = core_slot(k), local_grad[weight]
        rows = pl.ds(aligned(c * half, 16), half)
        for i in range(4):
            for j in range(2):
                total[i, j, rows, cols] = total[i, j, rows, cols] + slot[i, j]
        if share:
            r2_copy(k).start()
        else:
            r3_copy(k).start()

    def reduce_3(k):
        weight, half, share, both, cols = reduce_refs(k)
        r2_copy(k).wait_recv()
        total = local_grad[weight]
        rows = pl.ds(aligned(c * half + y * (share + both), 16), share)
        for i in range(4):
            for j in range(2):
                total[i, j, rows, cols] = total[i, j, rows, cols] + from_y[k][i, j]
        r3_copy(k).start()

    def reduce_4(k):
        weight, half, share, both, cols = reduce_refs(k)
        r3_copy(k).wait_recv()
        total = local_grad[weight]
        rows = mine_rows(half, share, both)
        for i in range(4):
            total[i, x, rows, cols] = total[i, x, rows, cols] + from_x[k][i]
        for j in range(3):
            r4_copy(k, j).start()

    def reduce_5(k):
        weight, half, share, both, cols = reduce_refs(k)
        r4_bytes(k).wait_recv()
        value = local_grad[weight][z, x, mine_rows(half, share, both), cols].astype(WIDE)
        for j in range(3):
            value = value + from_z[k][j].astype(WIDE)
        part_out[k][...] = value.astype(NARROW)
        r5_copy(k).start()

    def reduce_6(k):
        _, half, share, both, _ = reduce_refs(k)
        r5_copy(k).wait_recv()
        own, came, whole = part_out[k], part_in[k], final[k]

        def rows(start, count):
            return pl.ds(aligned(start, 16), count)

        if share:
            whole[rows(y * (share + both), share), :] = own[rows(y * both, share), :].astype(WIDE)
            whole[rows((1 - y) * (share + both), share), :] = came[rows((1 - y) * both, share), :].astype(WIDE)
        if both:
            whole[share : share + both, :] = own[rows((1 - y) * share, both), :].astype(WIDE) + came[
                rows(y * share, both), :
            ].astype(WIDE)
        for copy in r6_copies(k):
            copy.start()

    def reduce_7(k):
        r6_incoming(k).wait_recv()
        r1_copy(k).wait_send()
        if reduce_refs(k)[2]:
            r2_copy(k).wait_send()
        r3_copy(k).wait_send()
        r4_bytes(k).wait_send()
        r5_copy(k).wait_send()
        remote, local = r6_copies(k)
        remote.wait_send()
        local.wait()

    def row(place):
        return vecs[place : place + 1, :]

    def layer_norm(unit, scale, out, gain, shift):
        def step(n, carry):
            rows = pl.ds(aligned(n * 96, 96), 96)
            values = resid[rows, :]
            center = values - jnp.mean(values, axis=1, keepdims=True)
            factor = lax.rsqrt(jnp.mean(center * center, axis=1, keepdims=True) + 1e-6)
            units = center * factor
            scale[rows, :] = factor
            unit[rows, :] = units.astype(NARROW)
            out[rows, :] = (units * row(gain) + row(shift)).astype(NARROW)
            return carry

        lax.fori_loop(0, tokens // 96, step, 0)

    def eight(values):
        return jnp.sum(values.reshape(values.shape[0] // 8, 8, values.shape[1]), axis=0)

    def norm_backward(unit, scale, gain, upstream, keep_wide, places):
        fold[...] = jnp.zeros_like(fold)

        def step(n, carry):
            rows = pl.ds(aligned(n * 96, 96), 96)
            grads = work[rows, :]
            units = unit[rows, :].astype(WIDE)
            inner = grads * row(gain)
            fold[0:8, :] += eight(grads * units)
            fold[8:16, :] += eight(grads)
            value = upstream[rows, :].astype(WIDE) + scale[rows, :] * (
                inner
                - jnp.mean(inner, axis=1, keepdims=True)
                - units * jnp.mean(inner * units, axis=1, keepdims=True)
            )
            if keep_wide:
                resid[rows, :] = value
            narrow = value.astype(NARROW)
            low[rows, :] = narrow
            fold[16:24, :] += eight(narrow.astype(WIDE))
            return carry

        lax.fori_loop(0, tokens // 96, step, 0)
        for n, place in enumerate(places):
            vec_sum[0, place : place + 1, :] = jnp.sum(fold[8 * n : 8 * n + 8, :], axis=0, keepdims=True)

    def column_sum(source, start, place, at=0, count=width):
        def step(n, total):
            return total + eight(source[pl.ds(aligned(n * 96, 96), 96), start : start + count].astype(WIDE))

        total = lax.fori_loop(0, tokens // 96, step, jnp.zeros((8, count), WIDE))
        vec_sum[0, place : place + 1, at : at + count] = jnp.sum(total, axis=0, keepdims=True)

    lane = lax.broadcasted_iota(jnp.int32, (1, 2 * HEAD_DIM), 1)

    def head_lanes(head, value):
        return jnp.where((lane < HEAD_DIM) == (head == 0), value, 0.0).astype(NARROW)

    factor = 1.0 / math.sqrt(HEAD_DIM)

    def attend_forward(p):
        def run():
            at = p * 128
            query = proj[:, pl.ds(at, 128)]
            keys = proj[:, pl.ds(width + at, 128)]
            values_t = proj[:, pl.ds(2 * width + at, 128)].T
            for head in range(2):
                scores = nt(keys * head_lanes(head, factor), query) + bias[...].astype(WIDE)
                largest = jnp.max(scores, axis=0, keepdims=True)
                expos = jnp.exp(scores - largest)
                total = jnp.sum(expos, axis=0, keepdims=True)
                mix = nn(values_t[64 * head : 64 * head + 64], expos.astype(NARROW)) * (1.0 / total)
                mixed_t[pl.ds(aligned(at + 64 * head, 64), 64), :] = mix.astype(NARROW)
                lse[pl.ds(2 * p + head, 1), :] = largest + jnp.log(total)

        return run

    def attend_backward(p):
        def run():
            at = p * 128
            query = proj[:, pl.ds(at, 128)]
            keys = proj[:, pl.ds(width + at, 128)]
            values = proj[:, pl.ds(2 * width + at, 128)]
            grads = mixed[:, pl.ds(at, 128)]
            keys_t = keys.T
            value_grads, key_grads = [], []
            for head in range(2):
                scores = nt(keys * head_lanes(head, factor), query) + bias[...].astype(WIDE)
                attend = jnp.exp(scores - lse[pl.ds(2 * p + head, 1), :])
                attend_grad = nt(values * head_lanes(head, 1.0), grads)
                scores_grad = (attend * (attend_grad - delta[pl.ds(2 * p + head, 1), :])).astype(NARROW)
                value_grads.append(nn(attend.astype(NARROW), grads))
                key_grads.append(nn(scores_grad, query))
                query_grad = nn(keys_t[64 * head : 64 * head + 64], scores_grad) * factor
                mixed_t[pl.ds(aligned(at + 64 * head, 64), 64), :] = query_grad.astype(NARROW)
            first_head = lane < HEAD_DIM
            pull[:, pl.ds(2 * width + at, 128)] = jnp.where(first_head, *value_grads).astype(NARROW)
            pull[:, pl.ds(width + at, 128)] = (jnp.where(first_head, *key_grads) * factor).astype(NARROW)

        return run

    barrier = pltpu.get_barrier_semaphore()
    partners = (at_core, at_y, at_x) + at_z
    for partner in partners:
        pl.semaphore_signal(barrier, inc=1, device_id=partner, device_id_type=MESH)
    load_stem = pltpu.make_async_copy(stem_hbm, stem, ref.load.at[0])
    load_cot = pltpu.make_async_copy(cot_hbm, cot, ref.load.at[1])
    load_stem.start()
    load_cot.start()
    pl.semaphore_wait(barrier, len(partners))

    v_send, v_recv = ref.v_send, ref.v_recv
    vec_z = [send(vec_in, vec_all.at[z, x], v_send.at[0], v_recv.at[0], at_z[j]) for j in range(3)]
    vec_z_part = vec_all.at[pl.ds(0, 3), x]
    vec_z_bytes = send(vec_z_part, vec_z_part, v_send.at[0], v_recv.at[0], at_z[0])
    vec_x_part = vec_all.at[:, x]
    vec_x = send(vec_x_part, vec_x_part, v_send.at[1], v_recv.at[1], at_x)
    vec_all[z, x] = vec_in[...]
    for copy in vec_z:
        copy.start()

    def vec_gather(n):
        if n == 0:
            vec_z_bytes.wait_recv()
            vec_x.start()
        else:
            vec_x.wait_recv()

    vec_from = ref.vec_from
    vec_partners = (at_core, at_y, at_x, at_z[0], at_z[1])

    def vec_copy(n):
        return send(vec_sum.at[n], vec_from.at[n], v_send.at[2 + n], v_recv.at[2 + n], vec_partners[n])

    def vec_step(n):
        vec_copy(n - 1).wait_recv()
        vec_sum[n] = vec_sum[n - 1] + vec_from[n - 1]
        if n < len(vec_partners):
            vec_copy(n).start()

    blocks = []
    block = blocks.append

    @block
    def make_bias():
        places = lax.broadcasted_iota(jnp.int32, (1, tokens), 1)
        places_down = lax.broadcasted_iota(jnp.int32, (tokens, 1), 0)
        labels = jnp.zeros((1, tokens), jnp.int32)
        labels_down = jnp.zeros((tokens, 1), jnp.int32)
        bound = 0
        for n in range(lengths.shape[1]):
            bound = bound + lengths[0, n]
            labels = labels + (places >= bound).astype(jnp.int32)
            labels_down = labels_down + (places_down >= bound).astype(jnp.int32)
        bias[...] = jnp.where(labels_down == labels, 0.0, -1e30).astype(NARROW)
        vec_sum[0] = jnp.zeros((VECTOR_ROWS, width), WIDE)

    @block
    def add_vectors():
        totals = vec_all[0, 0].astype(WIDE)
        for i in range(4):
            for j in range(2):
                if i + j > 0:
                    totals = totals + vec_all[i, j].astype(WIDE)
        vecs[...] = totals
        vec_z_bytes.wait_send()
        vec_x.wait_send()
        load_stem.wait()
        load_cot.wait()

    def chunks(plan, weight):
        return [item[1:3] for item in plan if item[0] == weight]

    def embed(start, count):
        def run():
            piece = full[EMBED][:, :, :, start : start + count].reshape(stem_width, count)
            offset = vecs[EMBED_BIAS : EMBED_BIAS + 1, start : start + count]
            resid[:, start : start + count] = nn(stem[...], piece) + offset

        return run

    def project(start, count):
        def run():
            value = nn(normed[...], full[JOINT][:, :, :, start : start + count].reshape(width, count))
            at = start % width
            if start // width == 0:
                value = value + vecs[QUERY_BIAS : QUERY_BIAS + 1, at : at + count]
            if start // width == 2:
                value = value + vecs[VALUE_BIAS : VALUE_BIAS + 1, at : at + count]
            proj[:, start : start + count] = value.astype(NARROW)

        return run

    for item in chunks(gather_plan, EMBED):
        block(embed(*item))

    @block
    def first_norm():
        layer_norm(unit1, scale1, normed, FIRST_GAIN, FIRST_SHIFT)

    for item in chunks(gather_plan, JOINT):
        block(project(*item))
    for p in range(HEADS // 2):
        block(attend_forward(p))

    @block
    def join_heads():
        mixed[...] = mixed_t[...].T
        resid[...] = resid[...] + nn(mixed[...], full[OUT][...].reshape(width, width)) + row(OUT_BIAS)

    @block
    def second_norm():
        layer_norm(unit2, scale2, normed_mid, SECOND_GAIN, SECOND_SHIFT)

    def expand_forward(i):
        def run():
            start = i * width
            work[...] = nn(normed_mid[...], full[EXPAND][:, :, :, start : start + width].reshape(width, width))

            def gelu_step(n, carry):
                rows = pl.ds(aligned(n * 64, 64), 64)
                for at in range(0, width, 128):
                    offset = vecs[EXPAND_BIAS + i : EXPAND_BIAS + i + 1, at : at + 128]
                    value, slope = gelu_pair(work[rows, at : at + 128] + offset)
                    hidden[rows, start + at : start + at + 128] = value.astype(NARROW)
                    pull[rows, start + at : start + at + 128] = slope.astype(NARROW)
                return carry

            lax.fori_loop(0, tokens // 64, gelu_step, 0)

        return run

    rows_shrink = sizes[SHRINK][0]

    def shrink_gradient(i):
        def run():
            for j in range(2):
                at = rows_shrink * (2 * i + j)
                local_grad[SHRINK][i, j] = tn(hidden[:, at : at + rows_shrink], cot[...]).astype(NARROW)

        return run

    for i in range(4):
        block(expand_forward(i))
        block(shrink_gradient(i))

    @block
    def cotangent_sum():
        column_sum(cot, 0, SHRINK_BIAS)

    def hidden_backward(i):
        def run():
            at = i * width
            grads = nt(cot[...], full[SHRINK][i].reshape(width, width))
            pull[:, at : at + width] = (grads * pull[:, at : at + width].astype(WIDE)).astype(NARROW)
            column_sum(pull, at, EXPAND_BIAS + i)

        return run

    for i in range(4):
        block(hidden_backward(i))
    store_act = pltpu.make_async_copy(low, act_hbm, ref.load.at[0])
    store_stem = pltpu.make_async_copy(hidden.at[:, pl.ds(0, stem_width)], stem_grad_hbm, ref.load.at[1])

    @block
    def activations():
        value = nn(hidden[...], full[SHRINK][...].reshape(mlp, width))
        low[...] = (resid[...] + value + row(SHRINK_BIAS)).astype(NARROW)
        store_act.start()
        pl.semaphore_signal(free, inc=1, device_id=at_core, device_id_type=MESH)

    @block
    def expand_backward():
        work[...] = nt(pull[...], full[EXPAND][...].reshape(width, mlp))

    def expand_gradient(i):
        def run():
            at = i * width
            value = tn(normed_mid[...], pull[:, at : at + width]).astype(NARROW)
            full[EXPAND][:, :, :, at : at + width] = value.reshape(4, 2, width // 8, width)

        return run

    for i in range(4):
        block(expand_gradient(i))

    @block
    def second_norm_backward():
        store_act.wait()
        norm_backward(unit2, scale2, SECOND_GAIN, cot, True, (SECOND_GAIN, SECOND_SHIFT, OUT_BIAS))

    @block
    def out_backward():
        mixed[...] = nt(low[...], full[OUT][...].reshape(width, width)).astype(NARROW)

    @block
    def out_gradient():
        full[OUT][...] = nn(mixed_t[...], low[...]).astype(NARROW).reshape(4, 2, width // 8, width)

    @block
    def row_sums():
        grads_t = mixed[...].T
        for head in range(HEADS):
            span = slice(64 * head, 64 * head + 64)
            product = grads_t[span].astype(WIDE) * mixed_t[span, :].astype(WIDE)
            delta[head : head + 1, :] = jnp.sum(product, axis=0, keepdims=True)

    def gather_query(half):
        def run():
            at = half * width // 2
            pull[:, at : at + width // 2] = mixed_t[at : at + width // 2, :].T
            column_sum(pull, at, QUERY_BIAS, at, width // 2)
            column_sum(pull, 2 * width + at, VALUE_BIAS, at, width // 2)

        return run

    def joint_backward(half):
        def run():
            total = 0.0 if half == 0 else work[...]
            for part in range(3):
                at = part * width + half * width // 2
                weight = full[JOINT][:, :, :, at : at + width // 2].reshape(width, width // 2)
                total = total + nt(pull[:, at : at + width // 2], weight)
            work[...] = total

        return run

    def joint_gradient(start, count):
        def run():
            value = tn(normed[...], pull[:, start : start + count]).astype(NARROW)
            full[JOINT][:, :, :, start : start + count] = value.reshape(4, 2, width // 8, count)

        return run

    for half in range(2):
        for p in range(HEADS // 4):
            block(attend_backward(half * HEADS // 4 + p))
        block(gather_query(half))
        block(joint_backward(half))
        for item in chunks(reduce_plan, JOINT)[3 * half : 3 * half + 3]:
            block(joint_gradient(*item))

    @block
    def first_norm_backward():
        norm_backward(unit1, scale1, FIRST_GAIN, resid, False, (FIRST_GAIN, FIRST_SHIFT, EMBED_BIAS))

    rows_embed = sizes[EMBED][0]

    def embed_gradient(start, count):
        def run():
            value = tn(stem[...], low[:, start : start + count]).astype(NARROW)
            local_grad[EMBED][:, :, 0:rows_embed, start : start + count] = value.reshape(4, 2, rows_embed, count)

        return run

    for item in chunks(reduce_plan, EMBED):
        block(embed_gradient(*item))

    @block
    def start_vectors():
        vec_copy(0).start()

    @block
    def stem_backward():
        value = nt(low[...], full[EMBED][...].reshape(stem_width, width))
        hidden[:, 0:stem_width] = value.astype(NARROW)
        store_stem.start()

    work_left = iter(blocks)
    steps = (
        lambda k: pl.when(dp >= 0)(next(work_left)),
        start_z,
        start_x,
        gather_z(0),
        gather_z(1),
        gather_z(2),
        gather_x,
        gather_y,
        gather_core,
        gather_sent,
        reduce_1,
        reduce_2,
        reduce_3,
        reduce_4,
        reduce_5,
        reduce_6,
        reduce_7,
        vec_gather,
        vec_step,
    )
    for code in ORDER:
        steps[code // 32](code % 32)
    vec_out[...] = vec_sum[len(vec_partners)]
    for n in range(len(vec_partners)):
        vec_copy(n).wait_send()
    store_stem.wait()


def plans(width, mlp):
    gather_plan = (
        [(EMBED,) + item for item in column_chunks(width, GATHER_STEPS[EMBED])]
        + [(JOINT,) + item for item in column_chunks(3 * width, GATHER_STEPS[JOINT])]
        + [(OUT,) + item for item in column_chunks(width, GATHER_STEPS[OUT])]
        + [(EXPAND,) + item for item in column_chunks(mlp, GATHER_STEPS[EXPAND])]
        + [(SHRINK,) + item for item in column_chunks(width, GATHER_STEPS[SHRINK])]
    )
    halves = (0, width // 2)
    reduce_plan = (
        [(SHRINK,) + item for item in column_chunks(width, REDUCE_STEPS[SHRINK])]
        + [(EXPAND,) + item for item in column_chunks(mlp, REDUCE_STEPS[EXPAND])]
        + [(OUT,) + item for item in column_chunks(width, REDUCE_STEPS[OUT])]
        + [(JOINT, part * width + at, width // 2) for at in halves for part in range(3)]
        + [(EMBED,) + item for item in column_chunks(width, REDUCE_STEPS[EMBED])]
    )
    return (
        [item + (16 * n,) for item, n in zip(gather_plan, GATHER_SHARES)],
        [item + (16 * n,) for item, n in zip(reduce_plan, REDUCE_SHARES)],
    )


def fused(mesh):
    def local(
        stem_features,
        lengths,
        embed_weight,
        embed_bias,
        before_gain,
        before_shift,
        joint_weight,
        query_bias,
        value_bias,
        output_weight,
        output_bias,
        middle_gain,
        middle_shift,
        expand_weight,
        expand_bias,
        shrink_weight,
        shrink_bias,
        cotangent,
    ):
        _, tokens, stem_width = stem_features.shape
        width = embed_weight.shape[1]
        mlp = expand_weight.shape[1]
        shards = (embed_weight, joint_weight, output_weight, expand_weight, shrink_weight)
        sizes = [item.shape for item in shards]
        fsdp = lax.axis_index(AXIS)

        nine = jnp.stack(
            [
                embed_bias,
                before_gain,
                before_shift,
                query_bias,
                value_bias,
                output_bias,
                middle_gain,
                middle_shift,
                shrink_bias,
            ]
        )
        piece = nine.shape[1]
        owner = jnp.arange(width) // piece
        rows_nine = jnp.where(owner[None] == fsdp, jnp.tile(nine, (1, width // piece)), 0)
        owner = jnp.arange(mlp) // expand_bias.shape[0]
        rows_expand = jnp.where(owner == fsdp, jnp.tile(expand_bias, mlp // expand_bias.shape[0]), 0)
        rows_expand = rows_expand.reshape(mlp // width, width)
        used = 9 + mlp // width
        vec_in = jnp.concatenate([rows_nine, rows_expand, jnp.zeros((VECTOR_ROWS - used, width), NARROW)])
        vec_in = vec_in.astype(NARROW)

        gather_plan, reduce_plan = plans(width, mlp)
        steps, folds = len(gather_plan), len(reduce_plan)
        vmem, dma = pltpu.VMEM, pltpu.SemaphoreType.DMA

        def each(make):
            return [make(sizes[n][0] // 2, share, cols) for n, _, cols, share in reduce_plan]

        def square(cols):
            return vmem((tokens, cols), NARROW)

        scratch = dict(
            full=[vmem((4, 2) + item, NARROW) for item in sizes],
            shrink_grad=vmem((4, 2) + sizes[SHRINK], NARROW),
            core_shrink=vmem((4, 2, sizes[SHRINK][0] // 2, width), NARROW),
            core_embed=vmem((4, 2, sizes[EMBED][0] // 2, width), NARROW),
            from_y=each(lambda half, share, cols: vmem((4, 2, max(share, 16), cols if share else 128), NARROW)),
            from_x=each(lambda half, share, cols: vmem((4, half - share, cols), NARROW)),
            from_z=each(lambda half, share, cols: vmem((3, half - share, cols), NARROW)),
            part_out=each(lambda half, share, cols: vmem((half - share, cols), NARROW)),
            part_in=each(lambda half, share, cols: vmem((half - share, cols), NARROW)),
            final=each(lambda half, share, cols: vmem((half, cols), WIDE)),
            resid=vmem((tokens, width), WIDE),
            work=vmem((tokens, width), WIDE),
            bias=square(tokens),
            unit1=square(width),
            unit2=square(width),
            normed=square(width),
            normed_mid=square(width),
            mixed=square(width),
            cot=square(width),
            low=square(width),
            scale1=vmem((tokens, 1), WIDE),
            scale2=vmem((tokens, 1), WIDE),
            proj=square(3 * width),
            mixed_t=vmem((width, tokens), NARROW),
            lse=vmem((16, tokens), WIDE),
            delta=vmem((16, tokens), WIDE),
            pull=square(mlp),
            hidden=square(mlp),
            stem=square(stem_width),
            vecs=vmem((VECTOR_ROWS, width), WIDE),
            vec_all=vmem((4, 2, VECTOR_ROWS, width), NARROW),
            vec_sum=vmem((6, VECTOR_ROWS, width), WIDE),
            vec_from=vmem((5, VECTOR_ROWS, width), WIDE),
            fold=vmem((24, width), WIDE),
            fill=dma((steps,)),
            g_send=dma((6, max(steps, folds))),
            g_recv=dma((7, steps)),
            r_recv=dma((6, folds)),
            r_done=dma((folds,)),
            load=dma((2,)),
            v_send=dma((7,)),
            v_recv=dma((7,)),
            free=pltpu.SemaphoreType.REGULAR,
        )
        names = list(scratch)

        def body(*refs):
            fused_kernel(tokens, width, stem_width, mlp, sizes, gather_plan, reduce_plan, names, *refs)

        far = pl.BlockSpec(memory_space=pl.ANY)
        near = pl.BlockSpec(memory_space=pltpu.VMEM)
        outs = pl.pallas_call(
            body,
            out_shape=(
                jax.ShapeDtypeStruct((tokens, width), NARROW),
                jax.ShapeDtypeStruct((tokens, stem_width), NARROW),
            )
            + tuple(jax.ShapeDtypeStruct(item, WIDE) for item in sizes)
            + (jax.ShapeDtypeStruct((VECTOR_ROWS, width), WIDE),),
            in_specs=[near, pl.BlockSpec(memory_space=pltpu.SMEM)] + [far] * 7,
            out_specs=(far,) * 7 + (near,),
            scratch_shapes=list(scratch.values()),
            compiler_params=pltpu.CompilerParams(
                collective_id=0, has_side_effects=True, vmem_limit_bytes=64 * 2**20
            ),
        )(vec_in, lengths, stem_features[0], cotangent[0], *shards)
        act, stem_grad, grads, vec_out = outs[0], outs[1], outs[2:7], outs[7]
        mine = lax.dynamic_slice(vec_out, (0, fsdp * piece), (9, piece))
        mine_expand = vec_out[9:used].reshape(mlp)
        mine_expand = lax.dynamic_slice(mine_expand, (fsdp * expand_bias.shape[0],), expand_bias.shape)
        return (
            act[None],
            stem_grad[None],
            grads[EMBED],
            mine[EMBED_BIAS],
            mine[FIRST_GAIN],
            mine[FIRST_SHIFT],
            grads[JOINT],
            mine[QUERY_BIAS],
            mine[VALUE_BIAS],
            grads[OUT],
            mine[OUT_BIAS],
            mine[SECOND_GAIN],
            mine[SECOND_SHIFT],
            grads[EXPAND],
            mine_expand,
            grads[SHRINK],
            mine[SHRINK_BIAS],
        )

    return local


def normalize(values):
    center = values - jnp.mean(values, axis=-1, keepdims=True)
    scaled = lax.rsqrt(jnp.mean(center * center, axis=-1, keepdims=True) + 1e-06)
    return (center * scaled, scaled)


def norm_backward(upstream, unit, scaled, gain):
    gain_part = jnp.sum(upstream * unit, axis=0)
    shift_part = jnp.sum(upstream, axis=0)
    inner = upstream * gain
    result = scaled * (
        inner
        - jnp.mean(inner, axis=-1, keepdims=True)
        - unit * jnp.mean(inner * unit, axis=-1, keepdims=True)
    )
    return (result, gain_part, shift_part)


def region_mask(lengths, row_len):
    bounds = jnp.cumsum(lengths, axis=1)
    places = jnp.arange(row_len, dtype=jnp.int32)
    labels = jnp.sum((places[None, :, None] >= bounds[:, None, :]).astype(jnp.int32), axis=2)
    return labels[:, :, None] == labels[:, None, :]


def column_sum(matrix):
    return jnp.sum(matrix.astype(jnp.float32), axis=0)


def general(
    stem_features,
    lengths,
    embed_weight,
    embed_bias,
    before_gain,
    before_shift,
    joint_weight,
    query_bias,
    value_bias,
    output_weight,
    output_bias,
    middle_gain,
    middle_shift,
    expand_weight,
    expand_bias,
    shrink_weight,
    shrink_bias,
    cotangent,
):
    wide = jnp.float32
    narrow = jnp.bfloat16
    shards = (
        embed_weight,
        embed_bias,
        before_gain,
        before_shift,
        joint_weight,
        query_bias,
        value_bias,
        output_weight,
        output_bias,
        middle_gain,
        middle_shift,
        expand_weight,
        expand_bias,
        shrink_weight,
        shrink_bias,
    )
    gathered = tuple(lax.all_gather(item, AXIS, axis=0, tiled=True) for item in shards)
    (
        embedding,
        embed_offset,
        first_gain,
        first_shift,
        joint,
        query_offset,
        value_offset,
        outward,
        out_offset,
        second_gain,
        second_shift,
        expand,
        expand_offset,
        shrink,
        shrink_offset,
    ) = gathered
    rows, row_len, stem_width = stem_features.shape
    width = embed_weight.shape[1]
    tokens = rows * row_len
    factor = 1.0 / math.sqrt(HEAD_DIM)
    heads_shape = (rows, row_len, HEADS, HEAD_DIM)
    same_region = region_mask(lengths, row_len)[:, None]
    inputs = stem_features.reshape(tokens, stem_width)
    embedded = jnp.dot(inputs, embedding, preferred_element_type=wide) + embed_offset.astype(wide)
    unit_first, scale_first = normalize(embedded)
    normed = (unit_first * first_gain.astype(wide) + first_shift.astype(wide)).astype(narrow)
    joint_offset = jnp.concatenate(
        [query_offset, jnp.zeros_like(query_offset), value_offset]
    ).astype(wide)
    projected = (jnp.dot(normed, joint, preferred_element_type=wide) + joint_offset).astype(narrow)
    query = projected[:, :width].reshape(heads_shape)
    keys = projected[:, width : 2 * width].reshape(heads_shape)
    values = projected[:, 2 * width :].reshape(heads_shape)

    def masked_scores():
        products = jnp.einsum("rqhe,rkhe->rhqk", query, keys, preferred_element_type=wide) * factor
        return jnp.where(same_region, products, -1e30)

    scores = masked_scores()
    largest = jnp.max(scores, axis=-1, keepdims=True)
    expos = jnp.exp(scores - largest)
    totals = jnp.sum(expos, axis=-1, keepdims=True)
    log_total = largest + jnp.log(totals)
    attend = (expos / totals).astype(narrow)
    mixed = jnp.einsum("rhqk,rkhe->rqhe", attend, values, preferred_element_type=wide)
    mixed = mixed.reshape(tokens, width).astype(narrow)
    residual = (
        embedded + jnp.dot(mixed, outward, preferred_element_type=wide) + out_offset.astype(wide)
    )
    unit_second, scale_second = normalize(residual)
    normed_mid = (unit_second * second_gain.astype(wide) + second_shift.astype(wide)).astype(narrow)
    upper = jnp.dot(normed_mid, expand, preferred_element_type=wide) + expand_offset.astype(wide)
    hidden_wide, gelu_pull = jax.vjp(lambda inner: jax.nn.gelu(inner, approximate=False), upper)
    hidden = hidden_wide.astype(narrow)
    output = (
        residual + jnp.dot(hidden, shrink, preferred_element_type=wide) + shrink_offset.astype(wide)
    )
    activations = output.astype(narrow).reshape(rows, row_len, width)
    backward_set = gathered
    embedding = backward_set[0]
    first_gain = backward_set[2]
    joint = backward_set[4]
    outward = backward_set[7]
    second_gain = backward_set[9]
    expand = backward_set[11]
    shrink = backward_set[13]
    upstream = cotangent.reshape(tokens, width).astype(wide)
    upstream_low = upstream.astype(narrow)
    shrink_grad = jnp.einsum("tm,td->md", hidden, upstream_low, preferred_element_type=wide)
    shrink_offset_grad = column_sum(upstream_low)
    hidden_grad = jnp.einsum("td,md->tm", upstream_low, shrink, preferred_element_type=wide)
    upper_grad = gelu_pull(hidden_grad)[0].astype(narrow)
    expand_grad = jnp.einsum("td,tm->dm", normed_mid, upper_grad, preferred_element_type=wide)
    expand_offset_grad = column_sum(upper_grad)
    normed_mid_grad = jnp.einsum("tm,dm->td", upper_grad, expand, preferred_element_type=wide)
    second_part, second_gain_grad, second_shift_grad = norm_backward(
        normed_mid_grad, unit_second, scale_second, second_gain.astype(wide)
    )
    residual_grad = upstream + second_part
    residual_low = residual_grad.astype(narrow)
    outward_grad = jnp.einsum("te,td->ed", mixed, residual_low, preferred_element_type=wide)
    out_offset_grad = column_sum(residual_low)
    mixed_grad = jnp.einsum("td,ed->te", residual_low, outward, preferred_element_type=wide)
    mixed_grad = mixed_grad.astype(narrow).reshape(heads_shape)
    attend_wide = jnp.exp(masked_scores() - log_total)
    attend = attend_wide.astype(narrow)
    values_grad = jnp.einsum("rhqk,rqhe->rkhe", attend, mixed_grad, preferred_element_type=wide)
    attend_grad = jnp.einsum("rqhe,rkhe->rhqk", mixed_grad, values, preferred_element_type=wide)
    centered = jnp.sum(attend_grad * attend_wide, axis=-1, keepdims=True)
    scores_grad = (attend_wide * (attend_grad - centered)).astype(narrow)
    query_grad = (
        jnp.einsum("rhqk,rkhe->rqhe", scores_grad, keys, preferred_element_type=wide) * factor
    )
    keys_grad = (
        jnp.einsum("rhqk,rqhe->rkhe", scores_grad, query, preferred_element_type=wide) * factor
    )
    projected_grad = jnp.concatenate(
        [
            query_grad.reshape(tokens, width),
            keys_grad.reshape(tokens, width),
            values_grad.reshape(tokens, width),
        ],
        axis=1,
    ).astype(narrow)
    joint_grad = jnp.einsum("td,tj->dj", normed, projected_grad, preferred_element_type=wide)
    query_offset_grad = column_sum(projected_grad[:, :width])
    value_offset_grad = column_sum(projected_grad[:, 2 * width :])
    normed_grad = jnp.einsum("tj,dj->td", projected_grad, joint, preferred_element_type=wide)
    first_part, first_gain_grad, first_shift_grad = norm_backward(
        normed_grad, unit_first, scale_first, first_gain.astype(wide)
    )
    embedded_low = (residual_grad + first_part).astype(narrow)
    embedding_grad = jnp.einsum("ts,td->sd", inputs, embedded_low, preferred_element_type=wide)
    embed_offset_grad = column_sum(embedded_low)
    stem_gradient = jnp.einsum("td,sd->ts", embedded_low, embedding, preferred_element_type=wide)
    stem_gradient = stem_gradient.astype(narrow).reshape(rows, row_len, stem_width)
    terms = (
        embedding_grad,
        embed_offset_grad,
        first_gain_grad,
        first_shift_grad,
        joint_grad,
        query_offset_grad,
        value_offset_grad,
        outward_grad,
        out_offset_grad,
        second_gain_grad,
        second_shift_grad,
        expand_grad,
        expand_offset_grad,
        shrink_grad,
        shrink_offset_grad,
    )
    owned = tuple(lax.psum_scatter(item, AXIS, scatter_dimension=0, tiled=True) for item in terms)
    summed = lax.psum(owned, "dp")
    return (activations, stem_gradient) + tuple(summed)


def solution(mesh):
    rows, whole, vector = P(("dp", AXIS), None, None), P(AXIS, None), P(AXIS)
    params = (whole, vector, vector, vector, whole, vector, vector, whole, vector)
    params = params + (vector, vector, whole, vector, whole, vector)
    plain = mesh.shape["dp"] != 4 or mesh.shape[AXIS] != 8
    return jax.shard_map(
        general if plain else fused(mesh),
        mesh=mesh,
        in_specs=(rows, P(("dp", AXIS), None)) + params + (rows,),
        out_specs=(rows, rows) + params,
        check_vma=False,
    )
```

```python
import math
import types

import jax
import jax.numpy as jnp
from jax import lax
from jax.experimental import pallas as pl
from jax.experimental.pallas import tpu as pltpu
from jax.sharding import PartitionSpec as P

HEADS = 12
HEAD_DIM = 64
AXIS = "fsdp"
MESH = pl.DeviceIdType.MESH
WIDE = jnp.float32
NARROW = jnp.bfloat16

EMBED_BIAS, FIRST_GAIN, FIRST_SHIFT, QUERY_BIAS, VALUE_BIAS, OUT_BIAS = 0, 1, 2, 3, 4, 5
SECOND_GAIN, SECOND_SHIFT, SHRINK_BIAS, EXPAND_BIAS = 6, 7, 8, 9
VECTOR_ROWS = 16

EMBED, JOINT, OUT, EXPAND, SHRINK = 0, 1, 2, 3, 4

GATHER_STEPS = (256, 768, 768, 768, 128)
REDUCE_STEPS = (128, 384, 768, 768, 256)
GATHER_SHARES = (2, 0, 2, 1, 1, 1, 1, 1, 1, 0, 1, 6, 6, 6, 6, 5, 0)
REDUCE_SHARES = (0, 2, 6, 1, 1, 0, 1, 1, 1, 1, 1, 1, 1, 0, 2, 2, 2, 1, 2, 2)
ORDER = (
    32, 33, 34, 35, 36, 37, 64, 65, 66, 67, 68, 69, 0, 544, 545, 96, 128, 0, 97, 129,
    98, 130, 99, 131, 100, 132, 101, 133, 160, 38, 161, 39, 162, 40, 163, 41, 164, 42, 165, 43,
    102, 134, 103, 135, 192, 104, 136, 193, 194, 195, 105, 166, 44, 70, 137, 196, 197, 167, 45, 71,
    106, 138, 224, 168, 46, 72, 107, 225, 139, 226, 169, 47, 73, 227, 256, 0, 170, 48, 74, 257,
    108, 140, 0, 171, 75, 258, 0, 228, 198, 0, 288, 109, 141, 229, 289, 259, 0, 290, 172, 76,
    199, 110, 142, 260, 0, 291, 173, 77, 111, 143, 261, 0, 200, 0, 174, 78, 112, 230, 144, 292,
    0, 293, 0, 201, 175, 79, 0, 231, 202, 0, 262, 176, 80, 0, 203, 0, 232, 233, 0, 204,
    263, 294, 0, 234, 205, 0, 206, 235, 264, 295, 0, 265, 236, 207, 0, 266, 208, 296, 0, 237,
    267, 238, 297, 0, 268, 239, 240, 298, 0, 299, 0, 320, 321, 322, 269, 270, 300, 0, 271, 272,
    0, 0, 301, 302, 0, 352, 303, 304, 0, 353, 354, 0, 0, 385, 0, 323, 0, 324, 416, 0,
    325, 0, 326, 0, 355, 386, 356, 0, 357, 0, 327, 358, 417, 0, 0, 0, 448, 359, 387, 418,
    0, 0, 0, 388, 0, 328, 0, 329, 449, 421, 0, 330, 0, 390, 0, 360, 480, 450, 419, 361,
    362, 0, 391, 420, 0, 0, 481, 453, 512, 0, 331, 0, 332, 392, 422, 0, 333, 482, 0, 451,
    393, 0, 334, 0, 335, 363, 423, 394, 364, 513, 0, 336, 365, 0, 337, 485, 452, 424, 514, 0,
    338, 0, 339, 0, 0, 366, 483, 367, 425, 577, 368, 454, 395, 369, 426, 370, 371, 396, 578, 517,
    484, 455, 429, 579, 515, 398, 456, 399, 580, 427, 400, 457, 516, 486, 581, 428, 401, 430, 458, 402,
    431, 403, 432, 487, 461, 488, 518, 489, 433, 490, 459, 434, 435, 460, 462, 493, 519, 463, 520, 521,
    464, 491, 522, 465, 466, 467, 492, 494, 495, 525, 496, 497, 523, 498, 499, 524, 526, 527, 528, 529,
    530, 531,
)


def nn(left, right):
    return lax.dot_general(left, right, (((1,), (0,)), ((), ())), preferred_element_type=WIDE)


def nt(left, right):
    return lax.dot_general(left, right, (((1,), (1,)), ((), ())), preferred_element_type=WIDE)


def tn(left, right):
    return lax.dot_general(left, right, (((0,), (0,)), ((), ())), preferred_element_type=WIDE)


def aligned(value, step):
    return pl.multiple_of(value, step)


def gelu_pair(upper):
    cdf = 0.5 * (1.0 + lax.erf(upper * (1.0 / math.sqrt(2.0))))
    density = jnp.exp(-0.5 * upper * upper) * (1.0 / math.sqrt(2.0 * math.pi))
    return upper * cdf, cdf + upper * density


def column_chunks(width, step):
    return [(start, step) for start in range(0, width, step)]


def fused_kernel(tokens, width, stem_width, mlp, sizes, gather_plan, reduce_plan, names, *refs):
    vec_in, lengths, stem_hbm, cot_hbm = refs[:4]
    shard, (act_hbm, stem_grad_hbm) = refs[4:9], refs[9:11]
    result, vec_out = refs[11:16], refs[16]
    ref = types.SimpleNamespace(**dict(zip(names, refs[17:])))
    full = ref.full
    local_grad = [ref.core_shrink] + list(full[1:4]) + [ref.shrink_grad]
    resid, work, bias = ref.resid, ref.work, ref.bias
    unit1, unit2, scale1, scale2 = ref.unit1, ref.unit2, ref.scale1, ref.scale2
    normed, normed_mid, proj = ref.normed, ref.normed_mid, ref.proj
    mixed_t, mixed, lse, delta = ref.mixed_t, ref.mixed, ref.lse, ref.delta
    pull, hidden, cot, stem, low = ref.pull, ref.hidden, ref.cot, ref.stem, ref.low
    vecs, vec_all, vec_sum = ref.vecs, ref.vec_all, ref.vec_sum
    fold = ref.fold

    dp, fs = lax.axis_index("dp"), lax.axis_index(AXIS)
    y, c = lax.div(dp, 2), lax.rem(dp, 2)
    z, x = lax.div(fs, 2), lax.rem(fs, 2)
    z_others = (z + 1 - 2 * lax.rem(z, 2), lax.rem(z + 2, 4), 3 - z)
    at_core = (y * 2 + 1 - c, fs)
    at_y = ((1 - y) * 2 + c, fs)
    at_x = (dp, z * 2 + 1 - x)
    at_z = tuple((dp, other * 2 + x) for other in z_others)

    def send(src, dst, send_sem, recv_sem, where):
        return pltpu.make_async_remote_copy(
            src_ref=src,
            dst_ref=dst,
            send_sem=send_sem,
            recv_sem=recv_sem,
            device_id=where,
            device_id_type=MESH,
        )


    up = lax.div(z, 2)
    inner = (z == 1) | (z == 2)
    arrivals = (z_others[0], 2 - up, 3 - 3 * up)
    fill, g_send, g_recv = ref.fill, ref.g_send, ref.g_recv

    def gather_refs(k):
        weight, start, count, share = gather_plan[k]
        half = sizes[weight][0] // 2
        both = half - 2 * share
        mine = pl.ds(aligned(c * half + y * share, 16), share + both)
        passed = pl.ds(aligned(c * half + y * (share + both), 16), share)
        halves = pl.ds(aligned(c * half, 16), half)
        return full[weight], shard[weight], mine, passed, halves, pl.ds(start, count)

    def fill_copy(k):
        whole, own, _, _, halves, cols = gather_refs(k)
        return pltpu.make_async_copy(own.at[halves, cols], whole.at[z, x, halves, cols], fill.at[k])

    def own_copy(k, sent, got, where):
        whole, own, mine, _, _, cols = gather_refs(k)
        return send(own.at[mine, cols], whole.at[z, x, mine, cols], g_send.at[sent, k], g_recv.at[got, k], where)

    def same_copy(part, k, sent, got, where):
        return send(part, part, g_send.at[sent, k], g_recv.at[got, k], where)

    def z_copy(k, order, sent, got, where):
        whole, _, mine, _, _, cols = gather_refs(k)
        return same_copy(whole.at[arrivals[order], x, mine, cols], k, sent, got, where)

    def across(k, step):
        order, got, where = ((0, 2, at_z[2]), (1, 1, at_z[0]), (2, 2, at_z[0]))[step]
        return z_copy(k, order, 1, got, where)

    def x_copy(k, order):
        whole, _, mine, _, _, cols = gather_refs(k)
        return same_copy(whole.at[arrivals[order], x, mine, cols], k, 2, 3, at_x)

    def inner_bytes(k):
        whole, _, mine, _, _, cols = gather_refs(k)
        return same_copy(whole.at[:, x, mine, cols], k, 1, 1, at_z[2])

    def x_bytes(k):
        whole, _, mine, _, _, cols = gather_refs(k)
        return same_copy(whole.at[:, x, mine, cols], k, 2, 3, at_x)

    def y_copy(k, order):
        whole, _, _, passed, _, cols = gather_refs(k)
        return same_copy(whole.at[arrivals[order], x, passed, cols], k, 3, 4, at_y)

    def y_bytes(k):
        whole, _, _, passed, _, cols = gather_refs(k)
        return same_copy(whole.at[pl.ds(0, 3), x, passed, cols], k, 3, 4, at_y)

    def y_copy_late(k):
        whole, _, _, passed, _, cols = gather_refs(k)
        return same_copy(whole.at[:, 1 - x, passed, cols], k, 4, 5, at_y)

    def core_copy(k):
        whole, _, _, _, halves, cols = gather_refs(k)
        return same_copy(whole.at[:, :, halves, cols], k, 5, 6, at_core)

    def start_z(k):
        own_copy(k, 0, 0, at_z[0]).start()

        @pl.when(inner)
        def _():
            own_copy(k, 1, 1, at_z[2]).start()

        fill_copy(k).start()

    def start_x(k):
        own_copy(k, 2, 3, at_x).start()

    def gather_z(order):
        def step(k):
            z_copy(k, order, order, order, at_z[0]).wait_recv()

            @pl.when(inner)
            def _():
                across(k, order).start()

            x_copy(k, order).start()
            if gather_plan[k][3]:
                y_copy(k, order).start()

        return step

    def gather_x(k):
        x_bytes(k).wait_recv()
        if gather_plan[k][3]:
            y_copy_late(k).start()

    def gather_y(k):
        fill_copy(k).wait()
        if gather_plan[k][3]:
            y_bytes(k).wait_recv()
            y_copy_late(k).wait_recv()
        core_copy(k).start()

    def gather_core(k):
        core_copy(k).wait_recv()

    def gather_sent(k):
        own_copy(k, 0, 0, at_z[0]).wait_send()

        @pl.when(inner)
        def _():
            inner_bytes(k).wait_send()

        x_bytes(k).wait_send()
        if gather_plan[k][3]:
            y_bytes(k).wait_send()
            y_copy_late(k).wait_send()
        core_copy(k).wait_send()

    r_send, r_recv, r_done = g_send, ref.r_recv, ref.r_done
    from_y, from_x, from_z = ref.from_y, ref.from_x, ref.from_z
    part_out, part_in, final = ref.part_out, ref.part_in, ref.final
    free = ref.free

    def core_slot(k):
        weight, start, count, _ = reduce_plan[k]
        if weight == SHRINK:
            return ref.core_shrink.at[:, :, :, pl.ds(start, count)]
        if weight == EMBED:
            return ref.core_embed.at[:, :, :, pl.ds(start, count)]
        half = sizes[weight][0] // 2
        before = {EXPAND: 0, OUT: mlp // width, JOINT: mlp // width + 1}[weight]
        return full[SHRINK].at[:, :, pl.ds((before + start // width) * half, half), pl.ds(start % width, count)]

    def reduce_refs(k):
        weight, start, count, share = reduce_plan[k]
        half = sizes[weight][0] // 2
        return weight, half, share, half - 2 * share, pl.ds(start, count)

    def r1_copy(k):
        weight, half, _, _, cols = reduce_refs(k)
        src = local_grad[weight].at[:, :, pl.ds(aligned((1 - c) * half, 16), half), cols]
        return send(src, core_slot(k), r_send.at[0, k], r_recv.at[0, k], at_core)

    def r2_copy(k):
        weight, half, share, both, cols = reduce_refs(k)
        rows = pl.ds(aligned(c * half + (1 - y) * (share + both), 16), share)
        return send(
            local_grad[weight].at[:, :, rows, cols],
            from_y[k],
            r_send.at[1, k],
            r_recv.at[1, k],
            at_y,
        )

    def mine_rows(half, share, both):
        return pl.ds(aligned(c * half + y * share, 16), share + both)

    def r3_copy(k):
        weight, half, share, both, cols = reduce_refs(k)
        return send(
            local_grad[weight].at[:, 1 - x, mine_rows(half, share, both), cols],
            from_x[k],
            r_send.at[2, k],
            r_recv.at[2, k],
            at_x,
        )

    def r4_copy(k, j):
        weight, half, share, both, cols = reduce_refs(k)
        return send(
            local_grad[weight].at[z_others[j], x, mine_rows(half, share, both), cols],
            from_z[k].at[j],
            r_send.at[3, k],
            r_recv.at[3, k],
            at_z[j],
        )

    def r4_bytes(k):
        return send(from_z[k], from_z[k], r_send.at[3, k], r_recv.at[3, k], at_z[0])

    def r5_copy(k):
        return send(part_out[k], part_in[k], r_send.at[4, k], r_recv.at[4, k], at_y)

    def r6_copies(k):
        weight, half, _, _, cols = reduce_refs(k)
        rows = pl.ds(aligned(c * half, 16), half)
        src, dst = final[k], result[weight].at[rows, cols]
        return (
            send(src, dst, r_send.at[5, k], r_recv.at[5, k], at_core),
            pltpu.make_async_copy(src, dst, r_done.at[k]),
        )

    def r6_incoming(k):
        weight, half, _, _, cols = reduce_refs(k)
        rows = pl.ds(aligned((1 - c) * half, 16), half)
        part = result[weight].at[rows, cols]
        return send(part, part, r_send.at[5, k], r_recv.at[5, k], at_core)

    def reduce_1(k):
        if reduce_plan[k][:2] == (EXPAND, 0):
            pl.semaphore_wait(free, 1)
        r1_copy(k).start()

    def reduce_2(k):
        weight, half, share, _, cols = reduce_refs(k)
        r1_copy(k).wait_recv()
        slot, total = core_slot(k), local_grad[weight]
        rows = pl.ds(aligned(c * half, 16), half)
        for i in range(4):
            for j in range(2):
                total[i, j, rows, cols] = total[i, j, rows, cols] + slot[i, j]
        if share:
            r2_copy(k).start()
        else:
            r3_copy(k).start()

    def reduce_3(k):
        weight, half, share, both, cols = reduce_refs(k)
        r2_copy(k).wait_recv()
        total = local_grad[weight]
        rows = pl.ds(aligned(c * half + y * (share + both), 16), share)
        for i in range(4):
            for j in range(2):
                total[i, j, rows, cols] = total[i, j, rows, cols] + from_y[k][i, j]
        r3_copy(k).start()

    def reduce_4(k):
        weight, half, share, both, cols = reduce_refs(k)
        r3_copy(k).wait_recv()
        total = local_grad[weight]
        rows = mine_rows(half, share, both)
        for i in range(4):
            total[i, x, rows, cols] = total[i, x, rows, cols] + from_x[k][i]
        for j in range(3):
            r4_copy(k, j).start()

    def reduce_5(k):
        weight, half, share, both, cols = reduce_refs(k)
        r4_bytes(k).wait_recv()
        value = local_grad[weight][z, x, mine_rows(half, share, both), cols].astype(WIDE)
        for j in range(3):
            value = value + from_z[k][j].astype(WIDE)
        part_out[k][...] = value.astype(NARROW)
        r5_copy(k).start()

    def reduce_6(k):
        _, half, share, both, _ = reduce_refs(k)
        r5_copy(k).wait_recv()
        own, came, whole = part_out[k], part_in[k], final[k]

        def rows(start, count):
            return pl.ds(aligned(start, 16), count)

        if share:
            whole[rows(y * (share + both), share), :] = own[rows(y * both, share), :].astype(WIDE)
            whole[rows((1 - y) * (share + both), share), :] = came[rows((1 - y) * both, share), :].astype(WIDE)
        if both:
            whole[share : share + both, :] = own[rows((1 - y) * share, both), :].astype(WIDE) + came[
                rows(y * share, both), :
            ].astype(WIDE)
        for copy in r6_copies(k):
            copy.start()

    def reduce_7(k):
        r6_incoming(k).wait_recv()
        r1_copy(k).wait_send()
        if reduce_refs(k)[2]:
            r2_copy(k).wait_send()
        r3_copy(k).wait_send()
        r4_bytes(k).wait_send()
        r5_copy(k).wait_send()
        remote, local = r6_copies(k)
        remote.wait_send()
        local.wait()

    def row(place):
        return vecs[place : place + 1, :]

    def layer_norm(unit, scale, out, gain, shift):
        def step(n, carry):
            rows = pl.ds(aligned(n * 96, 96), 96)
            values = resid[rows, :]
            center = values - jnp.mean(values, axis=1, keepdims=True)
            factor = lax.rsqrt(jnp.mean(center * center, axis=1, keepdims=True) + 1e-6)
            units = center * factor
            scale[rows, :] = factor
            unit[rows, :] = units.astype(NARROW)
            out[rows, :] = (units * row(gain) + row(shift)).astype(NARROW)
            return carry

        lax.fori_loop(0, tokens // 96, step, 0)

    def eight(values):
        return jnp.sum(values.reshape(values.shape[0] // 8, 8, values.shape[1]), axis=0)

    def norm_backward(unit, scale, gain, upstream, keep_wide, places):
        fold[...] = jnp.zeros_like(fold)

        def step(n, carry):
            rows = pl.ds(aligned(n * 96, 96), 96)
            grads = work[rows, :]
            units = unit[rows, :].astype(WIDE)
            inner = grads * row(gain)
            fold[0:8, :] += eight(grads * units)
            fold[8:16, :] += eight(grads)
            value = upstream[rows, :].astype(WIDE) + scale[rows, :] * (
                inner
                - jnp.mean(inner, axis=1, keepdims=True)
                - units * jnp.mean(inner * units, axis=1, keepdims=True)
            )
            if keep_wide:
                resid[rows, :] = value
            narrow = value.astype(NARROW)
            low[rows, :] = narrow
            fold[16:24, :] += eight(narrow.astype(WIDE))
            return carry

        lax.fori_loop(0, tokens // 96, step, 0)
        for n, place in enumerate(places):
            vec_sum[0, place : place + 1, :] = jnp.sum(fold[8 * n : 8 * n + 8, :], axis=0, keepdims=True)

    def column_sum(source, start, place, at=0, count=width):
        def step(n, total):
            return total + eight(source[pl.ds(aligned(n * 96, 96), 96), start : start + count].astype(WIDE))

        total = lax.fori_loop(0, tokens // 96, step, jnp.zeros((8, count), WIDE))
        vec_sum[0, place : place + 1, at : at + count] = jnp.sum(total, axis=0, keepdims=True)

    lane = lax.broadcasted_iota(jnp.int32, (1, 2 * HEAD_DIM), 1)

    def head_lanes(head, value):
        return jnp.where((lane < HEAD_DIM) == (head == 0), value, 0.0).astype(NARROW)

    factor = 1.0 / math.sqrt(HEAD_DIM)

    def attend_forward(p):
        def run():
            at = p * 128
            query = proj[:, pl.ds(at, 128)]
            keys = proj[:, pl.ds(width + at, 128)]
            values_t = proj[:, pl.ds(2 * width + at, 128)].T
            for head in range(2):
                scores = nt(keys * head_lanes(head, factor), query) + bias[...].astype(WIDE)
                largest = jnp.max(scores, axis=0, keepdims=True)
                expos = jnp.exp(scores - largest)
                total = jnp.sum(expos, axis=0, keepdims=True)
                mix = nn(values_t[64 * head : 64 * head + 64], expos.astype(NARROW)) * (1.0 / total)
                mixed_t[pl.ds(aligned(at + 64 * head, 64), 64), :] = mix.astype(NARROW)
                lse[pl.ds(2 * p + head, 1), :] = largest + jnp.log(total)

        return run

    def attend_backward(p):
        def run():
            at = p * 128
            query = proj[:, pl.ds(at, 128)]
            keys = proj[:, pl.ds(width + at, 128)]
            values = proj[:, pl.ds(2 * width + at, 128)]
            grads = mixed[:, pl.ds(at, 128)]
            keys_t = keys.T
            value_grads, key_grads = [], []
            for head in range(2):
                scores = nt(keys * head_lanes(head, factor), query) + bias[...].astype(WIDE)
                attend = jnp.exp(scores - lse[pl.ds(2 * p + head, 1), :])
                attend_grad = nt(values * head_lanes(head, 1.0), grads)
                scores_grad = (attend * (attend_grad - delta[pl.ds(2 * p + head, 1), :])).astype(NARROW)
                value_grads.append(nn(attend.astype(NARROW), grads))
                key_grads.append(nn(scores_grad, query))
                query_grad = nn(keys_t[64 * head : 64 * head + 64], scores_grad) * factor
                mixed_t[pl.ds(aligned(at + 64 * head, 64), 64), :] = query_grad.astype(NARROW)
            first_head = lane < HEAD_DIM
            pull[:, pl.ds(2 * width + at, 128)] = jnp.where(first_head, *value_grads).astype(NARROW)
            pull[:, pl.ds(width + at, 128)] = (jnp.where(first_head, *key_grads) * factor).astype(NARROW)

        return run

    barrier = pltpu.get_barrier_semaphore()
    partners = (at_core, at_y, at_x) + at_z
    for partner in partners:
        pl.semaphore_signal(barrier, inc=1, device_id=partner, device_id_type=MESH)
    load_stem = pltpu.make_async_copy(stem_hbm, stem, ref.load.at[0])
    load_cot = pltpu.make_async_copy(cot_hbm, cot, ref.load.at[1])
    load_stem.start()
    load_cot.start()
    pl.semaphore_wait(barrier, len(partners))

    v_send, v_recv = ref.v_send, ref.v_recv
    vec_z = [send(vec_in, vec_all.at[z, x], v_send.at[0], v_recv.at[0], at_z[j]) for j in range(3)]
    vec_z_part = vec_all.at[pl.ds(0, 3), x]
    vec_z_bytes = send(vec_z_part, vec_z_part, v_send.at[0], v_recv.at[0], at_z[0])
    vec_x_part = vec_all.at[:, x]
    vec_x = send(vec_x_part, vec_x_part, v_send.at[1], v_recv.at[1], at_x)
    vec_all[z, x] = vec_in[...]
    for copy in vec_z:
        copy.start()

    def vec_gather(n):
        if n == 0:
            vec_z_bytes.wait_recv()
            vec_x.start()
        else:
            vec_x.wait_recv()

    vec_from = ref.vec_from
    vec_partners = (at_core, at_y, at_x, at_z[0], at_z[1])

    def vec_copy(n):
        return send(vec_sum.at[n], vec_from.at[n], v_send.at[2 + n], v_recv.at[2 + n], vec_partners[n])

    def vec_step(n):
        vec_copy(n - 1).wait_recv()
        vec_sum[n] = vec_sum[n - 1] + vec_from[n - 1]
        if n < len(vec_partners):
            vec_copy(n).start()

    blocks = []
    block = blocks.append

    @block
    def make_bias():
        places = lax.broadcasted_iota(jnp.int32, (1, tokens), 1)
        places_down = lax.broadcasted_iota(jnp.int32, (tokens, 1), 0)
        labels = jnp.zeros((1, tokens), jnp.int32)
        labels_down = jnp.zeros((tokens, 1), jnp.int32)
        bound = 0
        for n in range(lengths.shape[1]):
            bound = bound + lengths[0, n]
            labels = labels + (places >= bound).astype(jnp.int32)
            labels_down = labels_down + (places_down >= bound).astype(jnp.int32)
        bias[...] = jnp.where(labels_down == labels, 0.0, -1e30).astype(NARROW)
        vec_sum[0] = jnp.zeros((VECTOR_ROWS, width), WIDE)

    @block
    def add_vectors():
        totals = vec_all[0, 0].astype(WIDE)
        for i in range(4):
            for j in range(2):
                if i + j > 0:
                    totals = totals + vec_all[i, j].astype(WIDE)
        vecs[...] = totals
        vec_z_bytes.wait_send()
        vec_x.wait_send()
        load_stem.wait()
        load_cot.wait()

    def chunks(plan, weight):
        return [item[1:3] for item in plan if item[0] == weight]

    def embed(start, count):
        def run():
            piece = full[EMBED][:, :, :, start : start + count].reshape(stem_width, count)
            offset = vecs[EMBED_BIAS : EMBED_BIAS + 1, start : start + count]
            resid[:, start : start + count] = nn(stem[...], piece) + offset

        return run

    def project(start, count):
        def run():
            value = nn(normed[...], full[JOINT][:, :, :, start : start + count].reshape(width, count))
            at = start % width
            if start // width == 0:
                value = value + vecs[QUERY_BIAS : QUERY_BIAS + 1, at : at + count]
            if start // width == 2:
                value = value + vecs[VALUE_BIAS : VALUE_BIAS + 1, at : at + count]
            proj[:, start : start + count] = value.astype(NARROW)

        return run

    for item in chunks(gather_plan, EMBED):
        block(embed(*item))

    @block
    def first_norm():
        layer_norm(unit1, scale1, normed, FIRST_GAIN, FIRST_SHIFT)

    for item in chunks(gather_plan, JOINT):
        block(project(*item))
    for p in range(HEADS // 2):
        block(attend_forward(p))

    @block
    def join_heads():
        mixed[...] = mixed_t[...].T
        resid[...] = resid[...] + nn(mixed[...], full[OUT][...].reshape(width, width)) + row(OUT_BIAS)

    @block
    def second_norm():
        layer_norm(unit2, scale2, normed_mid, SECOND_GAIN, SECOND_SHIFT)

    def expand_forward(i):
        def run():
            start = i * width
            work[...] = nn(normed_mid[...], full[EXPAND][:, :, :, start : start + width].reshape(width, width))

            def gelu_step(n, carry):
                rows = pl.ds(aligned(n * 64, 64), 64)
                for at in range(0, width, 128):
                    offset = vecs[EXPAND_BIAS + i : EXPAND_BIAS + i + 1, at : at + 128]
                    value, slope = gelu_pair(work[rows, at : at + 128] + offset)
                    hidden[rows, start + at : start + at + 128] = value.astype(NARROW)
                    pull[rows, start + at : start + at + 128] = slope.astype(NARROW)
                return carry

            lax.fori_loop(0, tokens // 64, gelu_step, 0)

        return run

    rows_shrink = sizes[SHRINK][0]

    def shrink_gradient(i):
        def run():
            for j in range(2):
                at = rows_shrink * (2 * i + j)
                local_grad[SHRINK][i, j] = tn(hidden[:, at : at + rows_shrink], cot[...]).astype(NARROW)

        return run

    for i in range(4):
        block(expand_forward(i))
        block(shrink_gradient(i))

    @block
    def cotangent_sum():
        column_sum(cot, 0, SHRINK_BIAS)

    def hidden_backward(i):
        def run():
            at = i * width
            grads = nt(cot[...], full[SHRINK][i].reshape(width, width))
            pull[:, at : at + width] = (grads * pull[:, at : at + width].astype(WIDE)).astype(NARROW)
            column_sum(pull, at, EXPAND_BIAS + i)

        return run

    for i in range(4):
        block(hidden_backward(i))
    store_act = pltpu.make_async_copy(low, act_hbm, ref.load.at[0])
    store_stem = pltpu.make_async_copy(hidden.at[:, pl.ds(0, stem_width)], stem_grad_hbm, ref.load.at[1])

    @block
    def activations():
        value = nn(hidden[...], full[SHRINK][...].reshape(mlp, width))
        low[...] = (resid[...] + value + row(SHRINK_BIAS)).astype(NARROW)
        store_act.start()
        pl.semaphore_signal(free, inc=1, device_id=at_core, device_id_type=MESH)

    @block
    def expand_backward():
        work[...] = nt(pull[...], full[EXPAND][...].reshape(width, mlp))

    def expand_gradient(i):
        def run():
            at = i * width
            value = tn(normed_mid[...], pull[:, at : at + width]).astype(NARROW)
            full[EXPAND][:, :, :, at : at + width] = value.reshape(4, 2, width // 8, width)

        return run

    for i in range(4):
        block(expand_gradient(i))

    @block
    def second_norm_backward():
        store_act.wait()
        norm_backward(unit2, scale2, SECOND_GAIN, cot, True, (SECOND_GAIN, SECOND_SHIFT, OUT_BIAS))

    @block
    def out_backward():
        mixed[...] = nt(low[...], full[OUT][...].reshape(width, width)).astype(NARROW)

    @block
    def out_gradient():
        full[OUT][...] = nn(mixed_t[...], low[...]).astype(NARROW).reshape(4, 2, width // 8, width)

    @block
    def row_sums():
        grads_t = mixed[...].T
        for head in range(HEADS):
            span = slice(64 * head, 64 * head + 64)
            product = grads_t[span].astype(WIDE) * mixed_t[span, :].astype(WIDE)
            delta[head : head + 1, :] = jnp.sum(product, axis=0, keepdims=True)

    def gather_query(half):
        def run():
            at = half * width // 2
            pull[:, at : at + width // 2] = mixed_t[at : at + width // 2, :].T
            column_sum(pull, at, QUERY_BIAS, at, width // 2)
            column_sum(pull, 2 * width + at, VALUE_BIAS, at, width // 2)

        return run

    def joint_backward(half):
        def run():
            total = 0.0 if half == 0 else work[...]
            for part in range(3):
                at = part * width + half * width // 2
                weight = full[JOINT][:, :, :, at : at + width // 2].reshape(width, width // 2)
                total = total + nt(pull[:, at : at + width // 2], weight)
            work[...] = total

        return run

    def joint_gradient(start, count):
        def run():
            value = tn(normed[...], pull[:, start : start + count]).astype(NARROW)
            full[JOINT][:, :, :, start : start + count] = value.reshape(4, 2, width // 8, count)

        return run

    for half in range(2):
        for p in range(HEADS // 4):
            block(attend_backward(half * HEADS // 4 + p))
        block(gather_query(half))
        block(joint_backward(half))
        for item in chunks(reduce_plan, JOINT)[3 * half : 3 * half + 3]:
            block(joint_gradient(*item))

    @block
    def first_norm_backward():
        norm_backward(unit1, scale1, FIRST_GAIN, resid, False, (FIRST_GAIN, FIRST_SHIFT, EMBED_BIAS))

    rows_embed = sizes[EMBED][0]

    def embed_gradient(start, count):
        def run():
            value = tn(stem[...], low[:, start : start + count]).astype(NARROW)
            local_grad[EMBED][:, :, 0:rows_embed, start : start + count] = value.reshape(4, 2, rows_embed, count)

        return run

    for item in chunks(reduce_plan, EMBED):
        block(embed_gradient(*item))

    @block
    def start_vectors():
        vec_copy(0).start()

    @block
    def stem_backward():
        value = nt(low[...], full[EMBED][...].reshape(stem_width, width))
        hidden[:, 0:stem_width] = value.astype(NARROW)
        store_stem.start()

    work_left = iter(blocks)
    steps = (
        lambda k: pl.when(dp >= 0)(next(work_left)),
        start_z,
        start_x,
        gather_z(0),
        gather_z(1),
        gather_z(2),
        gather_x,
        gather_y,
        gather_core,
        gather_sent,
        reduce_1,
        reduce_2,
        reduce_3,
        reduce_4,
        reduce_5,
        reduce_6,
        reduce_7,
        vec_gather,
        vec_step,
    )
    for code in ORDER:
        steps[code // 32](code % 32)
    vec_out[...] = vec_sum[len(vec_partners)]
    for n in range(len(vec_partners)):
        vec_copy(n).wait_send()
    store_stem.wait()


def plans(width, mlp):
    gather_plan = (
        [(EMBED,) + item for item in column_chunks(width, GATHER_STEPS[EMBED])]
        + [(JOINT,) + item for item in column_chunks(3 * width, GATHER_STEPS[JOINT])]
        + [(OUT,) + item for item in column_chunks(width, GATHER_STEPS[OUT])]
        + [(EXPAND,) + item for item in column_chunks(mlp, GATHER_STEPS[EXPAND])]
        + [(SHRINK,) + item for item in column_chunks(width, GATHER_STEPS[SHRINK])]
    )
    halves = (0, width // 2)
    reduce_plan = (
        [(SHRINK,) + item for item in column_chunks(width, REDUCE_STEPS[SHRINK])]
        + [(EXPAND,) + item for item in column_chunks(mlp, REDUCE_STEPS[EXPAND])]
        + [(OUT,) + item for item in column_chunks(width, REDUCE_STEPS[OUT])]
        + [(JOINT, part * width + at, width // 2) for at in halves for part in range(3)]
        + [(EMBED,) + item for item in column_chunks(width, REDUCE_STEPS[EMBED])]
    )
    return (
        [item + (16 * n,) for item, n in zip(gather_plan, GATHER_SHARES)],
        [item + (16 * n,) for item, n in zip(reduce_plan, REDUCE_SHARES)],
    )


def fused(mesh):
    def local(
        stem_features,
        lengths,
        embed_weight,
        embed_bias,
        before_gain,
        before_shift,
        joint_weight,
        query_bias,
        value_bias,
        output_weight,
        output_bias,
        middle_gain,
        middle_shift,
        expand_weight,
        expand_bias,
        shrink_weight,
        shrink_bias,
        cotangent,
    ):
        _, tokens, stem_width = stem_features.shape
        width = embed_weight.shape[1]
        mlp = expand_weight.shape[1]
        shards = (embed_weight, joint_weight, output_weight, expand_weight, shrink_weight)
        sizes = [item.shape for item in shards]
        fsdp = lax.axis_index(AXIS)

        nine = jnp.stack(
            [
                embed_bias,
                before_gain,
                before_shift,
                query_bias,
                value_bias,
                output_bias,
                middle_gain,
                middle_shift,
                shrink_bias,
            ]
        )
        piece = nine.shape[1]
        owner = jnp.arange(width) // piece
        rows_nine = jnp.where(owner[None] == fsdp, jnp.tile(nine, (1, width // piece)), 0)
        piece_expand = expand_bias.shape[0]
        owner = (jnp.arange(mlp // width)[:, None] * width + jnp.arange(width)[None]) // piece_expand
        rows_expand = jnp.tile(expand_bias[None], (mlp // width, width // piece_expand))
        rows_expand = jnp.where(owner == fsdp, rows_expand, 0)
        used = 9 + mlp // width
        vec_in = jnp.concatenate([rows_nine, rows_expand, jnp.zeros((VECTOR_ROWS - used, width), NARROW)])
        vec_in = vec_in.astype(NARROW)

        gather_plan, reduce_plan = plans(width, mlp)
        steps, folds = len(gather_plan), len(reduce_plan)
        vmem, dma = pltpu.VMEM, pltpu.SemaphoreType.DMA

        def each(make):
            return [make(sizes[n][0] // 2, share, cols) for n, _, cols, share in reduce_plan]

        def square(cols):
            return vmem((tokens, cols), NARROW)

        scratch = dict(
            full=[vmem((4, 2) + item, NARROW) for item in sizes],
            shrink_grad=vmem((4, 2) + sizes[SHRINK], NARROW),
            core_shrink=vmem((4, 2, sizes[SHRINK][0] // 2, width), NARROW),
            core_embed=vmem((4, 2, sizes[EMBED][0] // 2, width), NARROW),
            from_y=each(lambda half, share, cols: vmem((4, 2, max(share, 16), cols if share else 128), NARROW)),
            from_x=each(lambda half, share, cols: vmem((4, half - share, cols), NARROW)),
            from_z=each(lambda half, share, cols: vmem((3, half - share, cols), NARROW)),
            part_out=each(lambda half, share, cols: vmem((half - share, cols), NARROW)),
            part_in=each(lambda half, share, cols: vmem((half - share, cols), NARROW)),
            final=each(lambda half, share, cols: vmem((half, cols), WIDE)),
            resid=vmem((tokens, width), WIDE),
            work=vmem((tokens, width), WIDE),
            bias=square(tokens),
            unit1=square(width),
            unit2=square(width),
            normed=square(width),
            normed_mid=square(width),
            mixed=square(width),
            cot=square(width),
            low=square(width),
            scale1=vmem((tokens, 1), WIDE),
            scale2=vmem((tokens, 1), WIDE),
            proj=square(3 * width),
            mixed_t=vmem((width, tokens), NARROW),
            lse=vmem((16, tokens), WIDE),
            delta=vmem((16, tokens), WIDE),
            pull=square(mlp),
            hidden=square(mlp),
            stem=square(stem_width),
            vecs=vmem((VECTOR_ROWS, width), WIDE),
            vec_all=vmem((4, 2, VECTOR_ROWS, width), NARROW),
            vec_sum=vmem((6, VECTOR_ROWS, width), WIDE),
            vec_from=vmem((5, VECTOR_ROWS, width), WIDE),
            fold=vmem((24, width), WIDE),
            fill=dma((steps,)),
            g_send=dma((6, max(steps, folds))),
            g_recv=dma((7, steps)),
            r_recv=dma((6, folds)),
            r_done=dma((folds,)),
            load=dma((2,)),
            v_send=dma((7,)),
            v_recv=dma((7,)),
            free=pltpu.SemaphoreType.REGULAR,
        )
        names = list(scratch)

        def body(*refs):
            fused_kernel(tokens, width, stem_width, mlp, sizes, gather_plan, reduce_plan, names, *refs)

        far = pl.BlockSpec(memory_space=pl.ANY)
        near = pl.BlockSpec(memory_space=pltpu.VMEM)
        outs = pl.pallas_call(
            body,
            out_shape=(
                jax.ShapeDtypeStruct((tokens, width), NARROW),
                jax.ShapeDtypeStruct((tokens, stem_width), NARROW),
            )
            + tuple(jax.ShapeDtypeStruct(item, WIDE) for item in sizes)
            + (jax.ShapeDtypeStruct((VECTOR_ROWS, width), WIDE),),
            in_specs=[near, pl.BlockSpec(memory_space=pltpu.SMEM)] + [far] * 7,
            out_specs=(far,) * 7 + (near,),
            scratch_shapes=list(scratch.values()),
            compiler_params=pltpu.CompilerParams(
                collective_id=0, has_side_effects=True, vmem_limit_bytes=64 * 2**20
            ),
        )(vec_in, lengths, stem_features[0], cotangent[0], *shards)
        act, stem_grad, grads, vec_out = outs[0], outs[1], outs[2:7], outs[7]
        mine = lax.dynamic_slice(vec_out, (0, fsdp * piece), (9, piece))
        start = fsdp * piece_expand
        mine_expand = lax.dynamic_slice(vec_out, (9 + start // width, start % width), (1, piece_expand))[0]
        return (
            act[None],
            stem_grad[None],
            grads[EMBED],
            mine[EMBED_BIAS],
            mine[FIRST_GAIN],
            mine[FIRST_SHIFT],
            grads[JOINT],
            mine[QUERY_BIAS],
            mine[VALUE_BIAS],
            grads[OUT],
            mine[OUT_BIAS],
            mine[SECOND_GAIN],
            mine[SECOND_SHIFT],
            grads[EXPAND],
            mine_expand,
            grads[SHRINK],
            mine[SHRINK_BIAS],
        )

    return local


def normalize(values):
    center = values - jnp.mean(values, axis=-1, keepdims=True)
    scaled = lax.rsqrt(jnp.mean(center * center, axis=-1, keepdims=True) + 1e-06)
    return (center * scaled, scaled)


def norm_backward(upstream, unit, scaled, gain):
    gain_part = jnp.sum(upstream * unit, axis=0)
    shift_part = jnp.sum(upstream, axis=0)
    inner = upstream * gain
    result = scaled * (
        inner
        - jnp.mean(inner, axis=-1, keepdims=True)
        - unit * jnp.mean(inner * unit, axis=-1, keepdims=True)
    )
    return (result, gain_part, shift_part)


def region_mask(lengths, row_len):
    bounds = jnp.cumsum(lengths, axis=1)
    places = jnp.arange(row_len, dtype=jnp.int32)
    labels = jnp.sum((places[None, :, None] >= bounds[:, None, :]).astype(jnp.int32), axis=2)
    return labels[:, :, None] == labels[:, None, :]


def column_sum(matrix):
    return jnp.sum(matrix.astype(jnp.float32), axis=0)


def general(
    stem_features,
    lengths,
    embed_weight,
    embed_bias,
    before_gain,
    before_shift,
    joint_weight,
    query_bias,
    value_bias,
    output_weight,
    output_bias,
    middle_gain,
    middle_shift,
    expand_weight,
    expand_bias,
    shrink_weight,
    shrink_bias,
    cotangent,
):
    wide = jnp.float32
    narrow = jnp.bfloat16
    shards = (
        embed_weight,
        embed_bias,
        before_gain,
        before_shift,
        joint_weight,
        query_bias,
        value_bias,
        output_weight,
        output_bias,
        middle_gain,
        middle_shift,
        expand_weight,
        expand_bias,
        shrink_weight,
        shrink_bias,
    )
    gathered = tuple(lax.all_gather(item, AXIS, axis=0, tiled=True) for item in shards)
    (
        embedding,
        embed_offset,
        first_gain,
        first_shift,
        joint,
        query_offset,
        value_offset,
        outward,
        out_offset,
        second_gain,
        second_shift,
        expand,
        expand_offset,
        shrink,
        shrink_offset,
    ) = gathered
    rows, row_len, stem_width = stem_features.shape
    width = embed_weight.shape[1]
    tokens = rows * row_len
    factor = 1.0 / math.sqrt(HEAD_DIM)
    heads_shape = (rows, row_len, HEADS, HEAD_DIM)
    same_region = region_mask(lengths, row_len)[:, None]
    inputs = stem_features.reshape(tokens, stem_width)
    embedded = jnp.dot(inputs, embedding, preferred_element_type=wide) + embed_offset.astype(wide)
    unit_first, scale_first = normalize(embedded)
    normed = (unit_first * first_gain.astype(wide) + first_shift.astype(wide)).astype(narrow)
    joint_offset = jnp.concatenate(
        [query_offset, jnp.zeros_like(query_offset), value_offset]
    ).astype(wide)
    projected = (jnp.dot(normed, joint, preferred_element_type=wide) + joint_offset).astype(narrow)
    query = projected[:, :width].reshape(heads_shape)
    keys = projected[:, width : 2 * width].reshape(heads_shape)
    values = projected[:, 2 * width :].reshape(heads_shape)

    def masked_scores():
        products = jnp.einsum("rqhe,rkhe->rhqk", query, keys, preferred_element_type=wide) * factor
        return jnp.where(same_region, products, -1e30)

    scores = masked_scores()
    largest = jnp.max(scores, axis=-1, keepdims=True)
    expos = jnp.exp(scores - largest)
    totals = jnp.sum(expos, axis=-1, keepdims=True)
    log_total = largest + jnp.log(totals)
    attend = (expos / totals).astype(narrow)
    mixed = jnp.einsum("rhqk,rkhe->rqhe", attend, values, preferred_element_type=wide)
    mixed = mixed.reshape(tokens, width).astype(narrow)
    residual = (
        embedded + jnp.dot(mixed, outward, preferred_element_type=wide) + out_offset.astype(wide)
    )
    unit_second, scale_second = normalize(residual)
    normed_mid = (unit_second * second_gain.astype(wide) + second_shift.astype(wide)).astype(narrow)
    upper = jnp.dot(normed_mid, expand, preferred_element_type=wide) + expand_offset.astype(wide)
    hidden_wide, gelu_pull = jax.vjp(lambda inner: jax.nn.gelu(inner, approximate=False), upper)
    hidden = hidden_wide.astype(narrow)
    output = (
        residual + jnp.dot(hidden, shrink, preferred_element_type=wide) + shrink_offset.astype(wide)
    )
    activations = output.astype(narrow).reshape(rows, row_len, width)
    backward_set = gathered
    embedding = backward_set[0]
    first_gain = backward_set[2]
    joint = backward_set[4]
    outward = backward_set[7]
    second_gain = backward_set[9]
    expand = backward_set[11]
    shrink = backward_set[13]
    upstream = cotangent.reshape(tokens, width).astype(wide)
    upstream_low = upstream.astype(narrow)
    shrink_grad = jnp.einsum("tm,td->md", hidden, upstream_low, preferred_element_type=wide)
    shrink_offset_grad = column_sum(upstream_low)
    hidden_grad = jnp.einsum("td,md->tm", upstream_low, shrink, preferred_element_type=wide)
    upper_grad = gelu_pull(hidden_grad)[0].astype(narrow)
    expand_grad = jnp.einsum("td,tm->dm", normed_mid, upper_grad, preferred_element_type=wide)
    expand_offset_grad = column_sum(upper_grad)
    normed_mid_grad = jnp.einsum("tm,dm->td", upper_grad, expand, preferred_element_type=wide)
    second_part, second_gain_grad, second_shift_grad = norm_backward(
        normed_mid_grad, unit_second, scale_second, second_gain.astype(wide)
    )
    residual_grad = upstream + second_part
    residual_low = residual_grad.astype(narrow)
    outward_grad = jnp.einsum("te,td->ed", mixed, residual_low, preferred_element_type=wide)
    out_offset_grad = column_sum(residual_low)
    mixed_grad = jnp.einsum("td,ed->te", residual_low, outward, preferred_element_type=wide)
    mixed_grad = mixed_grad.astype(narrow).reshape(heads_shape)
    attend_wide = jnp.exp(masked_scores() - log_total)
    attend = attend_wide.astype(narrow)
    values_grad = jnp.einsum("rhqk,rqhe->rkhe", attend, mixed_grad, preferred_element_type=wide)
    attend_grad = jnp.einsum("rqhe,rkhe->rhqk", mixed_grad, values, preferred_element_type=wide)
    centered = jnp.sum(attend_grad * attend_wide, axis=-1, keepdims=True)
    scores_grad = (attend_wide * (attend_grad - centered)).astype(narrow)
    query_grad = (
        jnp.einsum("rhqk,rkhe->rqhe", scores_grad, keys, preferred_element_type=wide) * factor
    )
    keys_grad = (
        jnp.einsum("rhqk,rqhe->rkhe", scores_grad, query, preferred_element_type=wide) * factor
    )
    projected_grad = jnp.concatenate(
        [
            query_grad.reshape(tokens, width),
            keys_grad.reshape(tokens, width),
            values_grad.reshape(tokens, width),
        ],
        axis=1,
    ).astype(narrow)
    joint_grad = jnp.einsum("td,tj->dj", normed, projected_grad, preferred_element_type=wide)
    query_offset_grad = column_sum(projected_grad[:, :width])
    value_offset_grad = column_sum(projected_grad[:, 2 * width :])
    normed_grad = jnp.einsum("tj,dj->td", projected_grad, joint, preferred_element_type=wide)
    first_part, first_gain_grad, first_shift_grad = norm_backward(
        normed_grad, unit_first, scale_first, first_gain.astype(wide)
    )
    embedded_low = (residual_grad + first_part).astype(narrow)
    embedding_grad = jnp.einsum("ts,td->sd", inputs, embedded_low, preferred_element_type=wide)
    embed_offset_grad = column_sum(embedded_low)
    stem_gradient = jnp.einsum("td,sd->ts", embedded_low, embedding, preferred_element_type=wide)
    stem_gradient = stem_gradient.astype(narrow).reshape(rows, row_len, stem_width)
    terms = (
        embedding_grad,
        embed_offset_grad,
        first_gain_grad,
        first_shift_grad,
        joint_grad,
        query_offset_grad,
        value_offset_grad,
        outward_grad,
        out_offset_grad,
        second_gain_grad,
        second_shift_grad,
        expand_grad,
        expand_offset_grad,
        shrink_grad,
        shrink_offset_grad,
    )
    owned = tuple(lax.psum_scatter(item, AXIS, scatter_dimension=0, tiled=True) for item in terms)
    summed = lax.psum(owned, "dp")
    return (activations, stem_gradient) + tuple(summed)


def solution(mesh):
    rows, whole, vector = P(("dp", AXIS), None, None), P(AXIS, None), P(AXIS)
    params = (whole, vector, vector, vector, whole, vector, vector, whole, vector)
    params = params + (vector, vector, whole, vector, whole, vector)
    plain = mesh.shape["dp"] != 4 or mesh.shape[AXIS] != 8
    return jax.shard_map(
        general if plain else fused(mesh),
        mesh=mesh,
        in_specs=(rows, P(("dp", AXIS), None)) + params + (rows,),
        out_specs=(rows, rows) + params,
        check_vma=False,
    )
```

```python
import math
import types

import jax
import jax.numpy as jnp
from jax import lax
from jax.experimental import pallas as pl
from jax.experimental.pallas import tpu as pltpu
from jax.sharding import PartitionSpec as P

HEADS = 12
HEAD_DIM = 64
AXIS = "fsdp"
MESH = pl.DeviceIdType.MESH
WIDE = jnp.float32
NARROW = jnp.bfloat16

EMBED_BIAS, FIRST_GAIN, FIRST_SHIFT, QUERY_BIAS, VALUE_BIAS, OUT_BIAS = 0, 1, 2, 3, 4, 5
SECOND_GAIN, SECOND_SHIFT, SHRINK_BIAS, EXPAND_BIAS = 6, 7, 8, 9
VECTOR_ROWS = 16

EMBED, JOINT, OUT, EXPAND, SHRINK = 0, 1, 2, 3, 4

GATHER_STEPS = (256, 768, 768, 768, 128)
REDUCE_STEPS = (128, 384, 768, 768, 256)
GATHER_SHARES = (2, 0, 2, 1, 1, 1, 1, 1, 1, 0, 1, 6, 6, 6, 6, 5, 0)
REDUCE_SHARES = (0, 2, 6, 1, 1, 0, 1, 1, 1, 1, 1, 1, 1, 0, 2, 2, 2, 1, 2, 2)
ORDER = (
    32, 33, 34, 35, 36, 37, 64, 65, 66, 67, 68, 69, 0, 544, 545, 96, 128, 0, 97, 129,
    98, 130, 99, 131, 100, 132, 101, 133, 160, 38, 161, 39, 162, 40, 163, 41, 164, 42, 165, 43,
    102, 134, 103, 135, 192, 104, 136, 193, 194, 195, 105, 166, 44, 70, 137, 196, 197, 167, 45, 71,
    106, 138, 224, 168, 46, 72, 107, 225, 139, 226, 169, 47, 73, 227, 256, 0, 170, 48, 74, 257,
    108, 140, 0, 171, 75, 258, 0, 228, 198, 0, 288, 109, 141, 229, 289, 259, 0, 290, 172, 76,
    199, 110, 142, 260, 0, 291, 173, 77, 111, 143, 261, 0, 200, 0, 174, 78, 112, 230, 144, 292,
    0, 293, 0, 201, 175, 79, 0, 231, 202, 0, 262, 176, 80, 0, 203, 0, 232, 233, 0, 204,
    263, 294, 0, 234, 205, 0, 206, 235, 264, 295, 0, 265, 236, 207, 0, 266, 208, 296, 0, 237,
    267, 238, 297, 0, 268, 239, 240, 298, 0, 299, 0, 320, 321, 322, 269, 270, 300, 0, 271, 272,
    0, 0, 301, 302, 0, 352, 303, 304, 0, 353, 354, 0, 0, 385, 0, 323, 0, 324, 416, 0,
    325, 0, 326, 0, 355, 386, 356, 0, 357, 0, 327, 358, 417, 0, 0, 0, 448, 359, 387, 418,
    0, 0, 0, 388, 0, 328, 0, 329, 449, 421, 0, 330, 0, 390, 0, 360, 480, 450, 419, 361,
    362, 0, 391, 420, 0, 0, 481, 453, 512, 0, 331, 0, 332, 392, 422, 0, 333, 482, 0, 451,
    393, 0, 334, 0, 335, 363, 423, 394, 364, 513, 0, 336, 365, 0, 337, 485, 452, 424, 514, 0,
    338, 0, 339, 0, 0, 366, 483, 367, 425, 577, 368, 454, 395, 369, 426, 370, 371, 396, 578, 517,
    484, 455, 429, 579, 515, 398, 456, 399, 580, 427, 400, 457, 516, 486, 581, 428, 401, 430, 458, 402,
    431, 403, 432, 487, 461, 488, 518, 489, 433, 490, 459, 434, 435, 460, 462, 493, 519, 463, 520, 521,
    464, 491, 522, 465, 466, 467, 492, 494, 495, 525, 496, 497, 523, 498, 499, 524, 526, 527, 528, 529,
    530, 531,
)


def nn(left, right):
    return lax.dot_general(left, right, (((1,), (0,)), ((), ())), preferred_element_type=WIDE)


def nt(left, right):
    return lax.dot_general(left, right, (((1,), (1,)), ((), ())), preferred_element_type=WIDE)


def tn(left, right):
    return lax.dot_general(left, right, (((0,), (0,)), ((), ())), preferred_element_type=WIDE)


def aligned(value, step):
    return pl.multiple_of(value, step)


def gelu_pair(upper):
    cdf = 0.5 * (1.0 + lax.erf(upper * (1.0 / math.sqrt(2.0))))
    density = jnp.exp(-0.5 * upper * upper) * (1.0 / math.sqrt(2.0 * math.pi))
    return upper * cdf, cdf + upper * density


def column_chunks(width, step):
    return [(start, step) for start in range(0, width, step)]


def fused_kernel(tokens, width, stem_width, mlp, sizes, gather_plan, reduce_plan, names, *refs):
    vec_in, lengths, stem_hbm, cot_hbm = refs[:4]
    shard, (act_hbm, stem_grad_hbm) = refs[4:9], refs[9:11]
    result, vec_out = refs[11:16], refs[16]
    ref = types.SimpleNamespace(**dict(zip(names, refs[17:])))
    full = ref.full
    local_grad = [ref.core_shrink] + list(full[1:4]) + [ref.shrink_grad]
    resid, work, bias = ref.resid, ref.work, ref.bias
    unit1, unit2, scale1, scale2 = ref.unit1, ref.unit2, ref.scale1, ref.scale2
    normed, normed_mid, proj = ref.normed, ref.normed_mid, ref.proj
    mixed_t, mixed, lse, delta = ref.mixed_t, ref.mixed, ref.lse, ref.delta
    pull, hidden, cot, stem, low = ref.pull, ref.hidden, ref.cot, ref.stem, ref.low
    vecs, vec_all, vec_sum = ref.vecs, ref.vec_all, ref.vec_sum
    fold = ref.fold

    dp, fs = lax.axis_index("dp"), lax.axis_index(AXIS)
    y, c = lax.div(dp, 2), lax.rem(dp, 2)
    z, x = lax.div(fs, 2), lax.rem(fs, 2)
    z_others = (z + 1 - 2 * lax.rem(z, 2), lax.rem(z + 2, 4), 3 - z)
    at_core = (y * 2 + 1 - c, fs)
    at_y = ((1 - y) * 2 + c, fs)
    at_x = (dp, z * 2 + 1 - x)
    at_z = tuple((dp, other * 2 + x) for other in z_others)

    def send(src, dst, send_sem, recv_sem, where):
        return pltpu.make_async_remote_copy(
            src_ref=src,
            dst_ref=dst,
            send_sem=send_sem,
            recv_sem=recv_sem,
            device_id=where,
            device_id_type=MESH,
        )


    up = lax.div(z, 2)
    inner = (z == 1) | (z == 2)
    arrivals = (z_others[0], 2 - up, 3 - 3 * up)
    fill, g_send, g_recv = ref.fill, ref.g_send, ref.g_recv

    def gather_refs(k):
        weight, start, count, share = gather_plan[k]
        half = sizes[weight][0] // 2
        both = half - 2 * share
        mine = pl.ds(aligned(c * half + y * share, 16), share + both)
        passed = pl.ds(aligned(c * half + y * (share + both), 16), share)
        halves = pl.ds(aligned(c * half, 16), half)
        return full[weight], shard[weight], mine, passed, halves, pl.ds(start, count)

    def fill_copy(k):
        whole, own, _, _, halves, cols = gather_refs(k)
        return pltpu.make_async_copy(own.at[halves, cols], whole.at[z, x, halves, cols], fill.at[k])

    def own_copy(k, sent, got, where):
        whole, own, mine, _, _, cols = gather_refs(k)
        return send(own.at[mine, cols], whole.at[z, x, mine, cols], g_send.at[sent, k], g_recv.at[got, k], where)

    def same_copy(part, k, sent, got, where):
        return send(part, part, g_send.at[sent, k], g_recv.at[got, k], where)

    def z_copy(k, order, sent, got, where):
        whole, _, mine, _, _, cols = gather_refs(k)
        return same_copy(whole.at[arrivals[order], x, mine, cols], k, sent, got, where)

    def across(k, step):
        order, got, where = ((0, 2, at_z[2]), (1, 1, at_z[0]), (2, 2, at_z[0]))[step]
        return z_copy(k, order, 1, got, where)

    def x_copy(k, order):
        whole, _, mine, _, _, cols = gather_refs(k)
        return same_copy(whole.at[arrivals[order], x, mine, cols], k, 2, 3, at_x)

    def inner_bytes(k):
        whole, _, mine, _, _, cols = gather_refs(k)
        return same_copy(whole.at[:, x, mine, cols], k, 1, 1, at_z[2])

    def x_bytes(k):
        whole, _, mine, _, _, cols = gather_refs(k)
        return same_copy(whole.at[:, x, mine, cols], k, 2, 3, at_x)

    def y_copy(k, order):
        whole, _, _, passed, _, cols = gather_refs(k)
        return same_copy(whole.at[arrivals[order], x, passed, cols], k, 3, 4, at_y)

    def y_bytes(k):
        whole, _, _, passed, _, cols = gather_refs(k)
        return same_copy(whole.at[pl.ds(0, 3), x, passed, cols], k, 3, 4, at_y)

    def y_copy_late(k):
        whole, _, _, passed, _, cols = gather_refs(k)
        return same_copy(whole.at[:, 1 - x, passed, cols], k, 4, 5, at_y)

    def core_copy(k):
        whole, _, _, _, halves, cols = gather_refs(k)
        return same_copy(whole.at[:, :, halves, cols], k, 5, 6, at_core)

    def start_z(k):
        own_copy(k, 0, 0, at_z[0]).start()

        @pl.when(inner)
        def _():
            own_copy(k, 1, 1, at_z[2]).start()

        fill_copy(k).start()

    def start_x(k):
        own_copy(k, 2, 3, at_x).start()

    def gather_z(order):
        def step(k):
            z_copy(k, order, order, order, at_z[0]).wait_recv()

            @pl.when(inner)
            def _():
                across(k, order).start()

            x_copy(k, order).start()
            if gather_plan[k][3]:
                y_copy(k, order).start()

        return step

    def gather_x(k):
        x_bytes(k).wait_recv()
        if gather_plan[k][3]:
            y_copy_late(k).start()

    def gather_y(k):
        fill_copy(k).wait()
        if gather_plan[k][3]:
            y_bytes(k).wait_recv()
            y_copy_late(k).wait_recv()
        core_copy(k).start()

    def gather_core(k):
        core_copy(k).wait_recv()

    def gather_sent(k):
        own_copy(k, 0, 0, at_z[0]).wait_send()

        @pl.when(inner)
        def _():
            inner_bytes(k).wait_send()

        x_bytes(k).wait_send()
        if gather_plan[k][3]:
            y_bytes(k).wait_send()
            y_copy_late(k).wait_send()
        core_copy(k).wait_send()

    r_send, r_recv, r_done = g_send, ref.r_recv, ref.r_done
    from_y, from_x, from_z = ref.from_y, ref.from_x, ref.from_z
    part_out, part_in, final = ref.part_out, ref.part_in, ref.final
    free = ref.free

    def core_slot(k):
        weight, start, count, _ = reduce_plan[k]
        if weight == SHRINK:
            return ref.core_shrink.at[:, :, :, pl.ds(start, count)]
        if weight == EMBED:
            return ref.core_embed.at[:, :, :, pl.ds(start, count)]
        half = sizes[weight][0] // 2
        before = {EXPAND: 0, OUT: mlp // width, JOINT: mlp // width + 1}[weight]
        return full[SHRINK].at[:, :, pl.ds((before + start // width) * half, half), pl.ds(start % width, count)]

    def reduce_refs(k):
        weight, start, count, share = reduce_plan[k]
        half = sizes[weight][0] // 2
        return weight, half, share, half - 2 * share, pl.ds(start, count)

    def r1_copy(k):
        weight, half, _, _, cols = reduce_refs(k)
        src = local_grad[weight].at[:, :, pl.ds(aligned((1 - c) * half, 16), half), cols]
        return send(src, core_slot(k), r_send.at[0, k], r_recv.at[0, k], at_core)

    def r2_copy(k):
        weight, half, share, both, cols = reduce_refs(k)
        rows = pl.ds(aligned(c * half + (1 - y) * (share + both), 16), share)
        return send(
            local_grad[weight].at[:, :, rows, cols],
            from_y[k],
            r_send.at[1, k],
            r_recv.at[1, k],
            at_y,
        )

    def mine_rows(half, share, both):
        return pl.ds(aligned(c * half + y * share, 16), share + both)

    def r3_copy(k):
        weight, half, share, both, cols = reduce_refs(k)
        return send(
            local_grad[weight].at[:, 1 - x, mine_rows(half, share, both), cols],
            from_x[k],
            r_send.at[2, k],
            r_recv.at[2, k],
            at_x,
        )

    def r4_copy(k, j):
        weight, half, share, both, cols = reduce_refs(k)
        return send(
            local_grad[weight].at[z_others[j], x, mine_rows(half, share, both), cols],
            from_z[k].at[j],
            r_send.at[3, k],
            r_recv.at[3, k],
            at_z[j],
        )

    def r4_bytes(k):
        return send(from_z[k], from_z[k], r_send.at[3, k], r_recv.at[3, k], at_z[0])

    def r5_copy(k):
        return send(part_out[k], part_in[k], r_send.at[4, k], r_recv.at[4, k], at_y)

    def r6_copies(k):
        weight, half, _, _, cols = reduce_refs(k)
        rows = pl.ds(aligned(c * half, 16), half)
        src, dst = final[k], result[weight].at[rows, cols]
        return (
            send(src, dst, r_send.at[5, k], r_recv.at[5, k], at_core),
            pltpu.make_async_copy(src, dst, r_done.at[k]),
        )

    def r6_incoming(k):
        weight, half, _, _, cols = reduce_refs(k)
        rows = pl.ds(aligned((1 - c) * half, 16), half)
        part = result[weight].at[rows, cols]
        return send(part, part, r_send.at[5, k], r_recv.at[5, k], at_core)

    def reduce_1(k):
        if reduce_plan[k][:2] == (EXPAND, 0):
            pl.semaphore_wait(free, 1)
        r1_copy(k).start()

    def reduce_2(k):
        weight, half, share, _, cols = reduce_refs(k)
        r1_copy(k).wait_recv()
        slot, total = core_slot(k), local_grad[weight]
        rows = pl.ds(aligned(c * half, 16), half)
        for i in range(4):
            for j in range(2):
                total[i, j, rows, cols] = total[i, j, rows, cols] + slot[i, j]
        if share:
            r2_copy(k).start()
        else:
            r3_copy(k).start()

    def reduce_3(k):
        weight, half, share, both, cols = reduce_refs(k)
        r2_copy(k).wait_recv()
        total = local_grad[weight]
        rows = pl.ds(aligned(c * half + y * (share + both), 16), share)
        for i in range(4):
            for j in range(2):
                total[i, j, rows, cols] = total[i, j, rows, cols] + from_y[k][i, j]
        r3_copy(k).start()

    def reduce_4(k):
        weight, half, share, both, cols = reduce_refs(k)
        r3_copy(k).wait_recv()
        total = local_grad[weight]
        rows = mine_rows(half, share, both)
        for i in range(4):
            total[i, x, rows, cols] = total[i, x, rows, cols] + from_x[k][i]
        for j in (2, 1, 0):
            r4_copy(k, j).start()

    def reduce_5(k):
        weight, half, share, both, cols = reduce_refs(k)
        r4_bytes(k).wait_recv()
        value = local_grad[weight][z, x, mine_rows(half, share, both), cols].astype(WIDE)
        for j in range(3):
            value = value + from_z[k][j].astype(WIDE)
        part_out[k][...] = value.astype(NARROW)
        r5_copy(k).start()

    def reduce_6(k):
        _, half, share, both, _ = reduce_refs(k)
        r5_copy(k).wait_recv()
        own, came, whole = part_out[k], part_in[k], final[k]

        def rows(start, count):
            return pl.ds(aligned(start, 16), count)

        if share:
            whole[rows(y * (share + both), share), :] = own[rows(y * both, share), :].astype(WIDE)
            whole[rows((1 - y) * (share + both), share), :] = came[rows((1 - y) * both, share), :].astype(WIDE)
        if both:
            whole[share : share + both, :] = own[rows((1 - y) * share, both), :].astype(WIDE) + came[
                rows(y * share, both), :
            ].astype(WIDE)
        for copy in r6_copies(k):
            copy.start()

    def reduce_7(k):
        r6_incoming(k).wait_recv()
        r1_copy(k).wait_send()
        if reduce_refs(k)[2]:
            r2_copy(k).wait_send()
        r3_copy(k).wait_send()
        r4_bytes(k).wait_send()
        r5_copy(k).wait_send()
        remote, local = r6_copies(k)
        remote.wait_send()
        local.wait()

    def row(place):
        return vecs[place : place + 1, :]

    def layer_norm(unit, scale, out, gain, shift):
        def step(n, carry):
            rows = pl.ds(aligned(n * 96, 96), 96)
            values = resid[rows, :]
            center = values - jnp.mean(values, axis=1, keepdims=True)
            factor = lax.rsqrt(jnp.mean(center * center, axis=1, keepdims=True) + 1e-6)
            units = center * factor
            scale[rows, :] = factor
            unit[rows, :] = units.astype(NARROW)
            out[rows, :] = (units * row(gain) + row(shift)).astype(NARROW)
            return carry

        lax.fori_loop(0, tokens // 96, step, 0)

    def eight(values):
        return jnp.sum(values.reshape(values.shape[0] // 8, 8, values.shape[1]), axis=0)

    def norm_backward(unit, scale, gain, upstream, keep_wide, places):
        fold[...] = jnp.zeros_like(fold)

        def step(n, carry):
            rows = pl.ds(aligned(n * 96, 96), 96)
            grads = work[rows, :]
            units = unit[rows, :].astype(WIDE)
            inner = grads * row(gain)
            fold[0:8, :] += eight(grads * units)
            fold[8:16, :] += eight(grads)
            value = upstream[rows, :].astype(WIDE) + scale[rows, :] * (
                inner
                - jnp.mean(inner, axis=1, keepdims=True)
                - units * jnp.mean(inner * units, axis=1, keepdims=True)
            )
            if keep_wide:
                resid[rows, :] = value
            narrow = value.astype(NARROW)
            low[rows, :] = narrow
            fold[16:24, :] += eight(narrow.astype(WIDE))
            return carry

        lax.fori_loop(0, tokens // 96, step, 0)
        for n, place in enumerate(places):
            vec_sum[0, place : place + 1, :] = jnp.sum(fold[8 * n : 8 * n + 8, :], axis=0, keepdims=True)

    def column_sum(source, start, place, at=0, count=width):
        def step(n, total):
            return total + eight(source[pl.ds(aligned(n * 96, 96), 96), start : start + count].astype(WIDE))

        total = lax.fori_loop(0, tokens // 96, step, jnp.zeros((8, count), WIDE))
        vec_sum[0, place : place + 1, at : at + count] = jnp.sum(total, axis=0, keepdims=True)

    lane = lax.broadcasted_iota(jnp.int32, (1, 2 * HEAD_DIM), 1)

    def head_lanes(head, value):
        return jnp.where((lane < HEAD_DIM) == (head == 0), value, 0.0).astype(NARROW)

    factor = 1.0 / math.sqrt(HEAD_DIM)

    def attend_forward(p):
        def run():
            at = p * 128
            query = proj[:, pl.ds(at, 128)]
            keys = proj[:, pl.ds(width + at, 128)]
            values_t = proj[:, pl.ds(2 * width + at, 128)].T
            for head in range(2):
                scores = nt(keys * head_lanes(head, factor), query) + bias[...].astype(WIDE)
                largest = jnp.max(scores, axis=0, keepdims=True)
                expos = jnp.exp(scores - largest)
                total = jnp.sum(expos, axis=0, keepdims=True)
                mix = nn(values_t[64 * head : 64 * head + 64], expos.astype(NARROW)) * (1.0 / total)
                mixed_t[pl.ds(aligned(at + 64 * head, 64), 64), :] = mix.astype(NARROW)
                lse[pl.ds(2 * p + head, 1), :] = largest + jnp.log(total)

        return run

    def attend_backward(p):
        def run():
            at = p * 128
            query = proj[:, pl.ds(at, 128)]
            keys = proj[:, pl.ds(width + at, 128)]
            values = proj[:, pl.ds(2 * width + at, 128)]
            grads = mixed[:, pl.ds(at, 128)]
            keys_t = keys.T
            value_grads, key_grads = [], []
            for head in range(2):
                scores = nt(keys * head_lanes(head, factor), query) + bias[...].astype(WIDE)
                attend = jnp.exp(scores - lse[pl.ds(2 * p + head, 1), :])
                attend_grad = nt(values * head_lanes(head, 1.0), grads)
                scores_grad = (attend * (attend_grad - delta[pl.ds(2 * p + head, 1), :])).astype(NARROW)
                value_grads.append(nn(attend.astype(NARROW), grads))
                key_grads.append(nn(scores_grad, query))
                query_grad = nn(keys_t[64 * head : 64 * head + 64], scores_grad) * factor
                mixed_t[pl.ds(aligned(at + 64 * head, 64), 64), :] = query_grad.astype(NARROW)
            first_head = lane < HEAD_DIM
            pull[:, pl.ds(2 * width + at, 128)] = jnp.where(first_head, *value_grads).astype(NARROW)
            pull[:, pl.ds(width + at, 128)] = (jnp.where(first_head, *key_grads) * factor).astype(NARROW)

        return run

    barrier = pltpu.get_barrier_semaphore()
    partners = (at_core, at_y, at_x) + at_z
    for partner in partners:
        pl.semaphore_signal(barrier, inc=1, device_id=partner, device_id_type=MESH)
    load_stem = pltpu.make_async_copy(stem_hbm, stem, ref.load.at[0])
    load_cot = pltpu.make_async_copy(cot_hbm, cot, ref.load.at[1])
    load_stem.start()
    load_cot.start()
    pl.semaphore_wait(barrier, len(partners))

    v_send, v_recv = ref.v_send, ref.v_recv
    vec_z = [send(vec_in, vec_all.at[z, x], v_send.at[0], v_recv.at[0], at_z[j]) for j in range(3)]
    vec_z_part = vec_all.at[pl.ds(0, 3), x]
    vec_z_bytes = send(vec_z_part, vec_z_part, v_send.at[0], v_recv.at[0], at_z[0])
    vec_x_part = vec_all.at[:, x]
    vec_x = send(vec_x_part, vec_x_part, v_send.at[1], v_recv.at[1], at_x)
    vec_all[z, x] = vec_in[...]
    for copy in vec_z:
        copy.start()

    def vec_gather(n):
        if n == 0:
            vec_z_bytes.wait_recv()
            vec_x.start()
        else:
            vec_x.wait_recv()

    vec_from = ref.vec_from
    vec_partners = (at_core, at_y, at_x, at_z[0], at_z[1])

    def vec_copy(n):
        return send(vec_sum.at[n], vec_from.at[n], v_send.at[2 + n], v_recv.at[2 + n], vec_partners[n])

    def vec_step(n):
        vec_copy(n - 1).wait_recv()
        vec_sum[n] = vec_sum[n - 1] + vec_from[n - 1]
        if n < len(vec_partners):
            vec_copy(n).start()

    blocks = []
    block = blocks.append

    @block
    def make_bias():
        places = lax.broadcasted_iota(jnp.int32, (1, tokens), 1)
        places_down = lax.broadcasted_iota(jnp.int32, (tokens, 1), 0)
        labels = jnp.zeros((1, tokens), jnp.int32)
        labels_down = jnp.zeros((tokens, 1), jnp.int32)
        bound = 0
        for n in range(lengths.shape[1]):
            bound = bound + lengths[0, n]
            labels = labels + (places >= bound).astype(jnp.int32)
            labels_down = labels_down + (places_down >= bound).astype(jnp.int32)
        bias[...] = jnp.where(labels_down == labels, 0.0, -1e30).astype(NARROW)
        vec_sum[0] = jnp.zeros((VECTOR_ROWS, width), WIDE)

    @block
    def add_vectors():
        totals = vec_all[0, 0].astype(WIDE)
        for i in range(4):
            for j in range(2):
                if i + j > 0:
                    totals = totals + vec_all[i, j].astype(WIDE)
        vecs[...] = totals
        vec_z_bytes.wait_send()
        vec_x.wait_send()
        load_stem.wait()
        load_cot.wait()

    def chunks(plan, weight):
        return [item[1:3] for item in plan if item[0] == weight]

    def embed(start, count):
        def run():
            piece = full[EMBED][:, :, :, start : start + count].reshape(stem_width, count)
            offset = vecs[EMBED_BIAS : EMBED_BIAS + 1, start : start + count]
            resid[:, start : start + count] = nn(stem[...], piece) + offset

        return run

    def project(start, count):
        def run():
            value = nn(normed[...], full[JOINT][:, :, :, start : start + count].reshape(width, count))
            at = start % width
            if start // width == 0:
                value = value + vecs[QUERY_BIAS : QUERY_BIAS + 1, at : at + count]
            if start // width == 2:
                value = value + vecs[VALUE_BIAS : VALUE_BIAS + 1, at : at + count]
            proj[:, start : start + count] = value.astype(NARROW)

        return run

    for item in chunks(gather_plan, EMBED):
        block(embed(*item))

    @block
    def first_norm():
        layer_norm(unit1, scale1, normed, FIRST_GAIN, FIRST_SHIFT)

    for item in chunks(gather_plan, JOINT):
        block(project(*item))
    for p in range(HEADS // 2):
        block(attend_forward(p))

    @block
    def join_heads():
        mixed[...] = mixed_t[...].T
        resid[...] = resid[...] + nn(mixed[...], full[OUT][...].reshape(width, width)) + row(OUT_BIAS)

    @block
    def second_norm():
        layer_norm(unit2, scale2, normed_mid, SECOND_GAIN, SECOND_SHIFT)

    def expand_forward(i):
        def run():
            start = i * width
            work[...] = nn(normed_mid[...], full[EXPAND][:, :, :, start : start + width].reshape(width, width))

            def gelu_step(n, carry):
                rows = pl.ds(aligned(n * 64, 64), 64)
                for at in range(0, width, 128):
                    offset = vecs[EXPAND_BIAS + i : EXPAND_BIAS + i + 1, at : at + 128]
                    value, slope = gelu_pair(work[rows, at : at + 128] + offset)
                    hidden[rows, start + at : start + at + 128] = value.astype(NARROW)
                    pull[rows, start + at : start + at + 128] = slope.astype(NARROW)
                return carry

            lax.fori_loop(0, tokens // 64, gelu_step, 0)

        return run

    rows_shrink = sizes[SHRINK][0]

    def shrink_gradient(i):
        def run():
            for j in range(2):
                at = rows_shrink * (2 * i + j)
                local_grad[SHRINK][i, j] = tn(hidden[:, at : at + rows_shrink], cot[...]).astype(NARROW)

        return run

    for i in range(4):
        block(expand_forward(i))
        block(shrink_gradient(i))

    @block
    def cotangent_sum():
        column_sum(cot, 0, SHRINK_BIAS)

    def hidden_backward(i):
        def run():
            at = i * width
            grads = nt(cot[...], full[SHRINK][i].reshape(width, width))
            pull[:, at : at + width] = (grads * pull[:, at : at + width].astype(WIDE)).astype(NARROW)
            column_sum(pull, at, EXPAND_BIAS + i)

        return run

    for i in range(4):
        block(hidden_backward(i))
    store_act = pltpu.make_async_copy(low, act_hbm, ref.load.at[0])
    store_stem = pltpu.make_async_copy(hidden.at[:, pl.ds(0, stem_width)], stem_grad_hbm, ref.load.at[1])

    @block
    def activations():
        value = nn(hidden[...], full[SHRINK][...].reshape(mlp, width))
        low[...] = (resid[...] + value + row(SHRINK_BIAS)).astype(NARROW)
        store_act.start()
        pl.semaphore_signal(free, inc=1, device_id=at_core, device_id_type=MESH)

    @block
    def expand_backward():
        work[...] = nt(pull[...], full[EXPAND][...].reshape(width, mlp))

    def expand_gradient(i):
        def run():
            at = i * width
            value = tn(normed_mid[...], pull[:, at : at + width]).astype(NARROW)
            full[EXPAND][:, :, :, at : at + width] = value.reshape(4, 2, width // 8, width)

        return run

    for i in range(4):
        block(expand_gradient(i))

    @block
    def second_norm_backward():
        store_act.wait()
        norm_backward(unit2, scale2, SECOND_GAIN, cot, True, (SECOND_GAIN, SECOND_SHIFT, OUT_BIAS))

    @block
    def out_backward():
        mixed[...] = nt(low[...], full[OUT][...].reshape(width, width)).astype(NARROW)

    @block
    def out_gradient():
        full[OUT][...] = nn(mixed_t[...], low[...]).astype(NARROW).reshape(4, 2, width // 8, width)

    @block
    def row_sums():
        grads_t = mixed[...].T
        for head in range(HEADS):
            span = slice(64 * head, 64 * head + 64)
            product = grads_t[span].astype(WIDE) * mixed_t[span, :].astype(WIDE)
            delta[head : head + 1, :] = jnp.sum(product, axis=0, keepdims=True)

    def gather_query(half):
        def run():
            at = half * width // 2
            pull[:, at : at + width // 2] = mixed_t[at : at + width // 2, :].T
            column_sum(pull, at, QUERY_BIAS, at, width // 2)
            column_sum(pull, 2 * width + at, VALUE_BIAS, at, width // 2)

        return run

    def joint_backward(half):
        def run():
            total = 0.0 if half == 0 else work[...]
            for part in range(3):
                at = part * width + half * width // 2
                weight = full[JOINT][:, :, :, at : at + width // 2].reshape(width, width // 2)
                total = total + nt(pull[:, at : at + width // 2], weight)
            work[...] = total

        return run

    def joint_gradient(start, count):
        def run():
            value = tn(normed[...], pull[:, start : start + count]).astype(NARROW)
            full[JOINT][:, :, :, start : start + count] = value.reshape(4, 2, width // 8, count)

        return run

    for half in range(2):
        for p in range(HEADS // 4):
            block(attend_backward(half * HEADS // 4 + p))
        block(gather_query(half))
        block(joint_backward(half))
        for item in chunks(reduce_plan, JOINT)[3 * half : 3 * half + 3]:
            block(joint_gradient(*item))

    @block
    def first_norm_backward():
        norm_backward(unit1, scale1, FIRST_GAIN, resid, False, (FIRST_GAIN, FIRST_SHIFT, EMBED_BIAS))

    rows_embed = sizes[EMBED][0]

    def embed_gradient(start, count):
        def run():
            value = tn(stem[...], low[:, start : start + count]).astype(NARROW)
            local_grad[EMBED][:, :, 0:rows_embed, start : start + count] = value.reshape(4, 2, rows_embed, count)

        return run

    for item in chunks(reduce_plan, EMBED):
        block(embed_gradient(*item))

    @block
    def start_vectors():
        vec_copy(0).start()

    @block
    def stem_backward():
        value = nt(low[...], full[EMBED][...].reshape(stem_width, width))
        hidden[:, 0:stem_width] = value.astype(NARROW)
        store_stem.start()

    work_left = iter(blocks)
    steps = (
        lambda k: pl.when(dp >= 0)(next(work_left)),
        start_z,
        start_x,
        gather_z(0),
        gather_z(1),
        gather_z(2),
        gather_x,
        gather_y,
        gather_core,
        gather_sent,
        reduce_1,
        reduce_2,
        reduce_3,
        reduce_4,
        reduce_5,
        reduce_6,
        reduce_7,
        vec_gather,
        vec_step,
    )
    for code in ORDER:
        steps[code // 32](code % 32)
    vec_out[...] = vec_sum[len(vec_partners)]
    for n in range(len(vec_partners)):
        vec_copy(n).wait_send()
    store_stem.wait()


def plans(width, mlp):
    gather_plan = (
        [(EMBED,) + item for item in column_chunks(width, GATHER_STEPS[EMBED])]
        + [(JOINT,) + item for item in column_chunks(3 * width, GATHER_STEPS[JOINT])]
        + [(OUT,) + item for item in column_chunks(width, GATHER_STEPS[OUT])]
        + [(EXPAND,) + item for item in column_chunks(mlp, GATHER_STEPS[EXPAND])]
        + [(SHRINK,) + item for item in column_chunks(width, GATHER_STEPS[SHRINK])]
    )
    halves = (0, width // 2)
    reduce_plan = (
        [(SHRINK,) + item for item in column_chunks(width, REDUCE_STEPS[SHRINK])]
        + [(EXPAND,) + item for item in column_chunks(mlp, REDUCE_STEPS[EXPAND])]
        + [(OUT,) + item for item in column_chunks(width, REDUCE_STEPS[OUT])]
        + [(JOINT, part * width + at, width // 2) for at in halves for part in range(3)]
        + [(EMBED,) + item for item in column_chunks(width, REDUCE_STEPS[EMBED])]
    )
    return (
        [item + (16 * n,) for item, n in zip(gather_plan, GATHER_SHARES)],
        [item + (16 * n,) for item, n in zip(reduce_plan, REDUCE_SHARES)],
    )


def fused(mesh):
    def local(
        stem_features,
        lengths,
        embed_weight,
        embed_bias,
        before_gain,
        before_shift,
        joint_weight,
        query_bias,
        value_bias,
        output_weight,
        output_bias,
        middle_gain,
        middle_shift,
        expand_weight,
        expand_bias,
        shrink_weight,
        shrink_bias,
        cotangent,
    ):
        _, tokens, stem_width = stem_features.shape
        width = embed_weight.shape[1]
        mlp = expand_weight.shape[1]
        shards = (embed_weight, joint_weight, output_weight, expand_weight, shrink_weight)
        sizes = [item.shape for item in shards]
        fsdp = lax.axis_index(AXIS)

        nine = jnp.stack(
            [
                embed_bias,
                before_gain,
                before_shift,
                query_bias,
                value_bias,
                output_bias,
                middle_gain,
                middle_shift,
                shrink_bias,
            ]
        )
        piece = nine.shape[1]
        owner = jnp.arange(width) // piece
        rows_nine = jnp.where(owner[None] == fsdp, jnp.tile(nine, (1, width // piece)), 0)
        piece_expand = expand_bias.shape[0]
        owner = (jnp.arange(mlp // width)[:, None] * width + jnp.arange(width)[None]) // piece_expand
        rows_expand = jnp.tile(expand_bias[None], (mlp // width, width // piece_expand))
        rows_expand = jnp.where(owner == fsdp, rows_expand, 0)
        used = 9 + mlp // width
        vec_in = jnp.concatenate([rows_nine, rows_expand, jnp.zeros((VECTOR_ROWS - used, width), NARROW)])
        vec_in = vec_in.astype(NARROW)

        gather_plan, reduce_plan = plans(width, mlp)
        steps, folds = len(gather_plan), len(reduce_plan)
        vmem, dma = pltpu.VMEM, pltpu.SemaphoreType.DMA

        def each(make):
            return [make(sizes[n][0] // 2, share, cols) for n, _, cols, share in reduce_plan]

        def square(cols):
            return vmem((tokens, cols), NARROW)

        scratch = dict(
            full=[vmem((4, 2) + item, NARROW) for item in sizes],
            shrink_grad=vmem((4, 2) + sizes[SHRINK], NARROW),
            core_shrink=vmem((4, 2, sizes[SHRINK][0] // 2, width), NARROW),
            core_embed=vmem((4, 2, sizes[EMBED][0] // 2, width), NARROW),
            from_y=each(lambda half, share, cols: vmem((4, 2, max(share, 16), cols if share else 128), NARROW)),
            from_x=each(lambda half, share, cols: vmem((4, half - share, cols), NARROW)),
            from_z=each(lambda half, share, cols: vmem((3, half - share, cols), NARROW)),
            part_out=each(lambda half, share, cols: vmem((half - share, cols), NARROW)),
            part_in=each(lambda half, share, cols: vmem((half - share, cols), NARROW)),
            final=each(lambda half, share, cols: vmem((half, cols), WIDE)),
            resid=vmem((tokens, width), WIDE),
            work=vmem((tokens, width), WIDE),
            bias=square(tokens),
            unit1=square(width),
            unit2=square(width),
            normed=square(width),
            normed_mid=square(width),
            mixed=square(width),
            cot=square(width),
            low=square(width),
            scale1=vmem((tokens, 1), WIDE),
            scale2=vmem((tokens, 1), WIDE),
            proj=square(3 * width),
            mixed_t=vmem((width, tokens), NARROW),
            lse=vmem((16, tokens), WIDE),
            delta=vmem((16, tokens), WIDE),
            pull=square(mlp),
            hidden=square(mlp),
            stem=square(stem_width),
            vecs=vmem((VECTOR_ROWS, width), WIDE),
            vec_all=vmem((4, 2, VECTOR_ROWS, width), NARROW),
            vec_sum=vmem((6, VECTOR_ROWS, width), WIDE),
            vec_from=vmem((5, VECTOR_ROWS, width), WIDE),
            fold=vmem((24, width), WIDE),
            fill=dma((steps,)),
            g_send=dma((6, max(steps, folds))),
            g_recv=dma((7, steps)),
            r_recv=dma((6, folds)),
            r_done=dma((folds,)),
            load=dma((2,)),
            v_send=dma((7,)),
            v_recv=dma((7,)),
            free=pltpu.SemaphoreType.REGULAR,
        )
        names = list(scratch)

        def body(*refs):
            fused_kernel(tokens, width, stem_width, mlp, sizes, gather_plan, reduce_plan, names, *refs)

        far = pl.BlockSpec(memory_space=pl.ANY)
        near = pl.BlockSpec(memory_space=pltpu.VMEM)
        outs = pl.pallas_call(
            body,
            out_shape=(
                jax.ShapeDtypeStruct((tokens, width), NARROW),
                jax.ShapeDtypeStruct((tokens, stem_width), NARROW),
            )
            + tuple(jax.ShapeDtypeStruct(item, WIDE) for item in sizes)
            + (jax.ShapeDtypeStruct((VECTOR_ROWS, width), WIDE),),
            in_specs=[near, pl.BlockSpec(memory_space=pltpu.SMEM)] + [far] * 7,
            out_specs=(far,) * 7 + (near,),
            scratch_shapes=list(scratch.values()),
            compiler_params=pltpu.CompilerParams(
                collective_id=0, has_side_effects=True, vmem_limit_bytes=64 * 2**20
            ),
        )(vec_in, lengths, stem_features[0], cotangent[0], *shards)
        act, stem_grad, grads, vec_out = outs[0], outs[1], outs[2:7], outs[7]
        mine = lax.dynamic_slice(vec_out, (0, fsdp * piece), (9, piece))
        start = fsdp * piece_expand
        mine_expand = lax.dynamic_slice(vec_out, (9 + start // width, start % width), (1, piece_expand))[0]
        return (
            act[None],
            stem_grad[None],
            grads[EMBED],
            mine[EMBED_BIAS],
            mine[FIRST_GAIN],
            mine[FIRST_SHIFT],
            grads[JOINT],
            mine[QUERY_BIAS],
            mine[VALUE_BIAS],
            grads[OUT],
            mine[OUT_BIAS],
            mine[SECOND_GAIN],
            mine[SECOND_SHIFT],
            grads[EXPAND],
            mine_expand,
            grads[SHRINK],
            mine[SHRINK_BIAS],
        )

    return local


def normalize(values):
    center = values - jnp.mean(values, axis=-1, keepdims=True)
    scaled = lax.rsqrt(jnp.mean(center * center, axis=-1, keepdims=True) + 1e-06)
    return (center * scaled, scaled)


def norm_backward(upstream, unit, scaled, gain):
    gain_part = jnp.sum(upstream * unit, axis=0)
    shift_part = jnp.sum(upstream, axis=0)
    inner = upstream * gain
    result = scaled * (
        inner
        - jnp.mean(inner, axis=-1, keepdims=True)
        - unit * jnp.mean(inner * unit, axis=-1, keepdims=True)
    )
    return (result, gain_part, shift_part)


def region_mask(lengths, row_len):
    bounds = jnp.cumsum(lengths, axis=1)
    places = jnp.arange(row_len, dtype=jnp.int32)
    labels = jnp.sum((places[None, :, None] >= bounds[:, None, :]).astype(jnp.int32), axis=2)
    return labels[:, :, None] == labels[:, None, :]


def column_sum(matrix):
    return jnp.sum(matrix.astype(jnp.float32), axis=0)


def general(
    stem_features,
    lengths,
    embed_weight,
    embed_bias,
    before_gain,
    before_shift,
    joint_weight,
    query_bias,
    value_bias,
    output_weight,
    output_bias,
    middle_gain,
    middle_shift,
    expand_weight,
    expand_bias,
    shrink_weight,
    shrink_bias,
    cotangent,
):
    wide = jnp.float32
    narrow = jnp.bfloat16
    shards = (
        embed_weight,
        embed_bias,
        before_gain,
        before_shift,
        joint_weight,
        query_bias,
        value_bias,
        output_weight,
        output_bias,
        middle_gain,
        middle_shift,
        expand_weight,
        expand_bias,
        shrink_weight,
        shrink_bias,
    )
    gathered = tuple(lax.all_gather(item, AXIS, axis=0, tiled=True) for item in shards)
    (
        embedding,
        embed_offset,
        first_gain,
        first_shift,
        joint,
        query_offset,
        value_offset,
        outward,
        out_offset,
        second_gain,
        second_shift,
        expand,
        expand_offset,
        shrink,
        shrink_offset,
    ) = gathered
    rows, row_len, stem_width = stem_features.shape
    width = embed_weight.shape[1]
    tokens = rows * row_len
    factor = 1.0 / math.sqrt(HEAD_DIM)
    heads_shape = (rows, row_len, HEADS, HEAD_DIM)
    same_region = region_mask(lengths, row_len)[:, None]
    inputs = stem_features.reshape(tokens, stem_width)
    embedded = jnp.dot(inputs, embedding, preferred_element_type=wide) + embed_offset.astype(wide)
    unit_first, scale_first = normalize(embedded)
    normed = (unit_first * first_gain.astype(wide) + first_shift.astype(wide)).astype(narrow)
    joint_offset = jnp.concatenate(
        [query_offset, jnp.zeros_like(query_offset), value_offset]
    ).astype(wide)
    projected = (jnp.dot(normed, joint, preferred_element_type=wide) + joint_offset).astype(narrow)
    query = projected[:, :width].reshape(heads_shape)
    keys = projected[:, width : 2 * width].reshape(heads_shape)
    values = projected[:, 2 * width :].reshape(heads_shape)

    def masked_scores():
        products = jnp.einsum("rqhe,rkhe->rhqk", query, keys, preferred_element_type=wide) * factor
        return jnp.where(same_region, products, -1e30)

    scores = masked_scores()
    largest = jnp.max(scores, axis=-1, keepdims=True)
    expos = jnp.exp(scores - largest)
    totals = jnp.sum(expos, axis=-1, keepdims=True)
    log_total = largest + jnp.log(totals)
    attend = (expos / totals).astype(narrow)
    mixed = jnp.einsum("rhqk,rkhe->rqhe", attend, values, preferred_element_type=wide)
    mixed = mixed.reshape(tokens, width).astype(narrow)
    residual = (
        embedded + jnp.dot(mixed, outward, preferred_element_type=wide) + out_offset.astype(wide)
    )
    unit_second, scale_second = normalize(residual)
    normed_mid = (unit_second * second_gain.astype(wide) + second_shift.astype(wide)).astype(narrow)
    upper = jnp.dot(normed_mid, expand, preferred_element_type=wide) + expand_offset.astype(wide)
    hidden_wide, gelu_pull = jax.vjp(lambda inner: jax.nn.gelu(inner, approximate=False), upper)
    hidden = hidden_wide.astype(narrow)
    output = (
        residual + jnp.dot(hidden, shrink, preferred_element_type=wide) + shrink_offset.astype(wide)
    )
    activations = output.astype(narrow).reshape(rows, row_len, width)
    backward_set = gathered
    embedding = backward_set[0]
    first_gain = backward_set[2]
    joint = backward_set[4]
    outward = backward_set[7]
    second_gain = backward_set[9]
    expand = backward_set[11]
    shrink = backward_set[13]
    upstream = cotangent.reshape(tokens, width).astype(wide)
    upstream_low = upstream.astype(narrow)
    shrink_grad = jnp.einsum("tm,td->md", hidden, upstream_low, preferred_element_type=wide)
    shrink_offset_grad = column_sum(upstream_low)
    hidden_grad = jnp.einsum("td,md->tm", upstream_low, shrink, preferred_element_type=wide)
    upper_grad = gelu_pull(hidden_grad)[0].astype(narrow)
    expand_grad = jnp.einsum("td,tm->dm", normed_mid, upper_grad, preferred_element_type=wide)
    expand_offset_grad = column_sum(upper_grad)
    normed_mid_grad = jnp.einsum("tm,dm->td", upper_grad, expand, preferred_element_type=wide)
    second_part, second_gain_grad, second_shift_grad = norm_backward(
        normed_mid_grad, unit_second, scale_second, second_gain.astype(wide)
    )
    residual_grad = upstream + second_part
    residual_low = residual_grad.astype(narrow)
    outward_grad = jnp.einsum("te,td->ed", mixed, residual_low, preferred_element_type=wide)
    out_offset_grad = column_sum(residual_low)
    mixed_grad = jnp.einsum("td,ed->te", residual_low, outward, preferred_element_type=wide)
    mixed_grad = mixed_grad.astype(narrow).reshape(heads_shape)
    attend_wide = jnp.exp(masked_scores() - log_total)
    attend = attend_wide.astype(narrow)
    values_grad = jnp.einsum("rhqk,rqhe->rkhe", attend, mixed_grad, preferred_element_type=wide)
    attend_grad = jnp.einsum("rqhe,rkhe->rhqk", mixed_grad, values, preferred_element_type=wide)
    centered = jnp.sum(attend_grad * attend_wide, axis=-1, keepdims=True)
    scores_grad = (attend_wide * (attend_grad - centered)).astype(narrow)
    query_grad = (
        jnp.einsum("rhqk,rkhe->rqhe", scores_grad, keys, preferred_element_type=wide) * factor
    )
    keys_grad = (
        jnp.einsum("rhqk,rqhe->rkhe", scores_grad, query, preferred_element_type=wide) * factor
    )
    projected_grad = jnp.concatenate(
        [
            query_grad.reshape(tokens, width),
            keys_grad.reshape(tokens, width),
            values_grad.reshape(tokens, width),
        ],
        axis=1,
    ).astype(narrow)
    joint_grad = jnp.einsum("td,tj->dj", normed, projected_grad, preferred_element_type=wide)
    query_offset_grad = column_sum(projected_grad[:, :width])
    value_offset_grad = column_sum(projected_grad[:, 2 * width :])
    normed_grad = jnp.einsum("tj,dj->td", projected_grad, joint, preferred_element_type=wide)
    first_part, first_gain_grad, first_shift_grad = norm_backward(
        normed_grad, unit_first, scale_first, first_gain.astype(wide)
    )
    embedded_low = (residual_grad + first_part).astype(narrow)
    embedding_grad = jnp.einsum("ts,td->sd", inputs, embedded_low, preferred_element_type=wide)
    embed_offset_grad = column_sum(embedded_low)
    stem_gradient = jnp.einsum("td,sd->ts", embedded_low, embedding, preferred_element_type=wide)
    stem_gradient = stem_gradient.astype(narrow).reshape(rows, row_len, stem_width)
    terms = (
        embedding_grad,
        embed_offset_grad,
        first_gain_grad,
        first_shift_grad,
        joint_grad,
        query_offset_grad,
        value_offset_grad,
        outward_grad,
        out_offset_grad,
        second_gain_grad,
        second_shift_grad,
        expand_grad,
        expand_offset_grad,
        shrink_grad,
        shrink_offset_grad,
    )
    owned = tuple(lax.psum_scatter(item, AXIS, scatter_dimension=0, tiled=True) for item in terms)
    summed = lax.psum(owned, "dp")
    return (activations, stem_gradient) + tuple(summed)


def solution(mesh):
    rows, whole, vector = P(("dp", AXIS), None, None), P(AXIS, None), P(AXIS)
    params = (whole, vector, vector, vector, whole, vector, vector, whole, vector)
    params = params + (vector, vector, whole, vector, whole, vector)
    plain = mesh.shape["dp"] != 4 or mesh.shape[AXIS] != 8
    return jax.shard_map(
        general if plain else fused(mesh),
        mesh=mesh,
        in_specs=(rows, P(("dp", AXIS), None)) + params + (rows,),
        out_specs=(rows, rows) + params,
        check_vma=False,
    )
```
